512 devices in a mesh: kp: 128 (over y, z_lo, x, core), own: 4 (over z_hi).
Axes of the slice: x: 4, y: 4, z: 16 (z_hi: 4, z_lo: 4; z = z_hi * 4 + z_lo), core: 2. Of those that a mesh axis runs over, the one named last changes fastest.
Arguments:
- pair_density: bfloat16 [256, 256, 2, 2048], P('kp', None, None, 'own'), may hold values from -6 to 6
- coulomb: float32 [2048], P('own'), may hold values from 0.1 to 10
Outputs:
- kernel: bfloat16 [4, 65536, 2, 512], P(None, ('kp', 'own'))
The draws below stay inside these ranges and needn't reach their ends.
All inputs are finite; a program needn't handle non-finite values.
Results may differ from the reference program's by a relative error of at most 0.013.
Values may be sent and summed in bfloat16 or wider, within the bound.
No kernel may reach another device: no remote copies, remote signals or barrier semaphores. Data moves between devices by JAX's collectives and lax.ppermute only.
A program may use at most 64 MiB of HBM per device.

```python
import math
import jax
import jax.numpy as jnp
from jax import lax

NT = 256
NG = 2048
K_DEV = 2
ROUNDS = 2
BLOCK = 32
NK = 256
N_KP = 128
N_OWN = 4


def level_of(rng, dims, split, least, high):
    def one(dim, blocks):
        steps = jax.random.uniform(jax.random.fold_in(jax.random.fold_in(rng, 6), dim), (blocks,), jnp.float32, least / len(split), high / len(split))
        return jnp.repeat(jnp.exp(steps), dims[dim] // blocks).reshape((-1,) + (1,) * (len(dims) - dim - 1))

    factor_of = one(*split[0])
    for cut in split[1:]:
        factor_of = factor_of * one(*cut)
    return factor_of


def scatter_about(rng, extent, spread, bound, cuts=(), kind=jnp.bfloat16):
    result = jax.random.normal(rng, extent, jnp.float32) * spread
    if len(cuts) > 0:
        result = level_of(rng, extent, cuts, -0.22, 0.18) * result
    return jnp.clip(result, min=-bound, max=bound).astype(kind)


def setup_inputs(seed: int = 0) -> dict:
    key_of = jax.random.split(jax.random.key(seed), 3)
    return {
        "pair_density": scatter_about(key_of[0], (NK, NT, 2, NG), 1.0, 6.0, ((0, 128), (3, 4))),
        "coulomb": jnp.clip(jnp.exp(math.log(10.0) - 4.6051702 * jax.random.uniform(key_of[1], (NG,), jnp.float32) ** level_of(key_of[1], (NG,), ((0, 4),), -0.2, 0.2)), 0.1, 10.0),
    }


def pair_block(left_group, right_group, scale_factor):
    row_total = left_group.shape[0]
    owner_count = left_group.shape[2]
    total_sum = jnp.zeros((row_total, 2 * row_total), jnp.float32)
    for owner in range(owner_count):
        left_rows = left_group[:, :, owner, :].reshape(row_total, -1)
        real_part = right_group[:, 0, owner, :]
        imag_part = right_group[:, 1, owner, :]
        right_side = jnp.concatenate([jnp.concatenate([real_part, imag_part], axis=1), jnp.concatenate([imag_part, -real_part], axis=1)], axis=0)
        product = jnp.dot(left_rows, right_side.T, preferred_element_type=jnp.float32) * scale_factor
        rounded = lax.optimization_barrier(product.astype(jnp.bfloat16))
        total_sum = total_sum + rounded.astype(jnp.float32)
    return total_sum.astype(jnp.bfloat16).reshape(row_total, 2, row_total)

def conj_block(kernel_part):
    flipped = jnp.stack([kernel_part[:, 0, :], -kernel_part[:, 1, :]], axis=1)
    return jnp.transpose(flipped, (2, 1, 0))

def reference(pair_density, coulomb):
    row_total = K_DEV * NT
    g_local = NG // N_OWN
    block_count = row_total // (BLOCK * N_OWN)
    scale_factor = 1.0 / NG ** 0.5
    weighted = (pair_density.astype(jnp.float32) * jnp.sqrt(coulomb)).astype(jnp.bfloat16)
    grouped = weighted.reshape(N_KP, row_total, 2, N_OWN, g_local)
    backward = []
    forward = []
    for offset in range(1, ROUNDS + 1):
        partner = jnp.roll(grouped, offset, axis=0)
        blocks_here = lax.map(lambda pair_items: pair_block(pair_items[0], pair_items[1], scale_factor), (grouped, partner))
        backward.append(blocks_here)
        forward.append(jax.vmap(conj_block)(jnp.roll(blocks_here, -offset, axis=0)))
    stacked = jnp.stack(backward + forward, axis=0)
    stacked = stacked.reshape(4, N_KP, block_count, N_OWN, BLOCK, 2, row_total)
    stacked = jnp.transpose(stacked, (0, 1, 3, 2, 4, 5, 6))
    return stacked.reshape(4, NK * NT, 2, row_total)
```

```python
import math

import jax
import jax.numpy as jnp
import numpy as np
from jax import lax
from jax.sharding import PartitionSpec as P

BLOCK = 32


def natural_order(owners, block_count):
    rows = np.arange(owners * block_count * BLOCK)
    owner, block, place = rows // (block_count * BLOCK), rows // BLOCK % block_count, rows % BLOCK
    return (block * owners + owner) * BLOCK + place


def body(pair_density, coulomb):
    points, transitions, _, g_local = pair_density.shape
    row_total = points * transitions
    owners = lax.axis_size("own")
    groups = lax.axis_size("kp")
    own_rows = row_total // owners
    half = own_rows // 2
    block_count = own_rows // BLOCK
    scale = 1.0 / math.sqrt(g_local * owners)
    me = lax.axis_index("own")
    odd = lax.axis_index("kp") % 2 == 1

    near_raw = lax.ppermute(pair_density, "kp", [(i, (i + 1) % groups) for i in range(groups)])
    ahead_raw = lax.ppermute(pair_density, "kp", [(i, (i - 2) % groups) for i in range(0, groups, 2)])
    behind_raw = lax.ppermute(near_raw, "kp", [(i, i + 1) for i in range(0, groups, 2)])

    def planes(raw):
        return raw.reshape(row_total, 2 * g_local)

    weighted = (pair_density.astype(jnp.float32) * coulomb).astype(jnp.bfloat16)
    weighted = weighted.reshape(block_count, owners, BLOCK, 2, g_local)
    weighted = jnp.roll(weighted, -me, axis=1)
    weighted = weighted.transpose(1, 3, 0, 2, 4).reshape(owners, 2, own_rows, g_local)
    real_part, imag_part = weighted[:, 0], weighted[:, 1]
    left = jnp.stack(
        [
            jnp.concatenate([real_part, imag_part], axis=-1),
            jnp.concatenate([-imag_part, real_part], axis=-1),
        ],
        axis=1,
    )

    def product(rows, right):
        out = lax.dot_general(
            rows, right, (((2,), (1,)), ((), ())), preferred_element_type=jnp.float32
        )
        return out * scale

    up = [(o, (o + 1) % owners) for o in range(owners)]
    down = [(o, (o - 1) % owners) for o in range(owners)]

    def first(right):
        to_up = jnp.concatenate([left[2, :, :half], left[1, :, half:]], axis=1)
        to_down = jnp.concatenate([left[3, :, :half], left[2, :, half:]], axis=1)
        return (
            lax.ppermute(product(to_up, right).astype(jnp.bfloat16), "own", up),
            lax.ppermute(product(to_down, right).astype(jnp.bfloat16), "own", down),
        )

    def second(right, from_down, from_up):
        to_up = product(left[1, :, :half], right) + from_down[:, :half].astype(jnp.float32)
        to_down = product(left[3, :, half:], right) + from_up[:, half:].astype(jnp.float32)
        return (
            lax.ppermute(to_up.astype(jnp.bfloat16), "own", up),
            lax.ppermute(to_down.astype(jnp.bfloat16), "own", down),
        )

    def third(right, from_down, from_up, late_down, late_up):
        low = product(left[0, :, :half], right) + from_up[:, :half].astype(jnp.float32) + late_down.astype(jnp.float32)
        high = product(left[0, :, half:], right) + from_down[:, half:].astype(jnp.float32) + late_up.astype(jnp.float32)
        return jnp.concatenate([low, high], axis=1).astype(jnp.bfloat16)

    order = natural_order(owners, block_count)
    pick = jnp.asarray(np.eye(row_total, dtype=np.float32)[order], jnp.bfloat16)

    def turned(block):
        sign = jnp.array([1.0, -1.0], jnp.bfloat16).reshape(2, 1, 1)
        out = lax.dot_general(
            pick, block * sign, (((1,), (2,)), ((), ())), preferred_element_type=jnp.float32
        )
        return out.astype(jnp.bfloat16)

    def gathered(pieces):
        swapped = lax.all_to_all(
            pieces.reshape(owners, own_rows, 2, own_rows), "own", split_axis=0, concat_axis=0, tiled=True
        )
        swapped = swapped.transpose(1, 2, 0, 3).reshape(own_rows, 2, row_total)
        out = lax.dot_general(swapped, pick, (((2,), (0,)), ((), ())), preferred_element_type=jnp.float32)
        return out.astype(jnp.bfloat16)

    right_1 = planes(near_raw)
    got_1 = first(right_1)
    right_2 = planes(jnp.where(odd, behind_raw, ahead_raw))
    got_2 = first(right_2)
    late_1 = second(right_1, *got_1)
    late_2 = second(right_2, *got_2)
    block_1 = third(right_1, *got_1, *late_1)
    back_1 = lax.ppermute(turned(block_1), "kp", [(i, (i - 1) % groups) for i in range(groups)])
    block_2 = third(right_2, *got_2, *late_2)
    back_2 = lax.ppermute(
        turned(block_2), "kp", [(i, (i - 2 if i % 2 else i + 2) % groups) for i in range(groups)]
    )
    back_1 = gathered(back_1)
    back_2 = gathered(back_2)
    block_1 = block_1.transpose(1, 0, 2)
    block_2 = block_2.transpose(1, 0, 2)
    return jnp.stack(
        [block_1, jnp.where(odd, block_2, back_2), back_1, jnp.where(odd, back_2, block_2)], axis=0
    )


def solution(mesh):
    placed = (P("kp", None, None, "own"), P("own"))
    return jax.shard_map(
        body,
        mesh=mesh,
        in_specs=placed,
        out_specs=P(None, ("kp", "own"), None, None),
        check_vma=False,
    )
```

```python
import math

import jax
import jax.numpy as jnp
import numpy as np
from jax import lax
from jax.sharding import PartitionSpec as P

BLOCK = 32


def natural_order(owners, block_count):
    rows = np.arange(owners * block_count * BLOCK)
    owner, block, place = rows // (block_count * BLOCK), rows // BLOCK % block_count, rows % BLOCK
    return (block * owners + owner) * BLOCK + place


def body(pair_density, coulomb):
    points, transitions, _, g_local = pair_density.shape
    row_total = points * transitions
    owners = lax.axis_size("own")
    groups = lax.axis_size("kp")
    own_rows = row_total // owners
    half = own_rows // 2
    block_count = own_rows // BLOCK
    scale = 1.0 / math.sqrt(g_local * owners)
    me = lax.axis_index("own")
    odd = lax.axis_index("kp") % 2 == 1

    near_raw = lax.ppermute(pair_density, "kp", [(i, (i + 1) % groups) for i in range(groups)])
    ahead_raw = lax.ppermute(pair_density, "kp", [(i, (i - 2) % groups) for i in range(0, groups, 2)])

    def planes(raw):
        return raw.reshape(row_total, 2 * g_local)

    weighted = (pair_density.astype(jnp.float32) * coulomb).astype(jnp.bfloat16)
    weighted = weighted.reshape(block_count, owners, BLOCK, 2, g_local)
    weighted = jnp.roll(weighted, -me, axis=1)
    weighted = weighted.transpose(1, 3, 0, 2, 4).reshape(owners, 2, own_rows, g_local)
    real_part, imag_part = weighted[:, 0], weighted[:, 1]
    left = jnp.stack(
        [
            jnp.concatenate([real_part, imag_part], axis=-1),
            jnp.concatenate([-imag_part, real_part], axis=-1),
        ],
        axis=1,
    )

    def product(rows, right):
        out = lax.dot_general(
            rows, right, (((2,), (1,)), ((), ())), preferred_element_type=jnp.float32
        )
        return out * scale

    up = [(o, (o + 1) % owners) for o in range(owners)]
    down = [(o, (o - 1) % owners) for o in range(owners)]

    def second_products(right, from_down, from_up):
        to_up = product(left[1, :, :half], right) + from_down[:, :half].astype(jnp.float32)
        to_down = product(left[3, :, half:], right) + from_up[:, half:].astype(jnp.float32)
        return to_up.astype(jnp.bfloat16), to_down.astype(jnp.bfloat16)

    def third(right, from_down, from_up, late_down, late_up):
        low = product(left[0, :, :half], right) + from_up[:, :half].astype(jnp.float32) + late_down.astype(jnp.float32)
        high = product(left[0, :, half:], right) + from_down[:, half:].astype(jnp.float32) + late_up.astype(jnp.float32)
        return jnp.concatenate([low, high], axis=1).astype(jnp.bfloat16)

    order = natural_order(owners, block_count)
    pick = jnp.asarray(np.eye(row_total, dtype=np.float32)[order], jnp.bfloat16)

    def turned(block):
        sign = jnp.array([1.0, -1.0], jnp.bfloat16).reshape(2, 1, 1)
        out = lax.dot_general(
            pick, block * sign, (((1,), (2,)), ((), ())), preferred_element_type=jnp.float32
        )
        return out.astype(jnp.bfloat16)

    def gathered(pieces):
        swapped = lax.all_to_all(
            pieces.reshape(owners, own_rows, 2, own_rows), "own", split_axis=0, concat_axis=0, tiled=True
        )
        swapped = swapped.transpose(1, 2, 0, 3).reshape(own_rows, 2, row_total)
        out = lax.dot_general(swapped, pick, (((2,), (0,)), ((), ())), preferred_element_type=jnp.float32)
        return out.astype(jnp.bfloat16)

    def first_products(right):
        to_up = jnp.concatenate([left[2, :, :half], left[1, :, half:]], axis=1)
        to_down = jnp.concatenate([left[3, :, :half], left[2, :, half:]], axis=1)
        return (product(to_up, right).astype(jnp.bfloat16), product(to_down, right).astype(jnp.bfloat16))

    def sends(pieces):
        return lax.ppermute(pieces[0], "own", up), lax.ppermute(pieces[1], "own", down)

    near_raw, ahead_raw, left = lax.optimization_barrier((near_raw, ahead_raw, left))
    behind_raw = lax.ppermute(near_raw, "kp", [(i, i + 1) for i in range(0, groups, 2)])
    right_1 = planes(near_raw)
    pieces_1 = first_products(right_1)
    got_1 = sends(pieces_1)
    right_2 = planes(jnp.where(odd, behind_raw, ahead_raw))
    pieces_2 = first_products(right_2)
    got_2 = sends(pieces_2)
    got_1, _ = lax.optimization_barrier((got_1, pieces_2))
    late_1 = sends(second_products(right_1, *got_1))
    pieces_2 = second_products(right_2, *got_2)
    late_2 = sends(pieces_2)
    late_1, _ = lax.optimization_barrier((late_1, pieces_2))
    block_1 = third(right_1, *got_1, *late_1)
    back_1 = lax.ppermute(turned(block_1), "kp", [(i, (i - 1) % groups) for i in range(groups)])
    block_2 = third(right_2, *got_2, *late_2)
    back_2 = lax.ppermute(
        turned(block_2), "kp", [(i, (i - 2 if i % 2 else i + 2) % groups) for i in range(groups)]
    )
    back_1 = gathered(back_1)
    back_2 = gathered(back_2)
    block_1 = block_1.transpose(1, 0, 2)
    block_2 = block_2.transpose(1, 0, 2)
    return jnp.stack(
        [block_1, jnp.where(odd, block_2, back_2), back_1, jnp.where(odd, back_2, block_2)], axis=0
    )


def solution(mesh):
    placed = (P("kp", None, None, "own"), P("own"))
    return jax.shard_map(
        body,
        mesh=mesh,
        in_specs=placed,
        out_specs=P(None, ("kp", "own"), None, None),
        check_vma=False,
    )
```

```python
import math

import jax
import jax.numpy as jnp
import numpy as np
from jax import lax
from jax.sharding import PartitionSpec as P

BLOCK = 32


def natural_order(owners, block_count):
    rows = np.arange(owners * block_count * BLOCK)
    owner, block, place = rows // (block_count * BLOCK), rows // BLOCK % block_count, rows % BLOCK
    return (block * owners + owner) * BLOCK + place


def body(pair_density, coulomb):
    points, transitions, _, g_local = pair_density.shape
    row_total = points * transitions
    owners = lax.axis_size("own")
    groups = lax.axis_size("kp")
    own_rows = row_total // owners
    half = own_rows // 2
    block_count = own_rows // BLOCK
    scale = 1.0 / math.sqrt(g_local * owners)
    me = lax.axis_index("own")
    odd = lax.axis_index("kp") % 2 == 1

    near_raw = lax.ppermute(pair_density, "kp", [(i, (i + 1) % groups) for i in range(groups)])
    ahead_raw = lax.ppermute(pair_density, "kp", [(i, (i - 2) % groups) for i in range(0, groups, 2)])

    def planes(raw):
        return raw.reshape(row_total, 2 * g_local)

    weighted = (pair_density.astype(jnp.float32) * coulomb).astype(jnp.bfloat16)
    weighted = weighted.reshape(block_count, owners, BLOCK, 2, g_local)
    weighted = jnp.roll(weighted, -me, axis=1)
    weighted = weighted.transpose(1, 3, 0, 2, 4).reshape(owners, 2, own_rows, g_local)
    real_part, imag_part = weighted[:, 0], weighted[:, 1]
    left = jnp.stack(
        [
            jnp.concatenate([real_part, imag_part], axis=-1),
            jnp.concatenate([-imag_part, real_part], axis=-1),
        ],
        axis=1,
    )

    def product(rows, right):
        out = lax.dot_general(
            rows, right, (((2,), (1,)), ((), ())), preferred_element_type=jnp.float32
        )
        return out * scale

    up = [(o, (o + 1) % owners) for o in range(owners)]
    down = [(o, (o - 1) % owners) for o in range(owners)]

    def second_products(right, from_down, from_up):
        low = jnp.pad(from_down, ((0, 0), (0, half), (0, 0))).astype(jnp.float32)
        high = jnp.pad(from_up, ((0, 0), (half, 0), (0, 0))).astype(jnp.float32)
        to_up = product(left[1], right) + low
        to_down = product(left[3], right) + high
        return to_up.astype(jnp.bfloat16), to_down.astype(jnp.bfloat16)

    def third(right, from_down, from_up):
        out = product(left[0], right) + from_down.astype(jnp.float32) + from_up.astype(jnp.float32)
        return out.astype(jnp.bfloat16)

    order = natural_order(owners, block_count)
    pick = jnp.asarray(np.eye(row_total, dtype=np.float32)[order], jnp.bfloat16)

    def turned(block):
        sign = jnp.array([1.0, -1.0], jnp.bfloat16).reshape(2, 1, 1)
        out = lax.dot_general(
            pick, block * sign, (((1,), (2,)), ((), ())), preferred_element_type=jnp.float32
        )
        return out.astype(jnp.bfloat16)

    def gathered(pieces):
        swapped = lax.all_to_all(
            pieces.reshape(owners, own_rows, 2, own_rows), "own", split_axis=0, concat_axis=0, tiled=True
        )
        swapped = swapped.transpose(1, 2, 0, 3).reshape(own_rows, 2, row_total)
        out = lax.dot_general(swapped, pick, (((2,), (0,)), ((), ())), preferred_element_type=jnp.float32)
        return out.astype(jnp.bfloat16)

    def first_products(right):
        return (
            product(left[2, :, :half], right).astype(jnp.bfloat16),
            product(left[2, :, half:], right).astype(jnp.bfloat16),
        )

    def sends(pieces):
        return lax.ppermute(pieces[0], "own", up), lax.ppermute(pieces[1], "own", down)

    near_raw, ahead_raw, left = lax.optimization_barrier((near_raw, ahead_raw, left))
    behind_raw = lax.ppermute(near_raw, "kp", [(i, i + 1) for i in range(0, groups, 2)])
    right_1 = planes(near_raw)
    pieces_1 = first_products(right_1)
    got_1 = sends(pieces_1)
    right_2 = planes(jnp.where(odd, behind_raw, ahead_raw))
    pieces_2 = first_products(right_2)
    got_2 = sends(pieces_2)
    got_1, _ = lax.optimization_barrier((got_1, pieces_2))
    late_1 = sends(second_products(right_1, *got_1))
    pieces_2 = second_products(right_2, *got_2)
    late_2 = sends(pieces_2)
    late_1, _ = lax.optimization_barrier((late_1, pieces_2))
    block_1 = third(right_1, *late_1)
    back_1 = lax.ppermute(turned(block_1), "kp", [(i, (i - 1) % groups) for i in range(groups)])
    block_2 = third(right_2, *late_2)
    back_2 = lax.ppermute(
        turned(block_2), "kp", [(i, (i - 2 if i % 2 else i + 2) % groups) for i in range(groups)]
    )
    back_1 = gathered(back_1)
    back_2 = gathered(back_2)
    block_1 = block_1.transpose(1, 0, 2)
    block_2 = block_2.transpose(1, 0, 2)
    return jnp.stack(
        [block_1, jnp.where(odd, block_2, back_2), back_1, jnp.where(odd, back_2, block_2)], axis=0
    )


def solution(mesh):
    placed = (P("kp", None, None, "own"), P("own"))
    return jax.shard_map(
        body,
        mesh=mesh,
        in_specs=placed,
        out_specs=P(None, ("kp", "own"), None, None),
        check_vma=False,
    )
```

```python
import math

import jax
import jax.numpy as jnp
import numpy as np
from jax import lax
from jax.sharding import PartitionSpec as P

BLOCK = 32


def natural_order(owners, block_count):
    rows = np.arange(owners * block_count * BLOCK)
    owner, block, place = rows // (block_count * BLOCK), rows // BLOCK % block_count, rows % BLOCK
    return (block * owners + owner) * BLOCK + place


def body(pair_density, coulomb):
    points, transitions, _, g_local = pair_density.shape
    row_total = points * transitions
    owners = lax.axis_size("own")
    groups = lax.axis_size("kp")
    own_rows = row_total // owners
    half = own_rows // 2
    block_count = own_rows // BLOCK
    scale = 1.0 / math.sqrt(g_local * owners)
    me = lax.axis_index("own")
    odd = lax.axis_index("kp") % 2 == 1

    near_raw = lax.ppermute(pair_density, "kp", [(i, (i + 1) % groups) for i in range(groups)])
    ahead_raw = lax.ppermute(pair_density, "kp", [(i, (i - 2) % groups) for i in range(0, groups, 2)])

    def planes(raw):
        return raw.reshape(row_total, 2 * g_local)

    weighted = (pair_density.astype(jnp.float32) * coulomb).astype(jnp.bfloat16)
    weighted = weighted.reshape(block_count, owners, BLOCK, 2, g_local)
    weighted = jnp.roll(weighted, -me, axis=1)
    weighted = weighted.transpose(1, 3, 0, 2, 4).reshape(owners, 2, own_rows, g_local)
    real_part, imag_part = weighted[:, 0], weighted[:, 1]
    left = jnp.stack(
        [
            jnp.concatenate([real_part, imag_part], axis=-1),
            jnp.concatenate([-imag_part, real_part], axis=-1),
        ],
        axis=1,
    )

    def product(rows, right):
        out = lax.dot_general(
            rows, right, (((2,), (1,)), ((), ())), preferred_element_type=jnp.float32
        )
        return out * scale

    up = [(o, (o + 1) % owners) for o in range(owners)]
    down = [(o, (o - 1) % owners) for o in range(owners)]

    def second_products(right, from_down, from_up):
        low = jnp.pad(from_down, ((0, 0), (0, half), (0, 0))).astype(jnp.float32)
        high = jnp.pad(from_up, ((0, 0), (half, 0), (0, 0))).astype(jnp.float32)
        to_up = product(left[1], right) + low
        to_down = product(left[3], right) + high
        return to_up.astype(jnp.bfloat16), to_down.astype(jnp.bfloat16)

    def third(right, from_down, from_up):
        out = product(left[0], right) + from_down.astype(jnp.float32) + from_up.astype(jnp.float32)
        return out.astype(jnp.bfloat16)

    order = natural_order(owners, block_count)
    pick = jnp.asarray(np.eye(row_total, dtype=np.float32)[order], jnp.bfloat16)
    pick = jnp.roll(pick.reshape(owners, own_rows, row_total), -me, axis=0)

    def turned_sends(block, partner):
        sign = jnp.array([1.0, -1.0], jnp.bfloat16).reshape(2, 1, 1)
        block = block * sign
        got = []
        for ahead in range(owners):
            piece = lax.dot_general(
                pick[ahead], block, (((1,), (2,)), ((), ())), preferred_element_type=jnp.float32
            ).astype(jnp.bfloat16)
            pairs = [
                (i * owners + o, partner(i) % groups * owners + (o + ahead) % owners)
                for i in range(groups)
                for o in range(owners)
            ]
            got.append(lax.ppermute(piece, ("kp", "own"), pairs))
        return got

    def natural(got):
        pieces = jnp.concatenate([got[-ahead % owners] for ahead in range(owners)], axis=2)
        out = lax.dot_general(
            pieces, pick.reshape(row_total, row_total), (((2,), (0,)), ((), ())), preferred_element_type=jnp.float32
        )
        return out.astype(jnp.bfloat16)

    def first_products(right):
        return (
            product(left[2, :, :half], right).astype(jnp.bfloat16),
            product(left[2, :, half:], right).astype(jnp.bfloat16),
        )

    def sends(pieces):
        return lax.ppermute(pieces[0], "own", up), lax.ppermute(pieces[1], "own", down)

    near_raw, ahead_raw, left = lax.optimization_barrier((near_raw, ahead_raw, left))
    behind_raw = lax.ppermute(near_raw, "kp", [(i, i + 1) for i in range(0, groups, 2)])
    right_1 = planes(near_raw)
    pieces_1 = first_products(right_1)
    got_1 = sends(pieces_1)
    right_2 = planes(jnp.where(odd, behind_raw, ahead_raw))
    pieces_2 = first_products(right_2)
    got_2 = sends(pieces_2)
    got_1, _ = lax.optimization_barrier((got_1, pieces_2))
    late_1 = sends(second_products(right_1, *got_1))
    pieces_2 = second_products(right_2, *got_2)
    late_2 = sends(pieces_2)
    late_1, _ = lax.optimization_barrier((late_1, pieces_2))
    block_1 = third(right_1, *late_1)
    back_1 = turned_sends(block_1, lambda i: i - 1)
    block_2 = third(right_2, *late_2)
    back_2 = turned_sends(block_2, lambda i: i - 2 if i % 2 else i + 2)
    back_1 = natural(back_1)
    back_2 = natural(back_2)
    block_1 = block_1.transpose(1, 0, 2)
    block_2 = block_2.transpose(1, 0, 2)
    return jnp.stack(
        [block_1, jnp.where(odd, block_2, back_2), back_1, jnp.where(odd, back_2, block_2)], axis=0
    )


def solution(mesh):
    placed = (P("kp", None, None, "own"), P("own"))
    return jax.shard_map(
        body,
        mesh=mesh,
        in_specs=placed,
        out_specs=P(None, ("kp", "own"), None, None),
        check_vma=False,
    )
```

```python
import math

import jax
import jax.numpy as jnp
import numpy as np
from jax import lax
from jax.sharding import PartitionSpec as P

BLOCK = 32


def owner_order(owners, blocks):
    count = owners * blocks * BLOCK
    rows = np.arange(count)
    owner, block, place = rows // (blocks * BLOCK), rows // BLOCK % blocks, rows % BLOCK
    column = (block * owners + owner) * BLOCK + place
    return np.eye(count, dtype=np.float32)[column].reshape(owners, blocks * BLOCK, count)


def body(pair_density, coulomb):
    points, transitions, _, g_local = pair_density.shape
    owners = lax.axis_size("own")
    groups = lax.axis_size("kp")
    blocks = transitions // (owners * BLOCK)
    rows = blocks * BLOCK
    depth = 2 * g_local
    scale = 1.0 / math.sqrt(g_local * owners)
    me = lax.axis_index("own")
    odd = lax.axis_index("kp") % 2 == 1
    parity = odd.astype(jnp.int32)

    def exchange_kp(value, partner):
        return lax.ppermute(value, "kp", [(i, partner(i) % groups) for i in range(groups)])

    def exchange_own(value, first):
        pairs = []
        for i in range(groups):
            flip = 1 if (i % 2 == 0) == first else 3
            pairs += [(i * owners + o, i * owners + (o ^ flip)) for o in range(owners)]
        return lax.ppermute(value, ("kp", "own"), pairs)

    def mate(i):
        return i + 1 if i % 2 == 0 else i - 1

    def across(i):
        return i - 1 if i % 2 == 0 else i + 1

    def second_next(i):
        return i + 2 if i % 2 == 0 else i - 2

    near_flip, far_flip = 1 + 2 * parity, 3 - 2 * parity
    relative = [me ^ near_flip, me ^ 2, me ^ far_flip, me]
    swapped = [me ^ far_flip, me ^ 2, me ^ near_flip, me]

    def by_owner(value, order, axis):
        return [lax.dynamic_index_in_dim(value, o, axis, keepdims=False) for o in order]

    plain = pair_density.reshape(points, transitions, depth)
    sent = jnp.stack([lax.dynamic_index_in_dim(plain, parity, 0, False), lax.dynamic_index_in_dim(plain, 1 - parity, 0, False)])
    mate_right = exchange_kp(sent, mate)
    next_right = exchange_kp(sent, across)

    weights = jnp.concatenate([coulomb, coulomb]) * scale
    weighted = (plain.astype(jnp.float32) * weights).astype(jnp.bfloat16)
    turned_weighted = jnp.concatenate([-weighted[..., g_local:], weighted[..., :g_local]], axis=-1)
    left = jnp.stack([weighted, turned_weighted], axis=1)
    left = left.reshape(points, 2, blocks, owners, BLOCK, depth)
    pieces = [x.reshape(points, 2 * rows, depth) for x in by_owner(left, relative, 3)]
    left_away = jnp.concatenate(pieces[:2], axis=1)
    left_second, left_own = pieces[2], pieces[3]

    def product(left_rows, right):
        return lax.dot_general(
            left_rows, right, (((2,), (2,)), ((0,), (0,))), preferred_element_type=jnp.float32
        )

    def whole(left_rows, right):
        out = lax.dot_general(
            left_rows.reshape(-1, depth),
            right.reshape(-1, depth),
            (((1,), (1,)), ((), ())),
            preferred_element_type=jnp.float32,
        )
        return out.reshape(points, -1, points * transitions)

    def wide(value):
        return value.astype(jnp.float32)

    def low(value):
        return value.astype(jnp.bfloat16)

    left_away, left_second, left_own, mate_right = lax.optimization_barrier(
        (left_away, left_second, left_own, mate_right)
    )
    away_mate = low(product(left_away, mate_right))
    next_right, _ = lax.optimization_barrier((next_right, away_mate))
    got_mate = exchange_own(away_mate, True)
    far_right = exchange_kp(next_right, mate)
    away_next = low(product(left_away, next_right))
    far_right, _ = lax.optimization_barrier((far_right, away_next))
    got_next = exchange_own(away_next, True)
    away_far = low(whole(left_away, far_right))
    got_mate, got_next, _ = lax.optimization_barrier((got_mate, got_next, away_far))
    got_far = exchange_own(away_far, True)

    def kept(got, slot):
        return wide(got[:, slot * 2 * rows : (slot + 1) * 2 * rows])

    second_pair = jnp.concatenate(
        [
            low(product(left_second, mate_right) + kept(got_mate, 1)),
            low(product(left_second, next_right) + kept(got_next, 1)),
        ],
        axis=2,
    )
    late_pair = exchange_own(second_pair, False)
    second_far = low(whole(left_second, far_right) + kept(got_far, 1))
    late_pair, _ = lax.optimization_barrier((late_pair, second_far))
    late_far = exchange_own(second_far, False)

    def finished(total):
        total = low(total).reshape(points, 2, rows, -1)
        return total.transpose(1, 0, 2, 3).reshape(2, points * rows, -1)

    block_mate = finished(product(left_own, mate_right) + kept(got_mate, 0) + wide(late_pair[..., :transitions]))
    block_next = finished(product(left_own, next_right) + kept(got_next, 0) + wide(late_pair[..., transitions:]))
    block_far = finished(whole(left_own, far_right) + kept(got_far, 0) + wide(late_far))

    pick_columns = jnp.asarray(owner_order(owners, blocks), jnp.bfloat16)
    pick_same = jnp.concatenate(by_owner(pick_columns, relative, 0), axis=0)
    pick_other = jnp.concatenate(by_owner(pick_columns, swapped, 0), axis=0)
    pick_rows = jnp.asarray(owner_order(owners, points * blocks), jnp.bfloat16)
    pick_rows = jnp.concatenate(by_owner(pick_rows, relative, 0), axis=0)
    sign = jnp.array([1.0, -1.0], jnp.bfloat16).reshape(2, 1, 1)

    def turned(block, pick):
        out = lax.dot_general(
            pick, block * sign, (((1,), (2,)), ((), ())), preferred_element_type=jnp.float32
        )
        return low(out).reshape(owners, rows, 2, points * rows)

    back_mate = exchange_kp(turned(block_mate, pick_other), mate)
    back_next = exchange_kp(turned(block_next, pick_other), across)
    back_far = exchange_kp(
        jnp.concatenate([turned(block_far[..., :transitions], pick_same), turned(block_far[..., transitions:], pick_same)], axis=1),
        second_next,
    )

    def natural(tiles, first, second):
        joined = jnp.concatenate([first[0], second[1], second[0], tiles[3]], axis=-1)
        out = lax.dot_general(joined, pick_rows, (((2,), (0,)), ((), ())), preferred_element_type=jnp.float32)
        return low(out)

    back_pair = jnp.concatenate([back_mate, back_next], axis=1)
    first_pair = exchange_own(back_pair[:2], True)
    first_far = exchange_own(back_far[:2], True)
    then_pair = exchange_own(jnp.stack([back_pair[2], first_pair[1]]), False)
    then_far = exchange_own(jnp.stack([back_far[2], first_far[1]]), False)
    back_pair = natural(back_pair, first_pair, then_pair)
    back_far = natural(back_far, first_far, then_far)

    def mixed(block, back):
        block = block.reshape(2, points, rows, transitions).transpose(1, 2, 0, 3)
        back = back.reshape(rows, 2, points, transitions)
        out = []
        for row_point in range(points):
            line = []
            for column_point in range(points):
                here = odd if row_point == column_point else ~odd
                line.append(jnp.where(here, block[row_point], back[:, :, column_point]))
            out.append(jnp.concatenate(line, axis=-1))
        return jnp.concatenate(out, axis=0)

    with_mate = mixed(block_mate, back_pair[:rows])
    with_next = mixed(block_next, back_pair[rows:])
    here_far = block_far.transpose(1, 0, 2)
    here_far = jnp.where(odd, jnp.roll(here_far, transitions, axis=2), here_far)
    back_far = jnp.where(odd, jnp.roll(back_far, rows, axis=0), back_far)
    return jnp.stack(
        [
            jnp.where(odd, with_mate, with_next),
            jnp.where(odd, here_far, back_far),
            jnp.where(odd, with_next, with_mate),
            jnp.where(odd, back_far, here_far),
        ],
        axis=0,
    )


def solution(mesh):
    placed = (P("kp", None, None, "own"), P("own"))
    return jax.shard_map(
        body,
        mesh=mesh,
        in_specs=placed,
        out_specs=P(None, ("kp", "own"), None, None),
        check_vma=False,
    )
```

```python
import math

import jax
import jax.numpy as jnp
import numpy as np
from jax import lax
from jax.experimental import pallas as pl
from jax.experimental.pallas import tpu as pltpu
from jax.sharding import PartitionSpec as P

BLOCK = 32


def owner_order(owners, blocks):
    count = owners * blocks * BLOCK
    rows = np.arange(count)
    owner, block, place = rows // (blocks * BLOCK), rows // BLOCK % blocks, rows % BLOCK
    column = (block * owners + owner) * BLOCK + place
    return np.eye(count, dtype=np.float32)[column].reshape(owners, blocks * BLOCK, count)


def local(kernel, shapes, *operands, scalars=0):
    vmem = pl.BlockSpec(memory_space=pltpu.VMEM)
    smem = pl.BlockSpec(memory_space=pltpu.SMEM)
    several = len(shapes) > 1
    out_shape = [jax.ShapeDtypeStruct(s, jnp.bfloat16) for s in shapes]
    return pl.pallas_call(
        kernel,
        out_shape=out_shape if several else out_shape[0],
        in_specs=[smem] * scalars + [vmem] * (len(operands) - scalars),
        out_specs=[vmem] * len(shapes) if several else vmem,
        compiler_params=pltpu.CompilerParams(vmem_limit_bytes=40 * 1024 * 1024),
        cost_estimate=pl.CostEstimate(flops=0, transcendentals=0, bytes_accessed=0),
    )(*operands)


def dots(left, right):
    return lax.dot_general(left, right, (((1,), (1,)), ((), ())), preferred_element_type=jnp.float32)


def low(value):
    return value.astype(jnp.bfloat16)


def wide(value):
    return value.astype(jnp.float32)


def left_kernel(order_ref, plain_ref, weight_ref, left_ref):
    points, transitions, depth = plain_ref.shape
    owners = order_ref.shape[0]
    blocks = transitions // (owners * BLOCK)
    weight = weight_ref[...]
    for point in range(points):
        for slot in range(owners):
            for block in range(blocks):
                start = pl.multiple_of((block * owners + order_ref[slot]) * BLOCK, BLOCK)
                rows = wide(plain_ref[point, pl.ds(start, BLOCK), :]) * weight
                place = pl.ds(block * BLOCK, BLOCK)
                left_ref[point, slot, 0, place, :] = low(rows)
                left_ref[point, slot, 1, place, : depth // 2] = low(-rows[:, depth // 2 :])
                left_ref[point, slot, 1, place, depth // 2 :] = low(rows[:, : depth // 2])


def away_kernel(left_ref, right_ref, out_ref):
    for point in range(out_ref.shape[0]):
        out_ref[point] = low(dots(left_ref[point], right_ref[point]))


def away_whole_kernel(left_ref, right_ref, out_ref):
    points, _, columns = out_ref.shape
    count = columns // points
    for point in range(points):
        for part in range(points):
            out_ref[point, :, part * count : (part + 1) * count] = low(dots(left_ref[point], right_ref[part]))


def second_pair_kernel(left_ref, mate_ref, next_ref, got_mate_ref, got_next_ref, out_ref):
    points, count, columns = out_ref.shape
    half = columns // 2
    for point in range(points):
        for part, (right_ref, got_ref) in enumerate(((mate_ref, got_mate_ref), (next_ref, got_next_ref))):
            total = dots(left_ref[point], right_ref[point]) + wide(got_ref[point, count:, :])
            out_ref[point, :, part * half : (part + 1) * half] = low(total)


def second_whole_kernel(left_ref, right_ref, got_ref, out_ref):
    points, count, columns = out_ref.shape
    half = columns // points
    for point in range(points):
        for part in range(points):
            span = pl.ds(part * half, half)
            total = dots(left_ref[point], right_ref[part]) + wide(got_ref[point, count:, span])
            out_ref[point, :, span] = low(total)


def picked(order_ref, slot, rows, owners, transitions):
    n = lax.broadcasted_iota(jnp.int32, (rows, transitions), 0)
    column = lax.broadcasted_iota(jnp.int32, (rows, transitions), 1)
    target = (n // BLOCK * owners + order_ref[slot]) * BLOCK + n % BLOCK
    return low(jnp.where(column == target, 1.0, 0.0))


def turn(order_ref, block_ref, span, back_ref, index):
    points, count, _ = block_ref.shape
    rows = count // 2
    owners = order_ref.shape[0]
    stacked = jnp.concatenate(
        [block_ref[point, p * rows : (p + 1) * rows, span] for p in range(2) for point in range(points)], axis=0
    )
    for slot in range(owners):
        pick = picked(order_ref, slot, rows, owners, stacked.shape[1])
        out = dots(pick, stacked)
        back_ref[slot, *index, 0] = low(out[:, : points * rows])
        back_ref[slot, *index, 1] = low(-out[:, points * rows :])


def finish_pair_kernel(
    order_ref, left_ref, mate_ref, next_ref, got_mate_ref, got_next_ref, late_ref,
    mate_block_ref, next_block_ref, mate_back_ref, next_back_ref,
):
    points, count, half = mate_block_ref.shape
    for part, (right_ref, got_ref, block_ref, back_ref) in enumerate(
        (
            (mate_ref, got_mate_ref, mate_block_ref, mate_back_ref),
            (next_ref, got_next_ref, next_block_ref, next_back_ref),
        )
    ):
        for point in range(points):
            total = dots(left_ref[point], right_ref[point]) + wide(got_ref[point, :count, :])
            block_ref[point] = low(total + wide(late_ref[point, :, part * half : (part + 1) * half]))
        turn(order_ref, block_ref, pl.ds(0, half), back_ref, ())


def finish_whole_kernel(order_ref, left_ref, right_ref, got_ref, late_ref, block_ref, back_ref):
    points, count, columns = block_ref.shape
    half = columns // points
    for part in range(points):
        span = pl.ds(part * half, half)
        for point in range(points):
            total = dots(left_ref[point], right_ref[part]) + wide(got_ref[point, :count, span])
            block_ref[point, :, span] = low(total + wide(late_ref[point, :, span]))
        turn(order_ref, block_ref, span, back_ref, (part,))


def body(pair_density, coulomb):
    points, transitions, _, g_local = pair_density.shape
    owners = lax.axis_size("own")
    groups = lax.axis_size("kp")
    blocks = transitions // (owners * BLOCK)
    rows = blocks * BLOCK
    depth = 2 * g_local
    scale = 1.0 / math.sqrt(g_local * owners)
    me = lax.axis_index("own")
    odd = lax.axis_index("kp") % 2 == 1
    parity = odd.astype(jnp.int32)

    def exchange_kp(value, partner):
        return lax.ppermute(value, "kp", [(i, partner(i) % groups) for i in range(groups)])

    def flips(i):
        return [1, 2, 3, 0] if i % 2 == 0 else [3, 2, 1, 0]

    def exchange(value, slot, partner):
        pairs = [
            (i * owners + o, partner(i) % groups * owners + (o ^ flips(i)[slot]))
            for i in range(groups)
            for o in range(owners)
        ]
        return lax.ppermute(value, ("kp", "own"), pairs)

    def exchange_own(value, first):
        return exchange(value, 0 if first else 2, lambda i: i)

    def mate(i):
        return i + 1 if i % 2 == 0 else i - 1

    def across(i):
        return i - 1 if i % 2 == 0 else i + 1

    def second_next(i):
        return i + 2 if i % 2 == 0 else i - 2

    near_flip, far_flip = 1 + 2 * parity, 3 - 2 * parity
    relative = jnp.stack([me ^ near_flip, me ^ 2, me ^ far_flip, me])
    swapped = jnp.stack([me ^ far_flip, me ^ 2, me ^ near_flip, me])

    plain = pair_density.reshape(points, transitions, depth)
    sent = jnp.stack([lax.dynamic_index_in_dim(plain, parity, 0, False), lax.dynamic_index_in_dim(plain, 1 - parity, 0, False)])
    mate_right = exchange_kp(sent, mate)
    next_right = exchange_kp(sent, across)

    weights = (jnp.concatenate([coulomb, coulomb]) * scale).reshape(1, depth)
    left = local(left_kernel, [(points, owners, 2, rows, depth)], relative, plain, weights, scalars=1)
    left_away = left[:, :2].reshape(points, 4 * rows, depth)
    left_second = left[:, 2].reshape(points, 2 * rows, depth)
    left_own = left[:, 3].reshape(points, 2 * rows, depth)

    left_away, left_second, left_own, mate_right = lax.optimization_barrier(
        (left_away, left_second, left_own, mate_right)
    )
    half_shape = (points, 4 * rows, transitions)
    whole_shape = (points, 4 * rows, points * transitions)
    late_shape = (points, 2 * rows, points * transitions)
    away_mate = local(away_kernel, [half_shape], left_away, mate_right)
    next_right, _ = lax.optimization_barrier((next_right, away_mate))
    got_mate = exchange_own(away_mate, True)
    far_right = exchange_kp(next_right, mate)
    away_next = local(away_kernel, [half_shape], left_away, next_right)
    far_right, _ = lax.optimization_barrier((far_right, away_next))
    got_next = exchange_own(away_next, True)
    away_far = local(away_whole_kernel, [whole_shape], left_away, far_right)
    got_mate, got_next, _ = lax.optimization_barrier((got_mate, got_next, away_far))
    got_far = exchange_own(away_far, True)

    second_pair = local(second_pair_kernel, [late_shape], left_second, mate_right, next_right, got_mate, got_next)
    late_pair = exchange_own(second_pair, False)
    second_far = local(second_whole_kernel, [late_shape], left_second, far_right, got_far)
    late_pair, _ = lax.optimization_barrier((late_pair, second_far))
    late_far = exchange_own(second_far, False)

    half_block = (points, 2 * rows, transitions)
    half_back = (owners, 2, rows, points * rows)
    block_mate, block_next, back_mate, back_next = local(
        finish_pair_kernel, [half_block, half_block, half_back, half_back],
        swapped, left_own, mate_right, next_right, got_mate, got_next, late_pair, scalars=1,
    )
    back_mate = exchange_kp(back_mate, mate)
    back_next = exchange_kp(back_next, across)
    block_far, back_far = local(
        finish_whole_kernel, [late_shape, (owners, points, 2, rows, points * rows)],
        relative, left_own, far_right, got_far, late_far, scalars=1,
    )
    back_far = [exchange(back_far[slot], slot, second_next) for slot in range(owners)]

    pick_rows = jnp.asarray(owner_order(owners, points * blocks), jnp.bfloat16)
    pick_rows = jnp.concatenate([lax.dynamic_index_in_dim(pick_rows, relative[slot], 0, False) for slot in range(owners)], axis=0)

    def natural(tiles):
        joined = jnp.concatenate(tiles, axis=-1)
        out = lax.dot_general(joined, pick_rows, (((3,), (0,)), ((), ())), preferred_element_type=jnp.float32)
        return low(out)

    back_pair = jnp.stack([back_mate, back_next], axis=1)
    first = exchange_own(back_pair[:2], True)
    then = exchange_own(jnp.stack([back_pair[2], first[1]]), False)
    back_pair = natural([first[0], then[1], then[0], back_pair[3]])
    back_far = natural(back_far)

    def mixed(block, back):
        block = block.reshape(points, 2, rows, transitions)
        back = back.reshape(2, rows, points, transitions)
        out = []
        for row_point in range(points):
            line = []
            for column_point in range(points):
                here = odd if row_point == column_point else ~odd
                line.append(jnp.where(here, block[row_point], back[:, :, column_point]))
            out.append(jnp.concatenate(line, axis=-1))
        return jnp.stack(out)

    with_mate = mixed(block_mate, back_pair[0])
    with_next = mixed(block_next, back_pair[1])
    here_far = block_far.reshape(points, 2, rows, points * transitions)
    here_far = jnp.where(odd, jnp.roll(here_far, transitions, axis=3), here_far)
    back_far = jnp.where(odd, back_far[::-1], back_far)
    out = jnp.stack(
        [
            jnp.where(odd, with_mate, with_next),
            jnp.where(odd, here_far, back_far),
            jnp.where(odd, with_next, with_mate),
            jnp.where(odd, back_far, here_far),
        ],
        axis=0,
    )
    return out.transpose(0, 1, 3, 2, 4).reshape(4, points * rows, 2, points * transitions)


def solution(mesh):
    placed = (P("kp", None, None, "own"), P("own"))
    return jax.shard_map(
        body,
        mesh=mesh,
        in_specs=placed,
        out_specs=P(None, ("kp", "own"), None, None),
        check_vma=False,
    )
```

```python
import math

import jax
import jax.numpy as jnp
import numpy as np
from jax import lax
from jax.experimental import pallas as pl
from jax.experimental.pallas import tpu as pltpu
from jax.sharding import PartitionSpec as P

BLOCK = 32


def owner_order(owners, blocks):
    count = owners * blocks * BLOCK
    rows = np.arange(count)
    owner, block, place = rows // (blocks * BLOCK), rows // BLOCK % blocks, rows % BLOCK
    column = (block * owners + owner) * BLOCK + place
    return np.eye(count, dtype=np.float32)[column].reshape(owners, blocks * BLOCK, count)


def local(kernel, shapes, *operands, scalars=0):
    vmem = pl.BlockSpec(memory_space=pltpu.VMEM)
    smem = pl.BlockSpec(memory_space=pltpu.SMEM)
    several = len(shapes) > 1
    out_shape = [jax.ShapeDtypeStruct(s, jnp.bfloat16) for s in shapes]
    return pl.pallas_call(
        kernel,
        out_shape=out_shape if several else out_shape[0],
        in_specs=[smem] * scalars + [vmem] * (len(operands) - scalars),
        out_specs=[vmem] * len(shapes) if several else vmem,
        compiler_params=pltpu.CompilerParams(vmem_limit_bytes=40 * 1024 * 1024),
        cost_estimate=pl.CostEstimate(flops=0, transcendentals=0, bytes_accessed=0),
    )(*operands)


def dots(left, right):
    return lax.dot_general(left, right, (((1,), (1,)), ((), ())), preferred_element_type=jnp.float32)


def low(value):
    return value.astype(jnp.bfloat16)


def wide(value):
    return value.astype(jnp.float32)


def left_kernel(order_ref, plain_ref, weight_ref, left_ref):
    points, transitions, depth = plain_ref.shape
    owners = order_ref.shape[0] - 1
    blocks = transitions // (owners * BLOCK)
    weight = weight_ref[...]
    for point in range(points):
        for slot in range(owners):
            for block in range(blocks):
                start = pl.multiple_of((block * owners + order_ref[slot]) * BLOCK, BLOCK)
                rows = wide(plain_ref[point, pl.ds(start, BLOCK), :]) * weight
                place = pl.ds(block * BLOCK, BLOCK)
                left_ref[point, slot, 0, place, :] = low(rows)
                left_ref[point, slot, 1, place, : depth // 2] = low(-rows[:, depth // 2 :])
                left_ref[point, slot, 1, place, depth // 2 :] = low(rows[:, : depth // 2])


def agreeing(order_ref, point):
    even = order_ref[order_ref.shape[0] - 1]
    return point + even - 2 * even * point


def away_kernel(order_ref, left_ref, right_ref, out_ref):
    for point in range(out_ref.shape[0]):
        out_ref[point] = low(dots(left_ref[point], right_ref[agreeing(order_ref, point)]))


def away_whole_kernel(left_ref, right_ref, out_ref):
    points, _, columns = out_ref.shape
    count = columns // points
    for point in range(points):
        for part in range(points):
            out_ref[point, :, part * count : (part + 1) * count] = low(dots(left_ref[point], right_ref[part]))


def second_kernel(order_ref, left_ref, right_ref, got_ref, out_ref):
    points, count, _ = out_ref.shape
    for point in range(points):
        total = dots(left_ref[point], right_ref[agreeing(order_ref, point)])
        out_ref[point] = low(total + wide(got_ref[point, count:, :]))


def second_whole_kernel(left_ref, right_ref, got_ref, out_ref):
    points, count, columns = out_ref.shape
    half = columns // points
    for point in range(points):
        for part in range(points):
            span = pl.ds(part * half, half)
            total = dots(left_ref[point], right_ref[part]) + wide(got_ref[point, count:, span])
            out_ref[point, :, span] = low(total)


def picked(order_ref, slot, rows, owners, transitions):
    n = lax.broadcasted_iota(jnp.int32, (rows, transitions), 0)
    column = lax.broadcasted_iota(jnp.int32, (rows, transitions), 1)
    target = (n // BLOCK * owners + order_ref[slot]) * BLOCK + n % BLOCK
    return low(jnp.where(column == target, 1.0, 0.0))


def turn(order_ref, block_ref, span, back_ref, index):
    points, count, _ = block_ref.shape
    rows = count // 2
    owners = order_ref.shape[0] - 1
    stacked = jnp.concatenate(
        [block_ref[point, p * rows : (p + 1) * rows, span] for p in range(2) for point in range(points)], axis=0
    )
    for slot in range(owners):
        pick = picked(order_ref, slot, rows, owners, stacked.shape[1])
        out = dots(pick, stacked)
        back_ref[slot, *index, 0] = low(out[:, : points * rows])
        back_ref[slot, *index, 1] = low(-out[:, points * rows :])


def finish_kernel(order_ref, left_ref, right_ref, got_ref, late_ref, block_ref, back_ref):
    points, count, columns = block_ref.shape
    for point in range(points):
        total = dots(left_ref[point], right_ref[agreeing(order_ref, point)]) + wide(got_ref[point, :count, :])
        block_ref[point] = low(total + wide(late_ref[point]))
    turn(order_ref, block_ref, pl.ds(0, columns), back_ref, ())


def finish_whole_kernel(order_ref, left_ref, right_ref, got_ref, late_ref, block_ref, back_ref):
    points, count, columns = block_ref.shape
    half = columns // points
    for part in range(points):
        span = pl.ds(part * half, half)
        for point in range(points):
            total = dots(left_ref[point], right_ref[part]) + wide(got_ref[point, :count, span])
            block_ref[point, :, span] = low(total + wide(late_ref[point, :, span]))
        turn(order_ref, block_ref, span, back_ref, (part,))


def body(pair_density, coulomb):
    points, transitions, _, g_local = pair_density.shape
    owners = lax.axis_size("own")
    groups = lax.axis_size("kp")
    blocks = transitions // (owners * BLOCK)
    rows = blocks * BLOCK
    depth = 2 * g_local
    scale = 1.0 / math.sqrt(g_local * owners)
    me = lax.axis_index("own")
    odd = lax.axis_index("kp") % 2 == 1
    parity = odd.astype(jnp.int32)

    def exchange_kp(value, partner):
        return lax.ppermute(value, "kp", [(i, partner(i) % groups) for i in range(groups)])

    def flips(i):
        return [1, 2, 3, 0] if i % 2 == 0 else [3, 2, 1, 0]

    def exchange(value, slot, partner):
        pairs = [
            (i * owners + o, partner(i) % groups * owners + (o ^ flips(i)[slot]))
            for i in range(groups)
            for o in range(owners)
        ]
        return lax.ppermute(value, ("kp", "own"), pairs)

    def exchange_own(value, first):
        return exchange(value, 0 if first else 2, lambda i: i)

    def mate(i):
        return i + 1 if i % 2 == 0 else i - 1

    def across(i):
        return i - 1 if i % 2 == 0 else i + 1

    def second_next(i):
        return i + 2 if i % 2 == 0 else i - 2

    near_flip, far_flip = 1 + 2 * parity, 3 - 2 * parity
    relative = jnp.stack([me ^ near_flip, me ^ 2, me ^ far_flip, me, 1 - parity])
    swapped = jnp.stack([me ^ far_flip, me ^ 2, me ^ near_flip, me, 1 - parity])

    plain = pair_density.reshape(points, transitions, depth)
    mate_right = exchange_kp(plain, mate)
    next_right = exchange_kp(plain, across)

    weights = (jnp.concatenate([coulomb, coulomb]) * scale).reshape(1, depth)
    left = local(left_kernel, [(points, owners, 2, rows, depth)], relative, plain, weights, scalars=1)
    left_away = left[:, :2].reshape(points, 4 * rows, depth)
    left_second = left[:, 2].reshape(points, 2 * rows, depth)
    left_own = left[:, 3].reshape(points, 2 * rows, depth)

    left_away, left_second, left_own, mate_right = lax.optimization_barrier(
        (left_away, left_second, left_own, mate_right)
    )
    half_away = [(points, 4 * rows, transitions)]
    whole_away = [(points, 4 * rows, points * transitions)]
    half_block = (points, 2 * rows, transitions)
    whole_block = (points, 2 * rows, points * transitions)
    half_back = (owners, 2, rows, points * rows)
    whole_back = (owners, points, 2, rows, points * rows)

    away_mate = local(away_kernel, half_away, relative, left_away, mate_right, scalars=1)
    got_mate = exchange_own(away_mate, True)
    second_mate = local(second_kernel, [half_block], relative, left_second, mate_right, got_mate, scalars=1)
    late_mate = exchange_own(second_mate, False)
    next_right, _ = lax.optimization_barrier((next_right, second_mate))
    far_right = exchange_kp(next_right, mate)
    away_next = local(away_kernel, half_away, relative, left_away, next_right, scalars=1)
    got_next = exchange_own(away_next, True)
    far_right, _ = lax.optimization_barrier((far_right, away_next))
    away_far = local(away_whole_kernel, whole_away, left_away, far_right)
    got_far = exchange_own(away_far, True)
    late_mate, _ = lax.optimization_barrier((late_mate, away_far))
    block_mate, back_mate = local(
        finish_kernel, [half_block, half_back], swapped, left_own, mate_right, got_mate, late_mate, scalars=1
    )
    got_next, _ = lax.optimization_barrier((got_next, back_mate))
    back_mate = exchange_kp(back_mate, mate)
    second_next_part = local(second_kernel, [half_block], relative, left_second, next_right, got_next, scalars=1)
    late_next = exchange_own(second_next_part, False)
    block_next, back_next = local(
        finish_kernel, [half_block, half_back], swapped, left_own, next_right, got_next, late_next, scalars=1
    )
    got_far, _ = lax.optimization_barrier((got_far, back_next))
    back_next = exchange_kp(back_next, across)
    second_far = local(second_whole_kernel, [whole_block], left_second, far_right, got_far)
    late_far = exchange_own(second_far, False)
    back_pair = jnp.stack([back_mate, back_next], axis=1)
    back_pair, _ = lax.optimization_barrier((back_pair, second_far))
    first = exchange_own(back_pair[:2], True)
    then = jnp.stack([back_pair[2], first[1]])
    late_far, _ = lax.optimization_barrier((late_far, then))
    then = exchange_own(then, False)
    block_far, back_far = local(
        finish_whole_kernel, [whole_block, whole_back], relative, left_own, far_right, got_far, late_far, scalars=1
    )
    back_far = [exchange(back_far[slot], slot, second_next) for slot in range(owners)]

    pick_rows = jnp.asarray(owner_order(owners, points * blocks), jnp.bfloat16)
    pick_rows = jnp.concatenate([lax.dynamic_index_in_dim(pick_rows, relative[slot], 0, False) for slot in range(owners)], axis=0)

    def natural(tiles):
        joined = jnp.concatenate(tiles, axis=-1)
        out = lax.dot_general(joined, pick_rows, (((3,), (0,)), ((), ())), preferred_element_type=jnp.float32)
        return low(out)

    back_pair = natural([first[0], then[1], then[0], back_pair[3]])
    back_far = natural(back_far)

    def mixed(block, back):
        block = block.reshape(points, 2, rows, transitions)
        back = back.reshape(2, rows, points, transitions)
        out = []
        for row_point in range(points):
            line = []
            for column_point in range(points):
                here = odd if row_point == column_point else ~odd
                line.append(jnp.where(here, block[row_point], back[:, :, column_point]))
            out.append(jnp.concatenate(line, axis=-1))
        return jnp.stack(out)

    with_mate = mixed(block_mate, back_pair[0])
    with_next = mixed(block_next, back_pair[1])
    here_far = block_far.reshape(points, 2, rows, points * transitions)
    out = jnp.stack(
        [
            jnp.where(odd, with_mate, with_next),
            jnp.where(odd, here_far, back_far),
            jnp.where(odd, with_next, with_mate),
            jnp.where(odd, back_far, here_far),
        ],
        axis=0,
    )
    return out.transpose(0, 1, 3, 2, 4).reshape(4, points * rows, 2, points * transitions)


def solution(mesh):
    placed = (P("kp", None, None, "own"), P("own"))
    return jax.shard_map(
        body,
        mesh=mesh,
        in_specs=placed,
        out_specs=P(None, ("kp", "own"), None, None),
        check_vma=False,
    )
```

```python
import math

import jax
import jax.numpy as jnp
import numpy as np
from jax import lax
from jax.experimental import pallas as pl
from jax.experimental.pallas import tpu as pltpu
from jax.sharding import PartitionSpec as P

BLOCK = 32


def owner_order(owners, blocks):
    count = owners * blocks * BLOCK
    rows = np.arange(count)
    owner, block, place = rows // (blocks * BLOCK), rows // BLOCK % blocks, rows % BLOCK
    column = (block * owners + owner) * BLOCK + place
    return np.eye(count, dtype=np.float32)[column].reshape(owners, blocks * BLOCK, count)


def local(kernel, shapes, *operands, scalars=0):
    vmem = pl.BlockSpec(memory_space=pltpu.VMEM)
    smem = pl.BlockSpec(memory_space=pltpu.SMEM)
    several = len(shapes) > 1
    out_shape = [jax.ShapeDtypeStruct(s, jnp.bfloat16) for s in shapes]
    return pl.pallas_call(
        kernel,
        out_shape=out_shape if several else out_shape[0],
        in_specs=[smem] * scalars + [vmem] * (len(operands) - scalars),
        out_specs=[vmem] * len(shapes) if several else vmem,
        compiler_params=pltpu.CompilerParams(vmem_limit_bytes=40 * 1024 * 1024),
        cost_estimate=pl.CostEstimate(flops=0, transcendentals=0, bytes_accessed=0),
    )(*operands)


def dots(left, right):
    return lax.dot_general(left, right, (((1,), (1,)), ((), ())), preferred_element_type=jnp.float32)


def low(value):
    return value.astype(jnp.bfloat16)


def wide(value):
    return value.astype(jnp.float32)


def left_kernel(order_ref, plain_ref, weight_ref, left_ref):
    points, transitions, depth = plain_ref.shape
    owners = order_ref.shape[0] - 1
    blocks = transitions // (owners * BLOCK)
    weight = weight_ref[...]
    for point in range(points):
        for slot in range(owners):
            for block in range(blocks):
                start = pl.multiple_of((block * owners + order_ref[slot]) * BLOCK, BLOCK)
                rows = wide(plain_ref[point, pl.ds(start, BLOCK), :]) * weight
                place = pl.ds(block * BLOCK, BLOCK)
                left_ref[point, slot, 0, place, :] = low(rows)
                left_ref[point, slot, 1, place, : depth // 2] = low(-rows[:, depth // 2 :])
                left_ref[point, slot, 1, place, depth // 2 :] = low(rows[:, : depth // 2])


def agreeing(order_ref, point):
    even = order_ref[order_ref.shape[0] - 1]
    return point + even - 2 * even * point


def pair_kernel(order_ref, left_ref, mate_ref, next_ref, out_ref):
    _, points, count, columns = out_ref.shape
    half = columns // 2
    for slot in range(order_ref.shape[0] - 1):
        for point in range(points):
            rows = left_ref[point, slot].reshape(count, -1)
            for part, right_ref in enumerate((mate_ref, next_ref)):
                out_ref[order_ref[slot], point, :, part * half : (part + 1) * half] = low(
                    dots(rows, right_ref[agreeing(order_ref, point)])
                )


def away_kernel(left_ref, right_ref, out_ref):
    points, _, columns = out_ref.shape
    half = columns // points
    for point in range(points):
        for part in range(points):
            out_ref[point, :, part * half : (part + 1) * half] = low(dots(left_ref[point], right_ref[part]))


def second_kernel(left_ref, right_ref, got_ref, out_ref):
    points, count, columns = out_ref.shape
    half = columns // points
    for point in range(points):
        for part in range(points):
            span = pl.ds(part * half, half)
            out_ref[point, :, span] = low(dots(left_ref[point], right_ref[part]) + wide(got_ref[point, count:, span]))


def picked(order_ref, slot, rows, owners, transitions):
    n = lax.broadcasted_iota(jnp.int32, (rows, transitions), 0)
    column = lax.broadcasted_iota(jnp.int32, (rows, transitions), 1)
    target = (n // BLOCK * owners + order_ref[slot]) * BLOCK + n % BLOCK
    return low(jnp.where(column == target, 1.0, 0.0))


def turn(order_ref, block_ref, span, back_ref, index):
    points, count, _ = block_ref.shape
    rows = count // 2
    owners = order_ref.shape[0] - 1
    stacked = jnp.concatenate(
        [block_ref[point, p * rows : (p + 1) * rows, span] for p in range(2) for point in range(points)], axis=0
    )
    for slot in range(owners):
        pick = picked(order_ref, slot, rows, owners, stacked.shape[1])
        out = dots(pick, stacked)
        back_ref[slot, *index, 0] = low(out[:, : points * rows])
        back_ref[slot, *index, 1] = low(-out[:, points * rows :])


def finish_kernel(order_ref, left_ref, right_ref, got_ref, late_ref, block_ref, back_ref):
    points, count, columns = block_ref.shape
    half = columns // points
    for part in range(points):
        span = pl.ds(part * half, half)
        for point in range(points):
            total = dots(left_ref[point], right_ref[part]) + wide(got_ref[point, :count, span])
            block_ref[point, :, span] = low(total + wide(late_ref[point, :, span]))
        turn(order_ref, block_ref, span, back_ref, (part,))


def turn_kernel(order_ref, block_ref, mate_back_ref, next_back_ref):
    half = block_ref.shape[2] // 2
    turn(order_ref, block_ref, pl.ds(0, half), mate_back_ref, ())
    turn(order_ref, block_ref, pl.ds(half, half), next_back_ref, ())


def body(pair_density, coulomb):
    points, transitions, _, g_local = pair_density.shape
    owners = lax.axis_size("own")
    groups = lax.axis_size("kp")
    blocks = transitions // (owners * BLOCK)
    rows = blocks * BLOCK
    depth = 2 * g_local
    scale = 1.0 / math.sqrt(g_local * owners)
    me = lax.axis_index("own")
    odd = lax.axis_index("kp") % 2 == 1
    parity = odd.astype(jnp.int32)

    def exchange_kp(value, partner):
        return lax.ppermute(value, "kp", [(i, partner(i) % groups) for i in range(groups)])

    def flips(i):
        return [1, 2, 3, 0] if i % 2 == 0 else [3, 2, 1, 0]

    def exchange(value, slot, partner):
        pairs = [
            (i * owners + o, partner(i) % groups * owners + (o ^ flips(i)[slot]))
            for i in range(groups)
            for o in range(owners)
        ]
        return lax.ppermute(value, ("kp", "own"), pairs)

    def exchange_own(value, first):
        return exchange(value, 0 if first else 2, lambda i: i)

    def mate(i):
        return i + 1 if i % 2 == 0 else i - 1

    def across(i):
        return i - 1 if i % 2 == 0 else i + 1

    def second_next(i):
        return i + 2 if i % 2 == 0 else i - 2

    near_flip, far_flip = 1 + 2 * parity, 3 - 2 * parity
    relative = jnp.stack([me ^ near_flip, me ^ 2, me ^ far_flip, me, 1 - parity])
    swapped = jnp.stack([me ^ far_flip, me ^ 2, me ^ near_flip, me, 1 - parity])

    plain = pair_density.reshape(points, transitions, depth)
    mate_right = exchange_kp(plain, mate)
    next_right = exchange_kp(plain, across)

    weights = (jnp.concatenate([coulomb, coulomb]) * scale).reshape(1, depth)
    left = local(left_kernel, [(points, owners, 2, rows, depth)], relative, plain, weights, scalars=1)
    left_away = left[:, :2].reshape(points, 4 * rows, depth)
    left_second = left[:, 2].reshape(points, 2 * rows, depth)
    left_own = left[:, 3].reshape(points, 2 * rows, depth)

    left_away, left_second, left_own, mate_right = lax.optimization_barrier(
        (left_away, left_second, left_own, mate_right)
    )
    columns = points * transitions
    half_back = (owners, 2, rows, points * rows)
    pair = local(
        pair_kernel, [(owners, points, 2 * rows, columns)], relative, left, mate_right, next_right, scalars=1
    )
    block_pair = lax.psum_scatter(pair.reshape(-1, columns), "own", scatter_dimension=0, tiled=True)
    block_pair = block_pair.reshape(points, 2 * rows, columns)
    far_right = exchange_kp(next_right, mate)
    far_right, _ = lax.optimization_barrier((far_right, pair))
    away = local(away_kernel, [(points, 4 * rows, columns)], left_away, far_right)
    got = exchange_own(away, True)
    second = local(second_kernel, [(points, 2 * rows, columns)], left_second, far_right, got)
    late = exchange_own(second, False)
    back_mate, back_next = local(turn_kernel, [half_back, half_back], swapped, block_pair, scalars=1)
    back_mate = exchange_kp(back_mate, mate)
    back_next = exchange_kp(back_next, across)
    back_pair = jnp.stack([back_mate, back_next], axis=1)
    first = exchange_own(back_pair[:2], True)
    then = exchange_own(jnp.stack([back_pair[2], first[1]]), False)
    block_far, back_far = local(
        finish_kernel, [(points, 2 * rows, columns), (owners, points, 2, rows, points * rows)],
        relative, left_own, far_right, got, late, scalars=1,
    )
    back_far = [exchange(back_far[slot], slot, second_next) for slot in range(owners)]
    block_mate, block_next = block_pair[..., :transitions], block_pair[..., transitions:]

    pick_rows = jnp.asarray(owner_order(owners, points * blocks), jnp.bfloat16)
    pick_rows = jnp.concatenate([lax.dynamic_index_in_dim(pick_rows, relative[slot], 0, False) for slot in range(owners)], axis=0)

    def natural(tiles):
        joined = jnp.concatenate(tiles, axis=-1)
        out = lax.dot_general(joined, pick_rows, (((3,), (0,)), ((), ())), preferred_element_type=jnp.float32)
        return low(out)

    back_pair = natural([first[0], then[1], then[0], back_pair[3]])
    back_far = natural(back_far)

    def mixed(block, back):
        block = block.reshape(points, 2, rows, transitions)
        back = back.reshape(2, rows, points, transitions)
        out = []
        for row_point in range(points):
            line = []
            for column_point in range(points):
                here = odd if row_point == column_point else ~odd
                line.append(jnp.where(here, block[row_point], back[:, :, column_point]))
            out.append(jnp.concatenate(line, axis=-1))
        return jnp.stack(out)

    with_mate = mixed(block_mate, back_pair[0])
    with_next = mixed(block_next, back_pair[1])
    here_far = block_far.reshape(points, 2, rows, points * transitions)
    out = jnp.stack(
        [
            jnp.where(odd, with_mate, with_next),
            jnp.where(odd, here_far, back_far),
            jnp.where(odd, with_next, with_mate),
            jnp.where(odd, back_far, here_far),
        ],
        axis=0,
    )
    return out.transpose(0, 1, 3, 2, 4).reshape(4, points * rows, 2, points * transitions)


def solution(mesh):
    placed = (P("kp", None, None, "own"), P("own"))
    return jax.shard_map(
        body,
        mesh=mesh,
        in_specs=placed,
        out_specs=P(None, ("kp", "own"), None, None),
        check_vma=False,
    )
```

```python
import math

import jax
import jax.numpy as jnp
import numpy as np
from jax import lax
from jax.experimental import pallas as pl
from jax.experimental.pallas import tpu as pltpu
from jax.sharding import PartitionSpec as P

BLOCK = 32


def owner_order(owners, blocks):
    count = owners * blocks * BLOCK
    rows = np.arange(count)
    owner, block, place = rows // (blocks * BLOCK), rows // BLOCK % blocks, rows % BLOCK
    column = (block * owners + owner) * BLOCK + place
    return np.eye(count, dtype=np.float32)[column].reshape(owners, blocks * BLOCK, count)


def local(kernel, shapes, *operands, scalars=0):
    vmem = pl.BlockSpec(memory_space=pltpu.VMEM)
    smem = pl.BlockSpec(memory_space=pltpu.SMEM)
    several = len(shapes) > 1
    out_shape = [jax.ShapeDtypeStruct(s, jnp.bfloat16) for s in shapes]
    return pl.pallas_call(
        kernel,
        out_shape=out_shape if several else out_shape[0],
        in_specs=[smem] * scalars + [vmem] * (len(operands) - scalars),
        out_specs=[vmem] * len(shapes) if several else vmem,
        compiler_params=pltpu.CompilerParams(vmem_limit_bytes=40 * 1024 * 1024),
        cost_estimate=pl.CostEstimate(flops=0, transcendentals=0, bytes_accessed=0),
    )(*operands)


def dots(left, right):
    return lax.dot_general(left, right, (((1,), (1,)), ((), ())), preferred_element_type=jnp.float32)


def low(value):
    return value.astype(jnp.bfloat16)


def wide(value):
    return value.astype(jnp.float32)


def left_kernel(order_ref, plain_ref, weight_ref, left_ref):
    points, transitions, depth = plain_ref.shape
    owners = order_ref.shape[0] - 1
    blocks = transitions // (owners * BLOCK)
    weight = weight_ref[...]
    for point in range(points):
        for slot in range(owners):
            for block in range(blocks):
                start = pl.multiple_of((block * owners + order_ref[slot]) * BLOCK, BLOCK)
                rows = wide(plain_ref[point, pl.ds(start, BLOCK), :]) * weight
                place = pl.ds(block * BLOCK, BLOCK)
                left_ref[point, slot, 0, place, :] = low(rows)
                left_ref[point, slot, 1, place, : depth // 2] = low(-rows[:, depth // 2 :])
                left_ref[point, slot, 1, place, depth // 2 :] = low(rows[:, : depth // 2])


def agreeing(order_ref, point):
    even = order_ref[order_ref.shape[0] - 1]
    return point + even - 2 * even * point


def away_pair_kernel(order_ref, left_ref, mate_ref, next_ref, out_ref):
    points, _, columns = out_ref.shape
    half = columns // 2
    for point in range(points):
        for part, right_ref in enumerate((mate_ref, next_ref)):
            out_ref[point, :, part * half : (part + 1) * half] = low(
                dots(left_ref[point], right_ref[agreeing(order_ref, point)])
            )


def away_far_kernel(left_ref, right_ref, out_ref):
    points, _, columns = out_ref.shape
    half = columns // points
    for point in range(points):
        for part in range(points):
            out_ref[point, :, part * half : (part + 1) * half] = low(dots(left_ref[point], right_ref[part]))


def picked(order_ref, slots, rows, owners, transitions):
    n = lax.broadcasted_iota(jnp.int32, (rows, transitions), 0)
    column = lax.broadcasted_iota(jnp.int32, (rows, transitions), 1)
    target = (n // BLOCK * owners) * BLOCK + n % BLOCK
    return jnp.concatenate(
        [low(jnp.where(column == target + order_ref[slot] * BLOCK, 1.0, 0.0)) for slot in slots], axis=0
    )


def second_part(order_ref, second_left, own_left, right, got_ref, point, part, out_ref):
    count = out_ref.shape[1]
    half = right.shape[0]
    owners = order_ref.shape[0] - 1
    span = pl.ds(part * half, half)
    out_ref[point, :, span] = low(dots(second_left, right) + wide(got_ref[point, count:, span]))
    own = low(dots(own_left, right) + wide(got_ref[point, :count, span]))
    pick = picked(order_ref, (2, 1), count // 2, owners, half)
    out_ref[point, :, pl.ds(2 * half + part * count, count)] = low(dots(own, pick))


def second_pair_kernel(order_ref, second_left_ref, own_left_ref, mate_ref, next_ref, got_ref, out_ref):
    for point in range(out_ref.shape[0]):
        for part, right_ref in enumerate((mate_ref, next_ref)):
            right = right_ref[agreeing(order_ref, point)]
            second_part(order_ref, second_left_ref[point], own_left_ref[point], right, got_ref, point, part, out_ref)


def second_far_kernel(order_ref, second_left_ref, own_left_ref, right_ref, got_ref, out_ref):
    for point in range(out_ref.shape[0]):
        for part in range(out_ref.shape[0]):
            second_part(
                order_ref, second_left_ref[point], own_left_ref[point], right_ref[part], got_ref, point, part, out_ref
            )


def turned_part(order_ref, block_ref, second_ref, late_ref, part, same_ref, first_ref, index):
    points, count, columns = block_ref.shape
    half = columns // 2
    rows = count // 2
    owners = order_ref.shape[0] - 1
    span = pl.ds(part * half, half)
    own = jnp.concatenate(
        [block_ref[point, p * rows : (p + 1) * rows, span] for p in range(2) for point in range(points)], axis=0
    )
    pick = picked(order_ref, (3, 0), rows, owners, half)
    others = []
    for point in range(points):
        other = dots(second_ref[point, :, span], pick) + wide(late_ref[point, :, pl.ds(columns + part * count, count)])
        others.append(low(other))
    other = jnp.concatenate(
        [others[point][p * rows : (p + 1) * rows] for p in range(2) for point in range(points)], axis=0
    )
    n = lax.broadcasted_iota(jnp.int32, (count, count), 0)
    same = low(jnp.where(n == lax.broadcasted_iota(jnp.int32, (count, count), 1), 1.0, 0.0))
    for source, out in enumerate((dots(pick, own), dots(same, other))):
        for to, ref in enumerate((same_ref, first_ref)):
            piece = out[to * rows : (to + 1) * rows]
            ref[source, *index, 0] = low(piece[:, : points * rows])
            ref[source, *index, 1] = low(-piece[:, points * rows :])


def finish_pair_kernel(
    order_ref, left_ref, mate_ref, next_ref, got_ref, second_ref, late_ref,
    block_ref, mate_same_ref, mate_first_ref, next_same_ref, next_first_ref,
):
    points, count, columns = block_ref.shape
    half = columns // 2
    for part, (right_ref, same_ref, first_ref) in enumerate(
        ((mate_ref, mate_same_ref, mate_first_ref), (next_ref, next_same_ref, next_first_ref))
    ):
        span = pl.ds(part * half, half)
        for point in range(points):
            total = dots(left_ref[point], right_ref[agreeing(order_ref, point)])
            total = total + wide(got_ref[point, :count, span]) + wide(late_ref[point, :, span])
            block_ref[point, :, span] = low(total)
        turned_part(order_ref, block_ref, second_ref, late_ref, part, same_ref, first_ref, ())


def finish_far_kernel(
    order_ref, left_ref, right_ref, got_ref, second_ref, late_ref, block_ref, same_ref, first_ref
):
    points, count, columns = block_ref.shape
    half = columns // points
    for part in range(points):
        span = pl.ds(part * half, half)
        for point in range(points):
            total = dots(left_ref[point], right_ref[part])
            total = total + wide(got_ref[point, :count, span]) + wide(late_ref[point, :, span])
            block_ref[point, :, span] = low(total)
        turned_part(order_ref, block_ref, second_ref, late_ref, part, same_ref, first_ref, (part,))


def body(pair_density, coulomb):
    points, transitions, _, g_local = pair_density.shape
    owners = lax.axis_size("own")
    groups = lax.axis_size("kp")
    blocks = transitions // (owners * BLOCK)
    rows = blocks * BLOCK
    depth = 2 * g_local
    scale = 1.0 / math.sqrt(g_local * owners)
    me = lax.axis_index("own")
    odd = lax.axis_index("kp") % 2 == 1
    parity = odd.astype(jnp.int32)

    def exchange_kp(value, partner):
        return lax.ppermute(value, "kp", [(i, partner(i) % groups) for i in range(groups)])

    def flips(i):
        return [1, 2, 3, 0] if i % 2 == 0 else [3, 2, 1, 0]

    def exchange(value, slot, partner):
        pairs = [
            (i * owners + o, partner(i) % groups * owners + (o ^ flips(i)[slot]))
            for i in range(groups)
            for o in range(owners)
        ]
        return lax.ppermute(value, ("kp", "own"), pairs)

    def exchange_own(value, first):
        return exchange(value, 0 if first else 2, lambda i: i)

    def mate(i):
        return i + 1 if i % 2 == 0 else i - 1

    def across(i):
        return i - 1 if i % 2 == 0 else i + 1

    def second_next(i):
        return i + 2 if i % 2 == 0 else i - 2

    near_flip, far_flip = 1 + 2 * parity, 3 - 2 * parity
    relative = jnp.stack([me ^ near_flip, me ^ 2, me ^ far_flip, me, 1 - parity])
    swapped = jnp.stack([me ^ far_flip, me ^ 2, me ^ near_flip, me, 1 - parity])

    plain = pair_density.reshape(points, transitions, depth)
    mate_right = exchange_kp(plain, mate)
    next_right = exchange_kp(plain, across)

    weights = (jnp.concatenate([coulomb, coulomb]) * scale).reshape(1, depth)
    left = local(left_kernel, [(points, owners, 2, rows, depth)], relative, plain, weights, scalars=1)
    left_away = left[:, :2].reshape(points, 4 * rows, depth)
    left_second = left[:, 2].reshape(points, 2 * rows, depth)
    left_own = left[:, 3].reshape(points, 2 * rows, depth)

    left_away, left_second, left_own, mate_right = lax.optimization_barrier(
        (left_away, left_second, left_own, mate_right)
    )
    columns = points * transitions
    away_shape = [(points, 4 * rows, columns)]
    second_shape = [(points, 2 * rows, columns + 4 * rows)]
    block_shape = (points, 2 * rows, columns)
    pair_back = (2, 2, rows, points * rows)
    far_back = (2, points, 2, rows, points * rows)

    far_right = exchange_kp(next_right, mate)
    away_pair = local(away_pair_kernel, away_shape, relative, left_away, mate_right, next_right, scalars=1)
    got_pair = exchange_own(away_pair, True)
    far_right, _ = lax.optimization_barrier((far_right, away_pair))
    away_far = local(away_far_kernel, away_shape, left_away, far_right)
    got_far = exchange_own(away_far, True)
    got_pair, _ = lax.optimization_barrier((got_pair, away_far))
    second_pair = local(
        second_pair_kernel, second_shape,
        relative, left_second, left_own, mate_right, next_right, got_pair, scalars=1,
    )
    late_pair = exchange_own(second_pair, False)
    second_far = local(
        second_far_kernel, second_shape, relative, left_second, left_own, far_right, got_far, scalars=1
    )
    late_pair, _ = lax.optimization_barrier((late_pair, second_far))
    late_far = exchange_own(second_far, False)
    block_pair, mate_same, mate_first, next_same, next_first = local(
        finish_pair_kernel, [block_shape] + [pair_back] * 4,
        relative, left_own, mate_right, next_right, got_pair, second_pair, late_pair, scalars=1,
    )
    mate_back = exchange(mate_same, 3, mate), exchange(mate_first, 0, mate)
    next_back = exchange(next_same, 3, across), exchange(next_first, 0, across)
    block_far, far_same, far_first = local(
        finish_far_kernel, [block_shape, far_back, far_back],
        relative, left_own, far_right, got_far, second_far, late_far, scalars=1,
    )
    far_back = exchange(far_same, 3, second_next), exchange(far_first, 0, second_next)

    pick_rows = jnp.asarray(owner_order(owners, points * blocks), jnp.bfloat16)

    def natural(back, order):
        same, first = back
        pick = jnp.concatenate(
            [lax.dynamic_index_in_dim(pick_rows, order[slot], 0, False) for slot in range(owners)], axis=0
        )
        joined = jnp.concatenate([first[0], first[1], same[1], same[0]], axis=-1)
        joined = joined.reshape(-1, 2, rows, columns)
        out = lax.dot_general(joined, pick, (((3,), (0,)), ((), ())), preferred_element_type=jnp.float32)
        return low(out)

    back_far = natural(far_back, relative)
    block_mate, block_next = block_pair[..., :transitions], block_pair[..., transitions:]

    def mixed(block, back):
        block = block.reshape(points, 2, rows, transitions)
        back = back.reshape(2, rows, points, transitions)
        out = []
        for row_point in range(points):
            line = []
            for column_point in range(points):
                here = odd if row_point == column_point else ~odd
                line.append(jnp.where(here, block[row_point], back[:, :, column_point]))
            out.append(jnp.concatenate(line, axis=-1))
        return jnp.stack(out)

    with_mate = mixed(block_mate, natural(mate_back, swapped)[0])
    with_next = mixed(block_next, natural(next_back, swapped)[0])
    here_far = block_far.reshape(points, 2, rows, points * transitions)
    out = jnp.stack(
        [
            jnp.where(odd, with_mate, with_next),
            jnp.where(odd, here_far, back_far),
            jnp.where(odd, with_next, with_mate),
            jnp.where(odd, back_far, here_far),
        ],
        axis=0,
    )
    return out.transpose(0, 1, 3, 2, 4).reshape(4, points * rows, 2, points * transitions)


def solution(mesh):
    placed = (P("kp", None, None, "own"), P("own"))
    return jax.shard_map(
        body,
        mesh=mesh,
        in_specs=placed,
        out_specs=P(None, ("kp", "own"), None, None),
        check_vma=False,
    )
```

```python
import math

import jax
import jax.numpy as jnp
import numpy as np
from jax import lax
from jax.experimental import pallas as pl
from jax.experimental.pallas import tpu as pltpu
from jax.sharding import PartitionSpec as P

BLOCK = 32


def owner_order(owners, blocks):
    count = owners * blocks * BLOCK
    rows = np.arange(count)
    owner, block, place = rows // (blocks * BLOCK), rows // BLOCK % blocks, rows % BLOCK
    column = (block * owners + owner) * BLOCK + place
    return np.eye(count, dtype=np.float32)[column].reshape(owners, blocks * BLOCK, count)


def local(kernel, shapes, *operands, scalars=0, moved=0):
    vmem = pl.BlockSpec(memory_space=pltpu.VMEM)
    smem = pl.BlockSpec(memory_space=pltpu.SMEM)
    several = len(shapes) > 1
    out_shape = [jax.ShapeDtypeStruct(s, jnp.bfloat16) for s in shapes]
    return pl.pallas_call(
        kernel,
        out_shape=out_shape if several else out_shape[0],
        in_specs=[smem] * scalars + [vmem] * (len(operands) - scalars),
        out_specs=[vmem] * len(shapes) if several else vmem,
        compiler_params=pltpu.CompilerParams(vmem_limit_bytes=40 * 1024 * 1024),
        cost_estimate=pl.CostEstimate(flops=0, transcendentals=0, bytes_accessed=moved),
    )(*operands)


def dots(left, right):
    return lax.dot_general(left, right, (((1,), (1,)), ((), ())), preferred_element_type=jnp.float32)


def low(value):
    return value.astype(jnp.bfloat16)


def wide(value):
    return value.astype(jnp.float32)


def left_kernel(order_ref, plain_ref, weight_ref, left_ref):
    points, transitions, depth = plain_ref.shape
    owners = order_ref.shape[0] - 1
    blocks = transitions // (owners * BLOCK)
    weight = weight_ref[...]
    for point in range(points):
        for slot in range(owners):
            for block in range(blocks):
                start = pl.multiple_of((block * owners + order_ref[slot]) * BLOCK, BLOCK)
                rows = wide(plain_ref[point, pl.ds(start, BLOCK), :]) * weight
                place = pl.ds(block * BLOCK, BLOCK)
                left_ref[point, slot, 0, place, :] = low(rows)
                left_ref[point, slot, 1, place, : depth // 2] = low(-rows[:, depth // 2 :])
                left_ref[point, slot, 1, place, depth // 2 :] = low(rows[:, : depth // 2])


def agreeing(order_ref, point):
    even = order_ref[order_ref.shape[0] - 1]
    return point + even - 2 * even * point


def away_pair_kernel(order_ref, left_ref, mate_ref, next_ref, out_ref):
    points, _, columns = out_ref.shape
    half = columns // 2
    for point in range(points):
        for part, right_ref in enumerate((mate_ref, next_ref)):
            out_ref[point, :, part * half : (part + 1) * half] = low(
                dots(left_ref[point], right_ref[agreeing(order_ref, point)])
            )


def away_far_kernel(left_ref, right_ref, out_ref):
    points, _, columns = out_ref.shape
    half = columns // points
    for point in range(points):
        for part in range(points):
            out_ref[point, :, part * half : (part + 1) * half] = low(dots(left_ref[point], right_ref[part]))


def picked(order_ref, slots, rows, owners, transitions):
    n = lax.broadcasted_iota(jnp.int32, (rows, transitions), 0)
    column = lax.broadcasted_iota(jnp.int32, (rows, transitions), 1)
    target = (n // BLOCK * owners) * BLOCK + n % BLOCK
    return jnp.concatenate(
        [low(jnp.where(column == target + order_ref[slot] * BLOCK, 1.0, 0.0)) for slot in slots], axis=0
    )


def second_part(order_ref, second_left, own_left, right, got_ref, point, part, out_ref):
    count = out_ref.shape[1]
    half = right.shape[0]
    owners = order_ref.shape[0] - 1
    span = pl.ds(part * half, half)
    out_ref[point, :, span] = low(dots(second_left, right) + wide(got_ref[point, count:, span]))
    own = low(dots(own_left, right) + wide(got_ref[point, :count, span]))
    pick = picked(order_ref, (2, 1), count // 2, owners, half)
    out_ref[point, :, pl.ds(2 * half + part * count, count)] = low(dots(own, pick))


def second_pair_kernel(order_ref, second_left_ref, own_left_ref, mate_ref, next_ref, got_ref, out_ref):
    for point in range(out_ref.shape[0]):
        for part, right_ref in enumerate((mate_ref, next_ref)):
            right = right_ref[agreeing(order_ref, point)]
            second_part(order_ref, second_left_ref[point], own_left_ref[point], right, got_ref, point, part, out_ref)


def second_far_kernel(order_ref, second_left_ref, own_left_ref, right_ref, got_ref, out_ref):
    for point in range(out_ref.shape[0]):
        for part in range(out_ref.shape[0]):
            second_part(
                order_ref, second_left_ref[point], own_left_ref[point], right_ref[part], got_ref, point, part, out_ref
            )


def turned_part(order_ref, block_ref, second_ref, late_ref, part, same_ref, first_ref, index):
    points, count, columns = block_ref.shape
    half = columns // 2
    rows = count // 2
    owners = order_ref.shape[0] - 1
    span = pl.ds(part * half, half)
    own = jnp.concatenate(
        [block_ref[point, p * rows : (p + 1) * rows, span] for p in range(2) for point in range(points)], axis=0
    )
    pick = picked(order_ref, (3, 0), rows, owners, half)
    others = []
    for point in range(points):
        other = dots(second_ref[point, :, span], pick) + wide(late_ref[point, :, pl.ds(columns + part * count, count)])
        others.append(low(other))
    other = jnp.concatenate(
        [others[point][p * rows : (p + 1) * rows] for p in range(2) for point in range(points)], axis=0
    )
    n = lax.broadcasted_iota(jnp.int32, (count, count), 0)
    same = low(jnp.where(n == lax.broadcasted_iota(jnp.int32, (count, count), 1), 1.0, 0.0))
    for source, out in enumerate((dots(pick, own), dots(same, other))):
        for to, ref in enumerate((same_ref, first_ref)):
            piece = out[to * rows : (to + 1) * rows]
            ref[source, *index, 0] = low(piece[:, : points * rows])
            ref[source, *index, 1] = low(-piece[:, points * rows :])


def finish_pair_kernel(
    order_ref, left_ref, mate_ref, next_ref, got_ref, second_ref, late_ref,
    block_ref, mate_same_ref, mate_first_ref, next_same_ref, next_first_ref,
):
    points, count, columns = block_ref.shape
    half = columns // 2
    for part, (right_ref, same_ref, first_ref) in enumerate(
        ((mate_ref, mate_same_ref, mate_first_ref), (next_ref, next_same_ref, next_first_ref))
    ):
        span = pl.ds(part * half, half)
        for point in range(points):
            total = dots(left_ref[point], right_ref[agreeing(order_ref, point)])
            total = total + wide(got_ref[point, :count, span]) + wide(late_ref[point, :, span])
            block_ref[point, :, span] = low(total)
        turned_part(order_ref, block_ref, second_ref, late_ref, part, same_ref, first_ref, ())


def finish_far_kernel(
    order_ref, left_ref, right_ref, got_ref, second_ref, late_ref, block_ref, same_ref, first_ref
):
    points, count, columns = block_ref.shape
    half = columns // points
    for part in range(points):
        span = pl.ds(part * half, half)
        for point in range(points):
            total = dots(left_ref[point], right_ref[part])
            total = total + wide(got_ref[point, :count, span]) + wide(late_ref[point, :, span])
            block_ref[point, :, span] = low(total)
        turned_part(order_ref, block_ref, second_ref, late_ref, part, same_ref, first_ref, (part,))


def body(pair_density, coulomb):
    points, transitions, _, g_local = pair_density.shape
    owners = lax.axis_size("own")
    groups = lax.axis_size("kp")
    blocks = transitions // (owners * BLOCK)
    rows = blocks * BLOCK
    depth = 2 * g_local
    scale = 1.0 / math.sqrt(g_local * owners)
    me = lax.axis_index("own")
    odd = lax.axis_index("kp") % 2 == 1
    parity = odd.astype(jnp.int32)

    def exchange_kp(value, partner):
        return lax.ppermute(value, "kp", [(i, partner(i) % groups) for i in range(groups)])

    def flips(i):
        return [1, 2, 3, 0] if i % 2 == 0 else [3, 2, 1, 0]

    def exchange(value, slot, partner):
        pairs = [
            (i * owners + o, partner(i) % groups * owners + (o ^ flips(i)[slot]))
            for i in range(groups)
            for o in range(owners)
        ]
        return lax.ppermute(value, ("kp", "own"), pairs)

    def exchange_own(value, first):
        return exchange(value, 0 if first else 2, lambda i: i)

    def mate(i):
        return i + 1 if i % 2 == 0 else i - 1

    def across(i):
        return i - 1 if i % 2 == 0 else i + 1

    def second_next(i):
        return i + 2 if i % 2 == 0 else i - 2

    near_flip, far_flip = 1 + 2 * parity, 3 - 2 * parity
    relative = jnp.stack([me ^ near_flip, me ^ 2, me ^ far_flip, me, 1 - parity])
    swapped = jnp.stack([me ^ far_flip, me ^ 2, me ^ near_flip, me, 1 - parity])

    plain = pair_density.reshape(points, transitions, depth)
    mate_right = exchange_kp(plain, mate)
    next_right = exchange_kp(plain, across)

    weights = (jnp.concatenate([coulomb, coulomb]) * scale).reshape(1, depth)
    left = local(left_kernel, [(points, owners, 2, rows, depth)], relative, plain, weights, scalars=1, moved=4 << 20)
    left_away = left[:, :2].reshape(points, 4 * rows, depth)
    left_second = left[:, 2].reshape(points, 2 * rows, depth)
    left_own = left[:, 3].reshape(points, 2 * rows, depth)

    left_away, left_second, left_own, mate_right = lax.optimization_barrier(
        (left_away, left_second, left_own, mate_right)
    )
    columns = points * transitions
    away_shape = [(points, 4 * rows, columns)]
    second_shape = [(points, 2 * rows, columns + 4 * rows)]
    block_shape = (points, 2 * rows, columns)
    pair_back = (2, 2, rows, points * rows)
    far_back = (2, points, 2, rows, points * rows)

    away_pair = local(away_pair_kernel, away_shape, relative, left_away, mate_right, next_right, scalars=1)
    got_pair = exchange_own(away_pair, True)
    passed_on, _ = lax.optimization_barrier((next_right, away_pair))
    far_right = exchange_kp(passed_on, mate)
    second_pair = local(
        second_pair_kernel, second_shape,
        relative, left_second, left_own, mate_right, next_right, got_pair, scalars=1,
    )
    late_pair = exchange_own(second_pair, False)
    far_right, _ = lax.optimization_barrier((far_right, second_pair))
    away_far = local(away_far_kernel, away_shape, left_away, far_right)
    got_far = exchange_own(away_far, True)
    late_pair, _ = lax.optimization_barrier((late_pair, away_far))
    block_pair, mate_same, mate_first, next_same, next_first = local(
        finish_pair_kernel, [block_shape] + [pair_back] * 4,
        relative, left_own, mate_right, next_right, got_pair, second_pair, late_pair, scalars=1,
    )
    mate_back = exchange(mate_same, 3, mate), exchange(mate_first, 0, mate)
    next_back = exchange(next_same, 3, across), exchange(next_first, 0, across)
    got_far, _ = lax.optimization_barrier((got_far, block_pair))
    second_far = local(
        second_far_kernel, second_shape, relative, left_second, left_own, far_right, got_far, scalars=1
    )
    late_far = exchange_own(second_far, False)
    mate_back, next_back, _ = lax.optimization_barrier((mate_back, next_back, second_far))
    block_far, far_same, far_first = local(
        finish_far_kernel, [block_shape, far_back, far_back],
        relative, left_own, far_right, got_far, second_far, late_far, scalars=1,
    )
    far_back = exchange(far_same, 3, second_next), exchange(far_first, 0, second_next)

    pick_rows = jnp.asarray(owner_order(owners, points * blocks), jnp.bfloat16)

    def natural(back, order):
        same, first = back
        pick = jnp.concatenate(
            [lax.dynamic_index_in_dim(pick_rows, order[slot], 0, False) for slot in range(owners)], axis=0
        )
        joined = jnp.concatenate([first[0], first[1], same[1], same[0]], axis=-1)
        joined = joined.reshape(-1, 2, rows, columns)
        out = lax.dot_general(joined, pick, (((3,), (0,)), ((), ())), preferred_element_type=jnp.float32)
        return low(out)

    back_far = natural(far_back, relative)
    block_mate, block_next = block_pair[..., :transitions], block_pair[..., transitions:]

    def mixed(block, back):
        block = block.reshape(points, 2, rows, transitions)
        back = back.reshape(2, rows, points, transitions)
        out = []
        for row_point in range(points):
            line = []
            for column_point in range(points):
                here = odd if row_point == column_point else ~odd
                line.append(jnp.where(here, block[row_point], back[:, :, column_point]))
            out.append(jnp.concatenate(line, axis=-1))
        return jnp.stack(out)

    with_mate = mixed(block_mate, natural(mate_back, swapped)[0])
    with_next = mixed(block_next, natural(next_back, swapped)[0])
    here_far = block_far.reshape(points, 2, rows, points * transitions)
    out = jnp.stack(
        [
            jnp.where(odd, with_mate, with_next),
            jnp.where(odd, here_far, back_far),
            jnp.where(odd, with_next, with_mate),
            jnp.where(odd, back_far, here_far),
        ],
        axis=0,
    )
    return out.transpose(0, 1, 3, 2, 4).reshape(4, points * rows, 2, points * transitions)


def solution(mesh):
    placed = (P("kp", None, None, "own"), P("own"))
    return jax.shard_map(
        body,
        mesh=mesh,
        in_specs=placed,
        out_specs=P(None, ("kp", "own"), None, None),
        check_vma=False,
    )
```

```python
import math

import jax
import jax.numpy as jnp
from jax import lax
from jax.experimental import pallas as pl
from jax.experimental.pallas import tpu as pltpu
from jax.sharding import PartitionSpec as P

BLOCK = 32


def local(kernel, shapes, *operands, scalars=0, moved=0):
    vmem = pl.BlockSpec(memory_space=pltpu.VMEM)
    smem = pl.BlockSpec(memory_space=pltpu.SMEM)
    several = len(shapes) > 1
    out_shape = [jax.ShapeDtypeStruct(s, jnp.bfloat16) for s in shapes]
    return pl.pallas_call(
        kernel,
        out_shape=out_shape if several else out_shape[0],
        in_specs=[smem] * scalars + [vmem] * (len(operands) - scalars),
        out_specs=[vmem] * len(shapes) if several else vmem,
        compiler_params=pltpu.CompilerParams(vmem_limit_bytes=40 * 1024 * 1024),
        cost_estimate=pl.CostEstimate(flops=0, transcendentals=0, bytes_accessed=moved),
    )(*operands)


def dots(left, right):
    return lax.dot_general(left, right, (((1,), (1,)), ((), ())), preferred_element_type=jnp.float32)


def low(value):
    return value.astype(jnp.bfloat16)


def wide(value):
    return value.astype(jnp.float32)


def left_kernel(order_ref, plain_ref, weight_ref, left_ref):
    points, transitions, depth = plain_ref.shape
    owners = order_ref.shape[0] - 1
    blocks = transitions // (owners * BLOCK)
    weight = weight_ref[...]
    for point in range(points):
        for slot in range(owners):
            for block in range(blocks):
                start = pl.multiple_of((block * owners + order_ref[slot]) * BLOCK, BLOCK)
                rows = wide(plain_ref[point, pl.ds(start, BLOCK), :]) * weight
                place = pl.ds(block * BLOCK, BLOCK)
                left_ref[point, slot, 0, place, :] = low(rows)
                left_ref[point, slot, 1, place, : depth // 2] = low(-rows[:, depth // 2 :])
                left_ref[point, slot, 1, place, depth // 2 :] = low(rows[:, : depth // 2])


def agreeing(order_ref, point):
    even = order_ref[order_ref.shape[0] - 1]
    return point + even - 2 * even * point


def away_pair_kernel(order_ref, left_ref, mate_ref, next_ref, out_ref):
    points, _, columns = out_ref.shape
    half = columns // 2
    for point in range(points):
        for part, right_ref in enumerate((mate_ref, next_ref)):
            out_ref[point, :, part * half : (part + 1) * half] = low(
                dots(left_ref[point], right_ref[agreeing(order_ref, point)])
            )


def away_far_kernel(left_ref, right_ref, out_ref):
    points, _, columns = out_ref.shape
    half = columns // points
    for point in range(points):
        for part in range(points):
            out_ref[point, :, part * half : (part + 1) * half] = low(dots(left_ref[point], right_ref[part]))


def rest_pair_kernel(order_ref, left_ref, mate_ref, next_ref, out_ref):
    _, points, count, columns = out_ref.shape
    half = columns // 2
    for point in range(points):
        rows = left_ref[point].reshape(2 * count, -1)
        for part, right_ref in enumerate((mate_ref, next_ref)):
            out = low(dots(rows, right_ref[agreeing(order_ref, point)]))
            out_ref[0, point, :, part * half : (part + 1) * half] = out[:count]
            out_ref[1, point, :, part * half : (part + 1) * half] = out[count:]


def rest_far_kernel(left_ref, right_ref, out_ref):
    _, points, count, columns = out_ref.shape
    half = columns // points
    for point in range(points):
        rows = left_ref[point].reshape(2 * count, -1)
        for part in range(points):
            out = low(dots(rows, right_ref[part]))
            out_ref[0, point, :, part * half : (part + 1) * half] = out[:count]
            out_ref[1, point, :, part * half : (part + 1) * half] = out[count:]


def picked(order_ref, slots, rows, owners, transitions):
    n = lax.broadcasted_iota(jnp.int32, (rows, transitions), 0)
    column = lax.broadcasted_iota(jnp.int32, (rows, transitions), 1)
    target = (n // BLOCK * owners) * BLOCK + n % BLOCK
    return jnp.concatenate(
        [low(jnp.where(column == target + order_ref[slot] * BLOCK, 1.0, 0.0)) for slot in slots], axis=0
    )


def second_kernel(order_ref, rest_ref, got_ref, out_ref):
    points, count, _ = out_ref.shape
    half = rest_ref.shape[3] // 2
    owners = order_ref.shape[0] - 1
    pick = picked(order_ref, (2, 1), count // 2, owners, half)
    for point in range(points):
        out_ref[point, :, : 2 * half] = low(wide(rest_ref[0, point]) + wide(got_ref[point, count:, :]))
        own = low(wide(rest_ref[1, point]) + wide(got_ref[point, :count, :]))
        for part in range(2):
            place = (2 * half + part * count, 2 * half + (part + 1) * count)
            out_ref[point, :, place[0] : place[1]] = low(dots(own[:, part * half : (part + 1) * half], pick))


def turned_part(order_ref, block_ref, second_ref, late_ref, part, same_ref, first_ref, index):
    points, count, columns = block_ref.shape
    half = columns // 2
    rows = count // 2
    owners = order_ref.shape[0] - 1
    span = pl.ds(part * half, half)
    own = jnp.concatenate(
        [block_ref[point, p * rows : (p + 1) * rows, span] for p in range(2) for point in range(points)], axis=0
    )
    pick = picked(order_ref, (3, 0), rows, owners, half)
    others = []
    for point in range(points):
        other = dots(second_ref[point, :, span], pick) + wide(late_ref[point, :, pl.ds(columns + part * count, count)])
        others.append(low(other))
    other = jnp.concatenate(
        [others[point][p * rows : (p + 1) * rows] for p in range(2) for point in range(points)], axis=0
    )
    n = lax.broadcasted_iota(jnp.int32, (count, count), 0)
    same = low(jnp.where(n == lax.broadcasted_iota(jnp.int32, (count, count), 1), 1.0, 0.0))
    for source, out in enumerate((dots(pick, own), dots(same, other))):
        for to, ref in enumerate((same_ref, first_ref)):
            piece = out[to * rows : (to + 1) * rows]
            ref[source, *index, 0] = low(piece[:, : points * rows])
            ref[source, *index, 1] = low(-piece[:, points * rows :])


def finish(order_ref, rest_ref, got_ref, second_ref, late_ref, block_ref):
    points, count, columns = block_ref.shape
    for point in range(points):
        total = wide(rest_ref[1, point]) + wide(got_ref[point, :count, :]) + wide(late_ref[point, :, :columns])
        block_ref[point] = low(total)


def finish_pair_kernel(
    order_ref, rest_ref, got_ref, second_ref, late_ref,
    block_ref, mate_same_ref, mate_first_ref, next_same_ref, next_first_ref,
):
    finish(order_ref, rest_ref, got_ref, second_ref, late_ref, block_ref)
    turned_part(order_ref, block_ref, second_ref, late_ref, 0, mate_same_ref, mate_first_ref, ())
    turned_part(order_ref, block_ref, second_ref, late_ref, 1, next_same_ref, next_first_ref, ())


def finish_far_kernel(order_ref, rest_ref, got_ref, second_ref, late_ref, block_ref, same_ref, first_ref):
    finish(order_ref, rest_ref, got_ref, second_ref, late_ref, block_ref)
    for part in range(block_ref.shape[0]):
        turned_part(order_ref, block_ref, second_ref, late_ref, part, same_ref, first_ref, (part,))


def merge_kernel(
    order_ref, pair_ref, far_ref, mate_same_ref, mate_first_ref, next_same_ref, next_first_ref,
    far_same_ref, far_first_ref, out_ref,
):
    points, count, columns = pair_ref.shape
    rows = count // 2
    half = columns // 2
    owners = order_ref.shape[0] - 1
    even = order_ref[owners]
    lanes = points * rows
    n = lax.broadcasted_iota(jnp.int32, (lanes, columns), 0)
    column = lax.broadcasted_iota(jnp.int32, (lanes, columns), 1)
    target = (n // BLOCK * owners) * BLOCK + n % BLOCK
    sources = [
        (mate_same_ref, 1, next_same_ref, 1, far_first_ref, 0),
        (mate_first_ref, 1, next_first_ref, 1, far_first_ref, 1),
        (mate_first_ref, 0, next_first_ref, 0, far_same_ref, 1),
        (mate_same_ref, 0, next_same_ref, 0, far_same_ref, 0),
    ]
    total = 0.0
    for slot, (mate_piece, i, next_piece, j, far_piece, k) in enumerate(sources):
        pick = low(jnp.where(column == target + order_ref[slot] * BLOCK, 1.0, 0.0))
        tiles = [mate_piece[i, p] for p in range(2)] + [next_piece[j, p] for p in range(2)]
        tiles += [far_piece[k, part, p] for part in range(points) for p in range(2)]
        total = total + lax.dot_general(
            jnp.concatenate(tiles, axis=0), pick, (((1,), (0,)), ((), ())), preferred_element_type=jnp.float32
        )
    back = low(total)
    for p in range(2):
        for part, place in ((0, 2 * even), (1, 2 - 2 * even)):
            natural = back[(2 * part + p) * rows : (2 * part + p + 1) * rows]
            for row_point in range(points):
                here = pair_ref[row_point, p * rows : (p + 1) * rows, part * half : (part + 1) * half]
                for column_point in range(points):
                    there = natural[:, column_point * half : (column_point + 1) * half]
                    mine = even == (0 if row_point == column_point else 1)
                    out_ref[
                        place, p, row_point * rows : (row_point + 1) * rows, column_point * half : (column_point + 1) * half
                    ] = jnp.where(mine, here, there)
        for point in range(points):
            span = slice(point * rows, (point + 1) * rows)
            out_ref[1 + 2 * even, p, span, :] = far_ref[point, p * rows : (p + 1) * rows, :]
            first = (4 + 2 * point + p) * rows
            out_ref[3 - 2 * even, p, span, :] = back[first : first + rows]


def body(pair_density, coulomb):
    points, transitions, _, g_local = pair_density.shape
    owners = lax.axis_size("own")
    groups = lax.axis_size("kp")
    blocks = transitions // (owners * BLOCK)
    rows = blocks * BLOCK
    depth = 2 * g_local
    scale = 1.0 / math.sqrt(g_local * owners)
    me = lax.axis_index("own")
    odd = lax.axis_index("kp") % 2 == 1
    parity = odd.astype(jnp.int32)

    def exchange_kp(value, partner):
        return lax.ppermute(value, "kp", [(i, partner(i) % groups) for i in range(groups)])

    def flips(i):
        return [1, 2, 3, 0] if i % 2 == 0 else [3, 2, 1, 0]

    def exchange(value, slot, partner):
        pairs = [
            (i * owners + o, partner(i) % groups * owners + (o ^ flips(i)[slot]))
            for i in range(groups)
            for o in range(owners)
        ]
        return lax.ppermute(value, ("kp", "own"), pairs)

    def exchange_own(value, first):
        return exchange(value, 0 if first else 2, lambda i: i)

    def mate(i):
        return i + 1 if i % 2 == 0 else i - 1

    def across(i):
        return i - 1 if i % 2 == 0 else i + 1

    def second_next(i):
        return i + 2 if i % 2 == 0 else i - 2

    near_flip, far_flip = 1 + 2 * parity, 3 - 2 * parity
    relative = jnp.stack([me ^ near_flip, me ^ 2, me ^ far_flip, me, 1 - parity])

    plain = pair_density.reshape(points, transitions, depth)
    mate_right = exchange_kp(plain, mate)
    next_right = exchange_kp(plain, across)

    weights = (jnp.concatenate([coulomb, coulomb]) * scale).reshape(1, depth)
    left = local(left_kernel, [(points, owners, 2, rows, depth)], relative, plain, weights, scalars=1, moved=4 << 20)
    left_away = left[:, :2].reshape(points, 4 * rows, depth)
    left_rest = left[:, 2:].reshape(points, 4 * rows, depth)

    left_away, left_rest, mate_right = lax.optimization_barrier((left_away, left_rest, mate_right))
    columns = points * transitions
    away_shape = [(points, 4 * rows, columns)]
    second_shape = [(points, 2 * rows, columns + 4 * rows)]
    block_shape = (points, 2 * rows, columns)
    pair_back = (2, 2, rows, points * rows)
    far_back = (2, points, 2, rows, points * rows)

    rest_shape = [(2, points, 2 * rows, columns)]

    far_right = exchange_kp(next_right, mate)
    away_pair = local(away_pair_kernel, away_shape, relative, left_away, mate_right, next_right, scalars=1)
    got_pair = exchange_own(away_pair, True)
    far_right, _ = lax.optimization_barrier((far_right, away_pair))
    away_far = local(away_far_kernel, away_shape, left_away, far_right)
    got_far = exchange_own(away_far, True)
    late_left, mate_right, next_right, far_right, _ = lax.optimization_barrier(
        (left_rest, mate_right, next_right, far_right, away_far)
    )
    rest_pair = local(
        rest_pair_kernel, rest_shape, relative, late_left, mate_right, next_right, scalars=1, moved=8 << 20
    )
    rest_far = local(rest_far_kernel, rest_shape, late_left, far_right, moved=8 << 20)
    got_pair, rest_pair, rest_far = lax.optimization_barrier((got_pair, rest_pair, rest_far))
    second_pair = local(second_kernel, second_shape, relative, rest_pair, got_pair, scalars=1)
    late_pair = exchange_own(second_pair, False)
    second_far = local(second_kernel, second_shape, relative, rest_far, got_far, scalars=1)
    late_pair, _ = lax.optimization_barrier((late_pair, second_far))
    late_far = exchange_own(second_far, False)
    block_pair, mate_same, mate_first, next_same, next_first = local(
        finish_pair_kernel, [block_shape] + [pair_back] * 4, relative, rest_pair, got_pair, second_pair, late_pair, scalars=1
    )
    block_far, far_same, far_first = local(
        finish_far_kernel, [block_shape, far_back, far_back], relative, rest_far, got_far, second_far, late_far, scalars=1
    )
    out = local(
        merge_kernel, [(4, 2, points * rows, columns)],
        relative, block_pair, block_far,
        exchange(mate_same, 3, mate), exchange(mate_first, 0, mate),
        exchange(next_same, 3, across), exchange(next_first, 0, across),
        exchange(far_same, 3, second_next), exchange(far_first, 0, second_next),
        scalars=1,
    )
    return out.transpose(0, 2, 1, 3)


def solution(mesh):
    placed = (P("kp", None, None, "own"), P("own"))
    return jax.shard_map(
        body,
        mesh=mesh,
        in_specs=placed,
        out_specs=P(None, ("kp", "own"), None, None),
        check_vma=False,
    )
```

```python
import math

import jax
import jax.numpy as jnp
from jax import lax
from jax.experimental import pallas as pl
from jax.experimental.pallas import tpu as pltpu
from jax.sharding import PartitionSpec as P

BLOCK = 32


def local(kernel, shapes, *operands, scalars=0, moved=0):
    vmem = pl.BlockSpec(memory_space=pltpu.VMEM)
    smem = pl.BlockSpec(memory_space=pltpu.SMEM)
    several = len(shapes) > 1
    out_shape = [jax.ShapeDtypeStruct(s, jnp.bfloat16) for s in shapes]
    return pl.pallas_call(
        kernel,
        out_shape=out_shape if several else out_shape[0],
        in_specs=[smem] * scalars + [vmem] * (len(operands) - scalars),
        out_specs=[vmem] * len(shapes) if several else vmem,
        compiler_params=pltpu.CompilerParams(vmem_limit_bytes=40 * 1024 * 1024),
        cost_estimate=pl.CostEstimate(flops=0, transcendentals=0, bytes_accessed=moved),
    )(*operands)


def dots(left, right):
    return lax.dot_general(left, right, (((1,), (1,)), ((), ())), preferred_element_type=jnp.float32)


def low(value):
    return value.astype(jnp.bfloat16)


def wide(value):
    return value.astype(jnp.float32)


def left_kernel(order_ref, plain_ref, weight_ref, away_ref, rest_ref):
    points, transitions, depth = plain_ref.shape
    owners = order_ref.shape[0] - 1
    blocks = transitions // (owners * BLOCK)
    weight = weight_ref[...]
    for point in range(points):
        for slot in range(owners):
            out_ref = (away_ref, rest_ref)[slot // 2]
            for block in range(blocks):
                start = pl.multiple_of((block * owners + order_ref[slot]) * BLOCK, BLOCK)
                rows = wide(plain_ref[point, pl.ds(start, BLOCK), :]) * weight
                real = pl.ds((slot % 2 * 2 * blocks + block) * BLOCK, BLOCK)
                imag = pl.ds(((slot % 2 * 2 + 1) * blocks + block) * BLOCK, BLOCK)
                out_ref[point, real, :] = low(rows)
                out_ref[point, imag, : depth // 2] = low(-rows[:, depth // 2 :])
                out_ref[point, imag, depth // 2 :] = low(rows[:, : depth // 2])


def agreeing(order_ref, point):
    even = order_ref[order_ref.shape[0] - 1]
    return point + even - 2 * even * point


def away_pair_kernel(order_ref, left_ref, mate_ref, next_ref, out_ref):
    points, _, columns = out_ref.shape
    half = columns // 2
    for point in range(points):
        for part, right_ref in enumerate((mate_ref, next_ref)):
            out_ref[point, :, part * half : (part + 1) * half] = low(
                dots(left_ref[point], right_ref[agreeing(order_ref, point)])
            )


def away_far_kernel(left_ref, right_ref, out_ref):
    points, _, columns = out_ref.shape
    half = columns // points
    for point in range(points):
        for part in range(points):
            out_ref[point, :, part * half : (part + 1) * half] = low(dots(left_ref[point], right_ref[part]))


def rest_pair_kernel(order_ref, left_ref, mate_ref, next_ref, out_ref):
    _, points, count, columns = out_ref.shape
    half = columns // 2
    for point in range(points):
        rows = left_ref[point].reshape(2 * count, -1)
        for part, right_ref in enumerate((mate_ref, next_ref)):
            out = low(dots(rows, right_ref[agreeing(order_ref, point)]))
            out_ref[0, point, :, part * half : (part + 1) * half] = out[:count]
            out_ref[1, point, :, part * half : (part + 1) * half] = out[count:]


def rest_far_kernel(left_ref, right_ref, out_ref):
    _, points, count, columns = out_ref.shape
    half = columns // points
    for point in range(points):
        rows = left_ref[point].reshape(2 * count, -1)
        for part in range(points):
            out = low(dots(rows, right_ref[part]))
            out_ref[0, point, :, part * half : (part + 1) * half] = out[:count]
            out_ref[1, point, :, part * half : (part + 1) * half] = out[count:]


def picked(order_ref, slots, rows, owners, transitions):
    n = lax.broadcasted_iota(jnp.int32, (rows, transitions), 0)
    column = lax.broadcasted_iota(jnp.int32, (rows, transitions), 1)
    target = (n // BLOCK * owners) * BLOCK + n % BLOCK
    return jnp.concatenate(
        [low(jnp.where(column == target + order_ref[slot] * BLOCK, 1.0, 0.0)) for slot in slots], axis=0
    )


def second_kernel(order_ref, rest_ref, got_ref, out_ref):
    points, count, _ = out_ref.shape
    half = rest_ref.shape[3] // 2
    owners = order_ref.shape[0] - 1
    pick = picked(order_ref, (2, 1), count // 2, owners, half)
    for point in range(points):
        out_ref[point, :, : 2 * half] = low(wide(rest_ref[0, point]) + wide(got_ref[point, count:, :]))
        own = low(wide(rest_ref[1, point]) + wide(got_ref[point, :count, :]))
        for part in range(2):
            place = (2 * half + part * count, 2 * half + (part + 1) * count)
            out_ref[point, :, place[0] : place[1]] = low(dots(own[:, part * half : (part + 1) * half], pick))


def turned_part(order_ref, block_ref, second_ref, late_ref, part, same_ref, first_ref, place):
    points, count, columns = block_ref.shape
    half = columns // 2
    rows = count // 2
    owners = order_ref.shape[0] - 1
    span = pl.ds(part * half, half)
    own = jnp.concatenate(
        [block_ref[point, p * rows : (p + 1) * rows, span] for p in range(2) for point in range(points)], axis=0
    )
    pick = picked(order_ref, (3, 0), rows, owners, half)
    others = []
    for point in range(points):
        other = dots(second_ref[point, :, span], pick) + wide(late_ref[point, :, pl.ds(columns + part * count, count)])
        others.append(low(other))
    other = jnp.concatenate(
        [others[point][p * rows : (p + 1) * rows] for p in range(2) for point in range(points)], axis=0
    )
    n = lax.broadcasted_iota(jnp.int32, (count, count), 0)
    same = low(jnp.where(n == lax.broadcasted_iota(jnp.int32, (count, count), 1), 1.0, 0.0))
    for source, out in enumerate((dots(pick, own), dots(same, other))):
        for to, ref in enumerate((same_ref, first_ref)):
            piece = out[to * rows : (to + 1) * rows]
            both = jnp.concatenate([low(piece[:, : points * rows]), low(-piece[:, points * rows :])], axis=0)
            if place is None:
                ref[source] = both
            else:
                ref[source, place] = both


def finish(rest_ref, got_ref, late_ref, block_ref):
    points, count, columns = block_ref.shape
    for point in range(points):
        total = wide(rest_ref[1, point]) + wide(got_ref[point, :count, :]) + wide(late_ref[point, :, :columns])
        block_ref[point] = low(total)


def finish_kernel(
    order_ref, rest_pair_ref, got_pair_ref, second_pair_ref, late_pair_ref,
    rest_far_ref, got_far_ref, second_far_ref, late_far_ref,
    block_ref, mate_same_ref, mate_first_ref, next_same_ref, next_first_ref, far_ref,
):
    points, count, columns = block_ref.shape
    finish(rest_pair_ref, got_pair_ref, late_pair_ref, block_ref)
    finish(rest_far_ref, got_far_ref, late_far_ref, far_ref)
    strips = columns // count
    for point in range(points):
        for strip in range(strips):
            mate_same_ref[2 + point * strips + strip] = far_ref[point, :, strip * count : (strip + 1) * count]
    turned_part(order_ref, block_ref, second_pair_ref, late_pair_ref, 0, mate_same_ref, mate_first_ref, None)
    turned_part(order_ref, block_ref, second_pair_ref, late_pair_ref, 1, next_same_ref, next_first_ref, 0)
    for part in range(points):
        turned_part(order_ref, far_ref, second_far_ref, late_far_ref, part, next_same_ref, next_first_ref, 1 + part)


def merge_kernel(
    order_ref, pair_ref, mate_same_ref, mate_first_ref, next_same_ref, next_first_ref, out_ref
):
    points, count, columns = pair_ref.shape
    rows = count // 2
    half = columns // 2
    owners = order_ref.shape[0] - 1
    even = order_ref[owners]
    lanes = points * rows
    strips = columns // count
    n = lax.broadcasted_iota(jnp.int32, (lanes, columns), 0)
    column = lax.broadcasted_iota(jnp.int32, (lanes, columns), 1)
    target = (n // BLOCK * owners) * BLOCK + n % BLOCK
    sources = [
        (mate_same_ref, next_same_ref, 1),
        (mate_first_ref, next_first_ref, 1),
        (mate_first_ref, next_first_ref, 0),
        (mate_same_ref, next_same_ref, 0),
    ]
    total = 0.0
    for slot, (mate_piece, next_piece, source) in enumerate(sources):
        pick = low(jnp.where(column == target + order_ref[slot] * BLOCK, 1.0, 0.0))
        tiles = [mate_piece[source]] + [next_piece[source, place] for place in range(1 + points)]
        total = total + lax.dot_general(
            jnp.concatenate(tiles, axis=0), pick, (((1,), (0,)), ((), ())), preferred_element_type=jnp.float32
        )
    back = low(total)
    for p in range(2):
        for part, place in ((0, 2 * even), (1, 2 - 2 * even)):
            natural = back[(2 * part + p) * rows : (2 * part + p + 1) * rows]
            for row_point in range(points):
                here = pair_ref[row_point, p * rows : (p + 1) * rows, part * half : (part + 1) * half]
                for column_point in range(points):
                    there = natural[:, column_point * half : (column_point + 1) * half]
                    mine = even == (0 if row_point == column_point else 1)
                    out_ref[
                        place, p, row_point * rows : (row_point + 1) * rows, column_point * half : (column_point + 1) * half
                    ] = jnp.where(mine, here, there)
        for point in range(points):
            span = slice(point * rows, (point + 1) * rows)
            for strip in range(strips):
                tile = mate_same_ref[2 + point * strips + strip, p * rows : (p + 1) * rows, :]
                out_ref[1 + 2 * even, p, span, strip * count : (strip + 1) * count] = tile
            first = (4 + 2 * point + p) * rows
            out_ref[3 - 2 * even, p, span, :] = back[first : first + rows]


def body(pair_density, coulomb):
    points, transitions, _, g_local = pair_density.shape
    owners = lax.axis_size("own")
    groups = lax.axis_size("kp")
    blocks = transitions // (owners * BLOCK)
    rows = blocks * BLOCK
    depth = 2 * g_local
    scale = 1.0 / math.sqrt(g_local * owners)
    me = lax.axis_index("own")
    odd = lax.axis_index("kp") % 2 == 1
    parity = odd.astype(jnp.int32)

    def exchange_kp(value, partner):
        return lax.ppermute(value, "kp", [(i, partner(i) % groups) for i in range(groups)])

    def flips(i):
        return [1, 2, 3, 0] if i % 2 == 0 else [3, 2, 1, 0]

    def exchange(value, slot, partner):
        pairs = [
            (i * owners + o, partner(i) % groups * owners + (o ^ flips(i)[slot]))
            for i in range(groups)
            for o in range(owners)
        ]
        return lax.ppermute(value, ("kp", "own"), pairs)

    def exchange_own(value, first):
        return exchange(value, 0 if first else 2, lambda i: i)

    def mate(i):
        return i + 1 if i % 2 == 0 else i - 1

    def across(i):
        return i - 1 if i % 2 == 0 else i + 1

    near_flip, far_flip = 1 + 2 * parity, 3 - 2 * parity
    relative = jnp.stack([me ^ near_flip, me ^ 2, me ^ far_flip, me, 1 - parity])

    plain = pair_density.reshape(points, transitions, depth)
    mate_right = exchange_kp(plain, mate)
    next_right = exchange_kp(plain, across)

    weights = (jnp.concatenate([coulomb, coulomb]) * scale).reshape(1, depth)
    left_shape = [(points, 4 * rows, depth)] * 2
    left_away, left_rest = local(left_kernel, left_shape, relative, plain, weights, scalars=1, moved=4 << 20)
    mate_away, mate_rest = local(left_kernel, left_shape, relative, mate_right, weights, scalars=1, moved=4 << 20)
    next_right, left_away, mate_away = lax.optimization_barrier((next_right, left_away, mate_away))

    columns = points * transitions
    away_shape = [(points, 4 * rows, columns)]
    rest_shape = [(2, points, 2 * rows, columns)]
    second_shape = [(points, 2 * rows, columns + 4 * rows)]

    away_pair = local(away_pair_kernel, away_shape, relative, left_away, mate_right, next_right, scalars=1)
    got_pair = exchange_own(away_pair, True)
    mate_away, _ = lax.optimization_barrier((mate_away, away_pair))
    away_far = local(away_far_kernel, away_shape, mate_away, next_right)
    got_far = exchange_own(away_far, True)
    left_rest, mate_rest, _ = lax.optimization_barrier((left_rest, mate_rest, away_far))
    rest_pair = local(
        rest_pair_kernel, rest_shape, relative, left_rest, mate_right, next_right, scalars=1, moved=8 << 20
    )
    rest_far = local(rest_far_kernel, rest_shape, mate_rest, next_right, moved=8 << 20)
    got_pair, rest_pair, rest_far = lax.optimization_barrier((got_pair, rest_pair, rest_far))
    second_pair = local(second_kernel, second_shape, relative, rest_pair, got_pair, scalars=1)
    late_pair = exchange_own(second_pair, False)
    got_far, _ = lax.optimization_barrier((got_far, second_pair))
    second_far = local(second_kernel, second_shape, relative, rest_far, got_far, scalars=1)
    late_far = exchange_own(second_far, False)
    tile = (2 * rows, points * rows)
    strips = points * columns // tile[1]
    block_pair, mate_same, mate_first, next_same, next_first, _ = local(
        finish_kernel,
        [
            (points, 2 * rows, columns),
            (2 + strips, *tile),
            (2, *tile),
            (2, 1 + points, *tile),
            (2, 1 + points, *tile),
            (points, 2 * rows, columns),
        ],
        relative, rest_pair, got_pair, second_pair, late_pair, rest_far, got_far, second_far, late_far, scalars=1,
    )
    out = local(
        merge_kernel, [(4, 2, points * rows, columns)],
        relative, block_pair,
        exchange(mate_same, 3, mate), exchange(mate_first, 0, mate),
        exchange(next_same, 3, across), exchange(next_first, 0, across),
        scalars=1,
    )
    return out.transpose(0, 2, 1, 3)


def solution(mesh):
    placed = (P("kp", None, None, "own"), P("own"))
    return jax.shard_map(
        body,
        mesh=mesh,
        in_specs=placed,
        out_specs=P(None, ("kp", "own"), None, None),
        check_vma=False,
    )
```

```python
import math

import jax
import jax.numpy as jnp
from jax import lax
from jax.experimental import pallas as pl
from jax.experimental.pallas import tpu as pltpu
from jax.sharding import PartitionSpec as P

BLOCK = 32


def local(kernel, shapes, *operands, scalars=0, moved=0):
    vmem = pl.BlockSpec(memory_space=pltpu.VMEM)
    smem = pl.BlockSpec(memory_space=pltpu.SMEM)
    several = len(shapes) > 1
    out_shape = [jax.ShapeDtypeStruct(s, jnp.bfloat16) for s in shapes]
    return pl.pallas_call(
        kernel,
        out_shape=out_shape if several else out_shape[0],
        in_specs=[smem] * scalars + [vmem] * (len(operands) - scalars),
        out_specs=[vmem] * len(shapes) if several else vmem,
        compiler_params=pltpu.CompilerParams(vmem_limit_bytes=40 * 1024 * 1024),
        cost_estimate=pl.CostEstimate(flops=0, transcendentals=0, bytes_accessed=moved),
    )(*operands)


def dots(left, right):
    return lax.dot_general(left, right, (((1,), (1,)), ((), ())), preferred_element_type=jnp.float32)


def low(value):
    return value.astype(jnp.bfloat16)


def wide(value):
    return value.astype(jnp.float32)


def left_kernel(order_ref, plain_ref, weight_ref, away_ref, rest_ref):
    points, transitions, depth = plain_ref.shape
    owners = order_ref.shape[0] - 1
    blocks = transitions // (owners * BLOCK)
    weight = weight_ref[...]
    for point in range(points):
        for slot in range(owners):
            out_ref = (away_ref, rest_ref)[slot // 2]
            for block in range(blocks):
                start = pl.multiple_of((block * owners + order_ref[slot]) * BLOCK, BLOCK)
                rows = wide(plain_ref[point, pl.ds(start, BLOCK), :]) * weight
                real = pl.ds((slot % 2 * 2 * blocks + block) * BLOCK, BLOCK)
                imag = pl.ds(((slot % 2 * 2 + 1) * blocks + block) * BLOCK, BLOCK)
                out_ref[point, real, :] = low(rows)
                out_ref[point, imag, : depth // 2] = low(-rows[:, depth // 2 :])
                out_ref[point, imag, depth // 2 :] = low(rows[:, : depth // 2])


def agreeing(order_ref, point):
    even = order_ref[order_ref.shape[0] - 1]
    return point + even - 2 * even * point


def away_pair_kernel(order_ref, left_ref, mate_ref, next_ref, out_ref):
    points, _, columns = out_ref.shape
    half = columns // 2
    for point in range(points):
        for part, right_ref in enumerate((mate_ref, next_ref)):
            out_ref[point, :, part * half : (part + 1) * half] = low(
                dots(left_ref[point], right_ref[agreeing(order_ref, point)])
            )


def away_far_kernel(left_ref, right_ref, out_ref):
    points, _, columns = out_ref.shape
    half = columns // points
    for point in range(points):
        for part in range(points):
            out_ref[point, :, part * half : (part + 1) * half] = low(dots(left_ref[point], right_ref[part]))


def rest_pair_kernel(order_ref, left_ref, mate_ref, next_ref, out_ref):
    _, points, count, columns = out_ref.shape
    half = columns // 2
    for point in range(points):
        rows = left_ref[point].reshape(2 * count, -1)
        for part, right_ref in enumerate((mate_ref, next_ref)):
            out = low(dots(rows, right_ref[agreeing(order_ref, point)]))
            out_ref[0, point, :, part * half : (part + 1) * half] = out[:count]
            out_ref[1, point, :, part * half : (part + 1) * half] = out[count:]


def rest_far_kernel(left_ref, right_ref, out_ref):
    _, points, count, columns = out_ref.shape
    half = columns // points
    for point in range(points):
        rows = left_ref[point].reshape(2 * count, -1)
        for part in range(points):
            out = low(dots(rows, right_ref[part]))
            out_ref[0, point, :, part * half : (part + 1) * half] = out[:count]
            out_ref[1, point, :, part * half : (part + 1) * half] = out[count:]


def picked(order_ref, slots, rows, owners, transitions):
    n = lax.broadcasted_iota(jnp.int32, (rows, transitions), 0)
    column = lax.broadcasted_iota(jnp.int32, (rows, transitions), 1)
    target = (n // BLOCK * owners) * BLOCK + n % BLOCK
    return jnp.concatenate(
        [low(jnp.where(column == target + order_ref[slot] * BLOCK, 1.0, 0.0)) for slot in slots], axis=0
    )


def second_kernel(order_ref, rest_ref, got_ref, out_ref):
    points, count, _ = out_ref.shape
    half = rest_ref.shape[3] // 2
    owners = order_ref.shape[0] - 1
    pick = picked(order_ref, (2, 1), count // 2, owners, half)
    for point in range(points):
        out_ref[point, :, : 2 * half] = low(wide(rest_ref[0, point]) + wide(got_ref[point, count:, :]))
        own = low(wide(rest_ref[1, point]) + wide(got_ref[point, :count, :]))
        for part in range(2):
            place = (2 * half + part * count, 2 * half + (part + 1) * count)
            out_ref[point, :, place[0] : place[1]] = low(dots(own[:, part * half : (part + 1) * half], pick))


def turned_part(order_ref, block_ref, second_ref, late_ref, part):
    points, count, columns = block_ref.shape
    half = columns // 2
    rows = count // 2
    owners = order_ref.shape[0] - 1
    span = pl.ds(part * half, half)
    own = jnp.concatenate(
        [block_ref[point, p * rows : (p + 1) * rows, span] for p in range(2) for point in range(points)], axis=0
    )
    pick = picked(order_ref, (3, 0), rows, owners, half)
    others = []
    for point in range(points):
        other = dots(second_ref[point, :, span], pick) + wide(late_ref[point, :, pl.ds(columns + part * count, count)])
        others.append(low(other))
    other = jnp.concatenate(
        [others[point][p * rows : (p + 1) * rows] for p in range(2) for point in range(points)], axis=0
    )
    n = lax.broadcasted_iota(jnp.int32, (count, count), 0)
    same = low(jnp.where(n == lax.broadcasted_iota(jnp.int32, (count, count), 1), 1.0, 0.0))
    pieces = []
    for out in (dots(pick, own), dots(same, other)):
        for to in range(2):
            piece = out[to * rows : (to + 1) * rows]
            pieces.append(jnp.concatenate([low(piece[:, : points * rows]), low(-piece[:, points * rows :])], axis=0))
    return (pieces[0], pieces[2]), (pieces[1], pieces[3])


def finish(rest_ref, got_ref, late_ref, block_ref):
    points, count, columns = block_ref.shape
    for point in range(points):
        total = wide(rest_ref[1, point]) + wide(got_ref[point, :count, :]) + wide(late_ref[point, :, :columns])
        block_ref[point] = low(total)


def finish_pair_kernel(
    order_ref, rest_ref, got_ref, second_ref, late_ref, block_ref, same_ref, first_ref
):
    finish(rest_ref, got_ref, late_ref, block_ref)
    for part in range(2):
        same, first = turned_part(order_ref, block_ref, second_ref, late_ref, part)
        for source in range(2):
            same_ref[part, source] = same[source]
            first_ref[part, source] = first[source]


def finish_far_kernel(order_ref, rest_ref, got_ref, second_ref, late_ref, block_ref, same_ref, first_ref):
    finish(rest_ref, got_ref, late_ref, block_ref)
    for part in range(block_ref.shape[0]):
        same, first = turned_part(order_ref, block_ref, second_ref, late_ref, part)
        for source in range(2):
            same_ref[part, source] = same[source]
            first_ref[part, source] = first[source]


def pack_kernel(pair_same_ref, passed_ref, far_same_ref, far_ref, to_mate_ref, to_next_ref):
    points, count, columns = far_ref.shape
    strips = columns // count
    for part, ref in enumerate((to_mate_ref, to_next_ref)):
        ref[0:2] = pair_same_ref[part]
        ref[2:4] = passed_ref[part]
    for point in range(points):
        to_next_ref[4 + 2 * point : 6 + 2 * point] = far_same_ref[point]
        for strip in range(strips):
            to_mate_ref[4 + point * strips + strip] = far_ref[point, :, strip * count : (strip + 1) * count]


def spread(order_ref, slot, lanes, columns):
    n = lax.broadcasted_iota(jnp.int32, (lanes, columns), 0)
    column = lax.broadcasted_iota(jnp.int32, (lanes, columns), 1)
    target = (n // BLOCK * (order_ref.shape[0] - 1) + order_ref[slot]) * BLOCK + n % BLOCK
    return low(jnp.where(column == target, 1.0, 0.0))


def merge_kernel(order_ref, pair_ref, far_first_ref, from_next_ref, from_mate_ref, out_ref):
    points, count, columns = pair_ref.shape
    rows = count // 2
    half = columns // 2
    even = order_ref[order_ref.shape[0] - 1]
    lanes = points * rows
    strips = columns // count
    back = 0.0
    for slot, source in enumerate((1, 3, 2, 0)):
        tiles = [from_mate_ref[source], from_next_ref[source]]
        if source < 2:
            tiles += [from_next_ref[4 + 2 * part + source] for part in range(points)]
        else:
            tiles += [far_first_ref[part, source - 2] for part in range(points)]
        back = back + lax.dot_general(
            jnp.concatenate(tiles, axis=0),
            spread(order_ref, slot, lanes, columns),
            (((1,), (0,)), ((), ())),
            preferred_element_type=jnp.float32,
        )
    back = low(back)
    for p in range(2):
        for part, place in ((0, 2 * even), (1, 2 - 2 * even)):
            natural = back[(2 * part + p) * rows : (2 * part + p + 1) * rows]
            for row_point in range(points):
                here = pair_ref[row_point, p * rows : (p + 1) * rows, part * half : (part + 1) * half]
                for column_point in range(points):
                    there = natural[:, column_point * half : (column_point + 1) * half]
                    mine = even == (0 if row_point == column_point else 1)
                    out_ref[
                        place, p, row_point * rows : (row_point + 1) * rows, column_point * half : (column_point + 1) * half
                    ] = jnp.where(mine, here, there)
        for point in range(points):
            span = slice(point * rows, (point + 1) * rows)
            for strip in range(strips):
                tile = from_mate_ref[4 + point * strips + strip, p * rows : (p + 1) * rows, :]
                out_ref[1 + 2 * even, p, span, strip * count : (strip + 1) * count] = tile
            first = (2 + point) * count + p * rows
            out_ref[3 - 2 * even, p, span, :] = back[first : first + rows]


def body(pair_density, coulomb):
    points, transitions, _, g_local = pair_density.shape
    owners = lax.axis_size("own")
    groups = lax.axis_size("kp")
    blocks = transitions // (owners * BLOCK)
    rows = blocks * BLOCK
    depth = 2 * g_local
    scale = 1.0 / math.sqrt(g_local * owners)
    me = lax.axis_index("own")
    odd = lax.axis_index("kp") % 2 == 1
    parity = odd.astype(jnp.int32)

    def exchange_kp(value, partner):
        return lax.ppermute(value, "kp", [(i, partner(i) % groups) for i in range(groups)])

    def flips(i):
        return [1, 2, 3, 0] if i % 2 == 0 else [3, 2, 1, 0]

    def exchange(value, slot, partner):
        pairs = [
            (i * owners + o, partner(i) % groups * owners + (o ^ flips(i)[slot]))
            for i in range(groups)
            for o in range(owners)
        ]
        return lax.ppermute(value, ("kp", "own"), pairs)

    def exchange_own(value, first):
        return exchange(value, 0 if first else 2, lambda i: i)

    def mate(i):
        return i + 1 if i % 2 == 0 else i - 1

    def across(i):
        return i - 1 if i % 2 == 0 else i + 1

    near_flip, far_flip = 1 + 2 * parity, 3 - 2 * parity
    relative = jnp.stack([me ^ near_flip, me ^ 2, me ^ far_flip, me, 1 - parity])

    plain = pair_density.reshape(points, transitions, depth)
    next_right = exchange_kp(plain, across)
    mate_right = exchange_kp(plain, mate)

    weights = (jnp.concatenate([coulomb, coulomb]) * scale).reshape(1, depth)
    left_shape = [(points, 4 * rows, depth)] * 2
    left_away, left_rest = local(left_kernel, left_shape, relative, plain, weights, scalars=1, moved=4 << 20)
    next_right, left_away = lax.optimization_barrier((next_right, left_away))

    columns = points * transitions
    away_shape = [(points, 4 * rows, columns)]
    rest_shape = [(2, points, 2 * rows, columns)]
    second_shape = [(points, 2 * rows, columns + 4 * rows)]

    away_pair = local(away_pair_kernel, away_shape, relative, left_away, mate_right, next_right, scalars=1)
    got_pair = exchange_own(away_pair, True)
    mate_left, _ = lax.optimization_barrier((mate_right, away_pair))
    mate_away, mate_rest = local(left_kernel, left_shape, relative, mate_left, weights, scalars=1)
    away_far = local(away_far_kernel, away_shape, mate_away, next_right)
    got_far = exchange_own(away_far, True)
    left_rest, mate_rest, _ = lax.optimization_barrier((left_rest, mate_rest, away_far))
    rest_pair = local(
        rest_pair_kernel, rest_shape, relative, left_rest, mate_right, next_right, scalars=1, moved=8 << 20
    )
    rest_far = local(rest_far_kernel, rest_shape, mate_rest, next_right, moved=8 << 20)
    got_pair, rest_pair, rest_far = lax.optimization_barrier((got_pair, rest_pair, rest_far))
    second_pair = local(second_kernel, second_shape, relative, rest_pair, got_pair, scalars=1)
    late_pair = exchange_own(second_pair, False)
    got_far, _ = lax.optimization_barrier((got_far, second_pair))
    second_far = local(second_kernel, second_shape, relative, rest_far, got_far, scalars=1)
    late_far = exchange_own(second_far, False)
    tile = (2 * rows, points * rows)
    strips = points * columns // tile[1]
    block_shape = (points, 2 * rows, columns)
    late_pair, _ = lax.optimization_barrier((late_pair, second_far))
    block_pair, same_pair, first_pair = local(
        finish_pair_kernel, [block_shape, (2, 2, *tile), (2, 2, *tile)],
        relative, rest_pair, got_pair, second_pair, late_pair, scalars=1,
    )
    passed_pair = exchange_own(first_pair, True)
    late_far, _ = lax.optimization_barrier((late_far, first_pair))
    block_far, far_same, far_first = local(
        finish_far_kernel, [block_shape, (points, 2, *tile), (points, 2, *tile)],
        relative, rest_far, got_far, second_far, late_far, scalars=1,
    )
    to_mate, to_next = local(
        pack_kernel, [(4 + strips, *tile), (4 + 2 * points, *tile)],
        same_pair, passed_pair, far_same, block_far, moved=16 << 20,
    )
    far_first = exchange(far_first, 0, across)
    from_next = exchange_kp(to_next, across)
    from_mate = exchange_kp(to_mate, mate)
    out = local(
        merge_kernel, [(4, 2, points * rows, columns)], relative, block_pair, far_first, from_next, from_mate, scalars=1
    )
    return out.transpose(0, 2, 1, 3)


def solution(mesh):
    placed = (P("kp", None, None, "own"), P("own"))
    return jax.shard_map(
        body,
        mesh=mesh,
        in_specs=placed,
        out_specs=P(None, ("kp", "own"), None, None),
        check_vma=False,
    )
```

```python
import math

import jax
import jax.numpy as jnp
from jax import lax
from jax.experimental import pallas as pl
from jax.experimental.pallas import tpu as pltpu
from jax.sharding import PartitionSpec as P

BLOCK = 32


def local(kernel, shapes, *operands, scalars=0, moved=0):
    vmem = pl.BlockSpec(memory_space=pltpu.VMEM)
    smem = pl.BlockSpec(memory_space=pltpu.SMEM)
    several = len(shapes) > 1
    out_shape = [jax.ShapeDtypeStruct(s, jnp.bfloat16) for s in shapes]
    return pl.pallas_call(
        kernel,
        out_shape=out_shape if several else out_shape[0],
        in_specs=[smem] * scalars + [vmem] * (len(operands) - scalars),
        out_specs=[vmem] * len(shapes) if several else vmem,
        compiler_params=pltpu.CompilerParams(vmem_limit_bytes=40 * 1024 * 1024),
        cost_estimate=pl.CostEstimate(flops=0, transcendentals=0, bytes_accessed=moved),
    )(*operands)


def dots(left, right):
    return lax.dot_general(left, right, (((1,), (1,)), ((), ())), preferred_element_type=jnp.float32)


def low(value):
    return value.astype(jnp.bfloat16)


def wide(value):
    return value.astype(jnp.float32)


def left_kernel(order_ref, plain_ref, weight_ref, away_ref, rest_ref):
    points, transitions, depth = plain_ref.shape
    owners = order_ref.shape[0] - 1
    blocks = transitions // (owners * BLOCK)
    weight = weight_ref[...]
    for point in range(points):
        for slot in range(owners):
            out_ref = (away_ref, rest_ref)[slot // 2]
            for block in range(blocks):
                start = pl.multiple_of((block * owners + order_ref[slot]) * BLOCK, BLOCK)
                rows = wide(plain_ref[point, pl.ds(start, BLOCK), :]) * weight
                real = pl.ds((slot % 2 * 2 * blocks + block) * BLOCK, BLOCK)
                imag = pl.ds(((slot % 2 * 2 + 1) * blocks + block) * BLOCK, BLOCK)
                out_ref[point, real, :] = low(rows)
                out_ref[point, imag, : depth // 2] = low(-rows[:, depth // 2 :])
                out_ref[point, imag, depth // 2 :] = low(rows[:, : depth // 2])


def agreeing(order_ref, point):
    even = order_ref[order_ref.shape[0] - 1]
    return point + even - 2 * even * point


def first_right(order_ref, point, mate_ref, near_ref):
    return mate_ref[agreeing(order_ref, point)], near_ref[...]


def second_right(order_ref, point, near_ref, later_ref):
    return jnp.where(agreeing(order_ref, point) == 0, near_ref[...], later_ref[...]), later_ref[...]


def away_kernel(rights):
    def kernel(order_ref, left_ref, mate_left_ref, one_ref, other_ref, out_ref):
        points, _, columns = out_ref.shape
        half = columns // 2
        for point in range(points):
            for part, right in enumerate(rights(order_ref, point, one_ref, other_ref)):
                rows = (left_ref, mate_left_ref)[part][point]
                out_ref[point, :, part * half : (part + 1) * half] = low(dots(rows, right))

    return kernel


def rest_kernel(rights):
    def kernel(order_ref, left_ref, mate_left_ref, one_ref, other_ref, out_ref):
        _, points, count, columns = out_ref.shape
        half = columns // 2
        for point in range(points):
            for part, right in enumerate(rights(order_ref, point, one_ref, other_ref)):
                out = low(dots((left_ref, mate_left_ref)[part][point], right))
                out_ref[0, point, :, part * half : (part + 1) * half] = out[:count]
                out_ref[1, point, :, part * half : (part + 1) * half] = out[count:]

    return kernel


def picked(order_ref, slots, rows, owners, transitions):
    n = lax.broadcasted_iota(jnp.int32, (rows, transitions), 0)
    column = lax.broadcasted_iota(jnp.int32, (rows, transitions), 1)
    target = (n // BLOCK * owners) * BLOCK + n % BLOCK
    return jnp.concatenate(
        [low(jnp.where(column == target + order_ref[slot] * BLOCK, 1.0, 0.0)) for slot in slots], axis=0
    )


def second_kernel(order_ref, rest_ref, got_ref, out_ref):
    points, count, _ = out_ref.shape
    half = rest_ref.shape[3] // 2
    owners = order_ref.shape[0] - 1
    pick = picked(order_ref, (2, 1), count // 2, owners, half)
    for point in range(points):
        out_ref[point, :, : 2 * half] = low(wide(rest_ref[0, point]) + wide(got_ref[point, count:, :]))
        own = low(wide(rest_ref[1, point]) + wide(got_ref[point, :count, :]))
        for part in range(2):
            place = (2 * half + part * count, 2 * half + (part + 1) * count)
            out_ref[point, :, place[0] : place[1]] = low(dots(own[:, part * half : (part + 1) * half], pick))


def turned_part(order_ref, block_ref, second_ref, late_ref, part):
    points, count, columns = block_ref.shape
    half = columns // 2
    rows = count // 2
    owners = order_ref.shape[0] - 1
    span = pl.ds(part * half, half)
    own = jnp.concatenate(
        [block_ref[point, p * rows : (p + 1) * rows, span] for p in range(2) for point in range(points)], axis=0
    )
    pick = picked(order_ref, (3, 0), rows, owners, half)
    others = []
    for point in range(points):
        other = dots(second_ref[point, :, span], pick) + wide(late_ref[point, :, pl.ds(columns + part * count, count)])
        others.append(low(other))
    other = jnp.concatenate(
        [others[point][p * rows : (p + 1) * rows] for p in range(2) for point in range(points)], axis=0
    )
    n = lax.broadcasted_iota(jnp.int32, (count, count), 0)
    same = low(jnp.where(n == lax.broadcasted_iota(jnp.int32, (count, count), 1), 1.0, 0.0))
    pieces = []
    for out in (dots(pick, own), dots(same, other)):
        for to in range(2):
            piece = out[to * rows : (to + 1) * rows]
            pieces.append(jnp.concatenate([low(piece[:, : points * rows]), low(-piece[:, points * rows :])], axis=0))
    return (pieces[0], pieces[2]), (pieces[1], pieces[3])


def finish(rest_ref, got_ref, late_ref, block_ref):
    points, count, columns = block_ref.shape
    for point in range(points):
        total = wide(rest_ref[1, point]) + wide(got_ref[point, :count, :]) + wide(late_ref[point, :, :columns])
        block_ref[point] = low(total)


def finish_kernel(order_ref, rest_ref, got_ref, second_ref, late_ref, block_ref, same_ref, first_ref):
    finish(rest_ref, got_ref, late_ref, block_ref)
    for part in range(2):
        same, first = turned_part(order_ref, block_ref, second_ref, late_ref, part)
        for source in range(2):
            same_ref[part, source] = same[source]
            first_ref[part, source] = first[source]


def pack_kernel(same_0_ref, passed_0_ref, same_1_ref, block_0_ref, block_1_ref, to_mate_ref, to_next_ref):
    points, count, columns = block_0_ref.shape
    strips = columns // 2 // count
    for part, ref in enumerate((to_mate_ref, to_next_ref)):
        ref[0:2] = same_0_ref[part]
        ref[2:4] = passed_0_ref[part]
        to_next_ref[4 + 2 * part : 6 + 2 * part] = same_1_ref[part]
    for point in range(points):
        for stream, ref in enumerate((block_0_ref, block_1_ref)):
            for strip in range(strips):
                tile = ref[point, :, columns // 2 + strip * count : columns // 2 + (strip + 1) * count]
                to_mate_ref[4 + (point * 2 + stream) * strips + strip] = tile


def spread(order_ref, slot, lanes, columns):
    n = lax.broadcasted_iota(jnp.int32, (lanes, columns), 0)
    column = lax.broadcasted_iota(jnp.int32, (lanes, columns), 1)
    target = (n // BLOCK * (order_ref.shape[0] - 1) + order_ref[slot]) * BLOCK + n % BLOCK
    return low(jnp.where(column == target, 1.0, 0.0))


def merge_kernel(order_ref, block_0_ref, block_1_ref, first_1_ref, from_next_ref, from_mate_ref, out_ref):
    points, count, columns = block_0_ref.shape
    rows = count // 2
    half = columns // 2
    even = order_ref[order_ref.shape[0] - 1]
    lanes = points * rows
    strips = columns // count
    back = 0.0
    for slot, source in enumerate((1, 3, 2, 0)):
        tiles = [from_mate_ref[source], from_next_ref[source]]
        for part in range(2):
            tiles += [from_next_ref[4 + 2 * part + source] if source < 2 else first_1_ref[part, source - 2]]
        back = back + lax.dot_general(
            jnp.concatenate(tiles, axis=0),
            spread(order_ref, slot, lanes, columns),
            (((1,), (0,)), ((), ())),
            preferred_element_type=jnp.float32,
        )
    back = low(back)
    for p in range(2):
        for kind, block_ref, place in ((0, block_0_ref, 2 * even), (2, block_1_ref, 2 - 2 * even)):
            natural = back[kind * count + p * rows : kind * count + (p + 1) * rows]
            for row_point in range(points):
                here = block_ref[row_point, p * rows : (p + 1) * rows, :half]
                for column_point in range(points):
                    there = natural[:, column_point * half : (column_point + 1) * half]
                    mine = even == (0 if row_point == column_point else 1)
                    out_ref[
                        place, p, row_point * rows : (row_point + 1) * rows, column_point * half : (column_point + 1) * half
                    ] = jnp.where(mine, here, there)
        for point in range(points):
            span = slice(point * rows, (point + 1) * rows)
            for strip in range(strips):
                tile = from_mate_ref[4 + point * strips + strip, p * rows : (p + 1) * rows, :]
                out_ref[1 + 2 * even, p, span, strip * count : (strip + 1) * count] = tile
            begin = (1 + 2 * point) * count + p * rows
            out_ref[3 - 2 * even, p, span, :] = back[begin : begin + rows]


def body(pair_density, coulomb):
    points, transitions, _, g_local = pair_density.shape
    owners = lax.axis_size("own")
    groups = lax.axis_size("kp")
    blocks = transitions // (owners * BLOCK)
    rows = blocks * BLOCK
    depth = 2 * g_local
    scale = 1.0 / math.sqrt(g_local * owners)
    me = lax.axis_index("own")
    odd = lax.axis_index("kp") % 2 == 1
    parity = odd.astype(jnp.int32)

    def exchange_kp(value, partner):
        return lax.ppermute(value, "kp", [(i, partner(i) % groups) for i in range(groups)])

    def flips(i):
        return [1, 2, 3, 0] if i % 2 == 0 else [3, 2, 1, 0]

    def exchange(value, slot, partner):
        pairs = [
            (i * owners + o, partner(i) % groups * owners + (o ^ flips(i)[slot]))
            for i in range(groups)
            for o in range(owners)
        ]
        return lax.ppermute(value, ("kp", "own"), pairs)

    def exchange_own(value, first):
        return exchange(value, 0 if first else 2, lambda i: i)

    def mate(i):
        return i + 1 if i % 2 == 0 else i - 1

    def across(i):
        return i - 1 if i % 2 == 0 else i + 1

    near_flip, far_flip = 1 + 2 * parity, 3 - 2 * parity
    relative = jnp.stack([me ^ near_flip, me ^ 2, me ^ far_flip, me, 1 - parity])

    plain = pair_density.reshape(points, transitions, depth)
    near = exchange_kp(plain[0], across)
    mate_right = exchange_kp(plain, mate)

    weights = (jnp.concatenate([coulomb, coulomb]) * scale).reshape(1, depth)
    left_shape = [(points, 4 * rows, depth)] * 2
    left_away, left_rest = local(left_kernel, left_shape, relative, plain, weights, scalars=1, moved=4 << 20)
    held, _ = lax.optimization_barrier((plain, left_away))
    later = exchange_kp(held[1], across)
    mate_away, mate_rest = local(left_kernel, left_shape, relative, mate_right, weights, scalars=1, moved=4 << 20)
    near, mate_away = lax.optimization_barrier((near, mate_away))

    columns = points * transitions
    away_shape = [(points, 4 * rows, columns)]
    rest_shape = [(2, points, 2 * rows, columns)]
    second_shape = [(points, 2 * rows, columns + 4 * rows)]
    block_shape = (points, 2 * rows, columns)
    tile = (2 * rows, points * rows)
    strips = points * columns // tile[1]

    away_0 = local(away_kernel(first_right), away_shape, relative, left_away, mate_away, mate_right, near, scalars=1)
    got_0 = exchange_own(away_0, True)
    later, _ = lax.optimization_barrier((later, away_0))
    away_1 = local(away_kernel(second_right), away_shape, relative, left_away, mate_away, near, later, scalars=1)
    got_1 = exchange_own(away_1, True)
    left_rest, mate_rest, _ = lax.optimization_barrier((left_rest, mate_rest, away_1))
    rest_0 = local(
        rest_kernel(first_right), rest_shape, relative, left_rest, mate_rest, mate_right, near, scalars=1, moved=8 << 20
    )
    rest_1 = local(
        rest_kernel(second_right), rest_shape, relative, left_rest, mate_rest, near, later, scalars=1, moved=8 << 20
    )
    got_0, rest_0, rest_1 = lax.optimization_barrier((got_0, rest_0, rest_1))
    second_0 = local(second_kernel, second_shape, relative, rest_0, got_0, scalars=1)
    late_0 = exchange_own(second_0, False)
    got_1, _ = lax.optimization_barrier((got_1, second_0))
    second_1 = local(second_kernel, second_shape, relative, rest_1, got_1, scalars=1)
    late_1 = exchange_own(second_1, False)
    late_0, _ = lax.optimization_barrier((late_0, second_1))
    finish_shape = [block_shape, (2, 2, *tile), (2, 2, *tile)]
    block_0, same_0, first_0 = local(finish_kernel, finish_shape, relative, rest_0, got_0, second_0, late_0, scalars=1)
    passed_0 = exchange_own(first_0, True)
    late_1, _ = lax.optimization_barrier((late_1, first_0))
    block_1, same_1, first_1 = local(finish_kernel, finish_shape, relative, rest_1, got_1, second_1, late_1, scalars=1)
    to_mate, to_next = local(
        pack_kernel, [(4 + strips, *tile), (8, *tile)], same_0, passed_0, same_1, block_0, block_1, moved=16 << 20
    )
    first_1 = exchange(first_1, 0, across)
    from_next = exchange_kp(to_next, across)
    from_mate = exchange_kp(to_mate, mate)
    out = local(
        merge_kernel, [(4, 2, points * rows, columns)],
        relative, block_0, block_1, first_1, from_next, from_mate, scalars=1,
    )
    return out.transpose(0, 2, 1, 3)


def solution(mesh):
    placed = (P("kp", None, None, "own"), P("own"))
    return jax.shard_map(
        body,
        mesh=mesh,
        in_specs=placed,
        out_specs=P(None, ("kp", "own"), None, None),
        check_vma=False,
    )
```

```python
import math

import jax
import jax.numpy as jnp
from jax import lax
from jax.experimental import pallas as pl
from jax.experimental.pallas import tpu as pltpu
from jax.sharding import PartitionSpec as P

BLOCK = 32


def local(kernel, shapes, *operands, scalars=0, moved=0):
    vmem = pl.BlockSpec(memory_space=pltpu.VMEM)
    smem = pl.BlockSpec(memory_space=pltpu.SMEM)
    several = len(shapes) > 1
    out_shape = [jax.ShapeDtypeStruct(s, jnp.bfloat16) for s in shapes]
    return pl.pallas_call(
        kernel,
        out_shape=out_shape if several else out_shape[0],
        in_specs=[smem] * scalars + [vmem] * (len(operands) - scalars),
        out_specs=[vmem] * len(shapes) if several else vmem,
        compiler_params=pltpu.CompilerParams(vmem_limit_bytes=40 * 1024 * 1024),
        cost_estimate=pl.CostEstimate(flops=0, transcendentals=0, bytes_accessed=moved),
    )(*operands)


def dots(left, right):
    return lax.dot_general(left, right, (((1,), (1,)), ((), ())), preferred_element_type=jnp.float32)


def low(value):
    return value.astype(jnp.bfloat16)


def wide(value):
    return value.astype(jnp.float32)


def left_kernel(order_ref, plain_ref, weight_ref, away_ref, rest_ref):
    points, transitions, depth = plain_ref.shape
    owners = order_ref.shape[0] - 1
    blocks = transitions // (owners * BLOCK)
    weight = weight_ref[...]
    for point in range(points):
        for slot in range(owners):
            out_ref = (away_ref, rest_ref)[slot // 2]
            for block in range(blocks):
                start = pl.multiple_of((block * owners + order_ref[slot]) * BLOCK, BLOCK)
                rows = wide(plain_ref[point, pl.ds(start, BLOCK), :]) * weight
                real = pl.ds((slot % 2 * 2 * blocks + block) * BLOCK, BLOCK)
                imag = pl.ds(((slot % 2 * 2 + 1) * blocks + block) * BLOCK, BLOCK)
                out_ref[point, real, :] = low(rows)
                out_ref[point, imag, : depth // 2] = low(-rows[:, depth // 2 :])
                out_ref[point, imag, depth // 2 :] = low(rows[:, : depth // 2])


def agreeing(order_ref, point):
    even = order_ref[order_ref.shape[0] - 1]
    return point + even - 2 * even * point


def first_right(order_ref, point, mate_ref, near_ref):
    return mate_ref[agreeing(order_ref, point)], near_ref[...]


def second_right(order_ref, point, near_ref, later_ref):
    return jnp.where(agreeing(order_ref, point) == 0, near_ref[...], later_ref[...]), later_ref[...]


def away_kernel(rights):
    def kernel(order_ref, left_ref, mate_left_ref, one_ref, other_ref, out_ref):
        points, _, columns = out_ref.shape
        half = columns // 2
        for point in range(points):
            for part, right in enumerate(rights(order_ref, point, one_ref, other_ref)):
                rows = (left_ref, mate_left_ref)[part][point]
                out_ref[point, :, part * half : (part + 1) * half] = low(dots(rows, right))

    return kernel


def rest_kernel(rights):
    def kernel(order_ref, left_ref, mate_left_ref, one_ref, other_ref, out_ref):
        _, points, count, columns = out_ref.shape
        half = columns // 2
        for point in range(points):
            for part, right in enumerate(rights(order_ref, point, one_ref, other_ref)):
                out = low(dots((left_ref, mate_left_ref)[part][point], right))
                out_ref[0, point, :, part * half : (part + 1) * half] = out[:count]
                out_ref[1, point, :, part * half : (part + 1) * half] = out[count:]

    return kernel


def picked(order_ref, slots, rows, owners, transitions):
    n = lax.broadcasted_iota(jnp.int32, (rows, transitions), 0)
    column = lax.broadcasted_iota(jnp.int32, (rows, transitions), 1)
    target = (n // BLOCK * owners) * BLOCK + n % BLOCK
    return jnp.concatenate(
        [low(jnp.where(column == target + order_ref[slot] * BLOCK, 1.0, 0.0)) for slot in slots], axis=0
    )


def second_kernel(order_ref, rest_ref, got_ref, out_ref):
    points, count, _ = out_ref.shape
    half = rest_ref.shape[3] // 2
    owners = order_ref.shape[0] - 1
    pick = picked(order_ref, (2, 1), count // 2, owners, half)
    for point in range(points):
        out_ref[point, :, : 2 * half] = low(wide(rest_ref[0, point]) + wide(got_ref[point, count:, :]))
        own = low(wide(rest_ref[1, point]) + wide(got_ref[point, :count, :]))
        for part in range(2):
            place = (2 * half + part * count, 2 * half + (part + 1) * count)
            out_ref[point, :, place[0] : place[1]] = low(dots(own[:, part * half : (part + 1) * half], pick))


def turned_part(order_ref, block_ref, second_ref, late_ref, part):
    points, count, columns = block_ref.shape
    half = columns // 2
    rows = count // 2
    owners = order_ref.shape[0] - 1
    span = pl.ds(part * half, half)
    own = jnp.concatenate(
        [block_ref[point, p * rows : (p + 1) * rows, span] for p in range(2) for point in range(points)], axis=0
    )
    pick = picked(order_ref, (3, 0), rows, owners, half)
    others = []
    for point in range(points):
        other = dots(second_ref[point, :, span], pick) + wide(late_ref[point, :, pl.ds(columns + part * count, count)])
        others.append(low(other))
    other = jnp.concatenate(
        [others[point][p * rows : (p + 1) * rows] for p in range(2) for point in range(points)], axis=0
    )
    n = lax.broadcasted_iota(jnp.int32, (count, count), 0)
    same = low(jnp.where(n == lax.broadcasted_iota(jnp.int32, (count, count), 1), 1.0, 0.0))
    pieces = []
    for out in (dots(pick, own), dots(same, other)):
        for to in range(2):
            piece = out[to * rows : (to + 1) * rows]
            pieces.append(jnp.concatenate([low(piece[:, : points * rows]), low(-piece[:, points * rows :])], axis=0))
    return (pieces[0], pieces[2]), (pieces[1], pieces[3])


def finish(rest_ref, got_ref, late_ref, block_ref):
    points, count, columns = block_ref.shape
    for point in range(points):
        total = wide(rest_ref[1, point]) + wide(got_ref[point, :count, :]) + wide(late_ref[point, :, :columns])
        block_ref[point] = low(total)


def finish_kernel(order_ref, rest_ref, got_ref, second_ref, late_ref, block_ref, same_ref, first_ref):
    finish(rest_ref, got_ref, late_ref, block_ref)
    for part in range(2):
        same, first = turned_part(order_ref, block_ref, second_ref, late_ref, part)
        for source in range(2):
            same_ref[part, source] = same[source]
            first_ref[part, source] = first[source]


def pack_kernel(same_0_ref, passed_0_ref, same_1_ref, block_0_ref, block_1_ref, to_mate_ref, to_next_ref):
    points, count, columns = block_0_ref.shape
    strips = columns // 2 // count
    for part, ref in enumerate((to_mate_ref, to_next_ref)):
        ref[0:2] = same_0_ref[part]
        ref[2:4] = passed_0_ref[part]
        to_next_ref[4 + 2 * part : 6 + 2 * part] = same_1_ref[part]
    for point in range(points):
        for stream, ref in enumerate((block_0_ref, block_1_ref)):
            for strip in range(strips):
                tile = ref[point, :, columns // 2 + strip * count : columns // 2 + (strip + 1) * count]
                to_mate_ref[4 + (point * 2 + stream) * strips + strip] = tile


def spread(order_ref, slot, lanes, columns):
    n = lax.broadcasted_iota(jnp.int32, (lanes, columns), 0)
    column = lax.broadcasted_iota(jnp.int32, (lanes, columns), 1)
    target = (n // BLOCK * (order_ref.shape[0] - 1) + order_ref[slot]) * BLOCK + n % BLOCK
    return low(jnp.where(column == target, 1.0, 0.0))


def merge_kernel(order_ref, block_0_ref, block_1_ref, first_1_ref, from_next_ref, from_mate_ref, out_ref):
    points, count, columns = block_0_ref.shape
    rows = count // 2
    half = columns // 2
    even = order_ref[order_ref.shape[0] - 1]
    lanes = points * rows
    strips = columns // count
    back = 0.0
    for slot, source in enumerate((1, 3, 2, 0)):
        tiles = [from_mate_ref[source], from_next_ref[source]]
        for part in range(2):
            tiles += [from_next_ref[4 + 2 * part + source] if source < 2 else first_1_ref[part, source - 2]]
        back = back + lax.dot_general(
            jnp.concatenate(tiles, axis=0),
            spread(order_ref, slot, lanes, columns),
            (((1,), (0,)), ((), ())),
            preferred_element_type=jnp.float32,
        )
    back = low(back)
    for p in range(2):
        for kind, block_ref, place in ((0, block_0_ref, 2 * even), (2, block_1_ref, 2 - 2 * even)):
            natural = back[kind * count + p * rows : kind * count + (p + 1) * rows]
            for row_point in range(points):
                here = block_ref[row_point, p * rows : (p + 1) * rows, :half]
                for column_point in range(points):
                    there = natural[:, column_point * half : (column_point + 1) * half]
                    mine = even == (0 if row_point == column_point else 1)
                    out_ref[
                        place, p, row_point * rows : (row_point + 1) * rows, column_point * half : (column_point + 1) * half
                    ] = jnp.where(mine, here, there)
        for point in range(points):
            span = slice(point * rows, (point + 1) * rows)
            for strip in range(strips):
                tile = from_mate_ref[4 + point * strips + strip, p * rows : (p + 1) * rows, :]
                out_ref[1 + 2 * even, p, span, strip * count : (strip + 1) * count] = tile
            begin = (1 + 2 * point) * count + p * rows
            out_ref[3 - 2 * even, p, span, :] = back[begin : begin + rows]


def body(pair_density, coulomb):
    points, transitions, _, g_local = pair_density.shape
    owners = lax.axis_size("own")
    groups = lax.axis_size("kp")
    blocks = transitions // (owners * BLOCK)
    rows = blocks * BLOCK
    depth = 2 * g_local
    scale = 1.0 / math.sqrt(g_local * owners)
    me = lax.axis_index("own")
    odd = lax.axis_index("kp") % 2 == 1
    parity = odd.astype(jnp.int32)

    def exchange_kp(value, partner):
        return lax.ppermute(value, "kp", [(i, partner(i) % groups) for i in range(groups)])

    def flips(i):
        return [1, 2, 3, 0] if i % 2 == 0 else [3, 2, 1, 0]

    def exchange(value, slot, partner):
        pairs = [
            (i * owners + o, partner(i) % groups * owners + (o ^ flips(i)[slot]))
            for i in range(groups)
            for o in range(owners)
        ]
        return lax.ppermute(value, ("kp", "own"), pairs)

    def exchange_own(value, first):
        return exchange(value, 0 if first else 2, lambda i: i)

    def mate(i):
        return i + 1 if i % 2 == 0 else i - 1

    def across(i):
        return i - 1 if i % 2 == 0 else i + 1

    near_flip, far_flip = 1 + 2 * parity, 3 - 2 * parity
    relative = jnp.stack([me ^ near_flip, me ^ 2, me ^ far_flip, me, 1 - parity])

    plain = lax.optimization_barrier(pair_density.reshape(points, transitions, depth))
    near = exchange_kp(plain[0], across)
    later = exchange_kp(plain[1], across)
    mate_right = exchange_kp(plain, mate)

    weights = (jnp.concatenate([coulomb, coulomb]) * scale).reshape(1, depth)
    left_shape = [(points, 4 * rows, depth)] * 2
    left_away, left_rest = local(left_kernel, left_shape, relative, plain, weights, scalars=1, moved=4 << 20)
    mate_away, mate_rest = local(left_kernel, left_shape, relative, mate_right, weights, scalars=1, moved=4 << 20)
    near, mate_away = lax.optimization_barrier((near, mate_away))

    columns = points * transitions
    away_shape = [(points, 4 * rows, columns)]
    rest_shape = [(2, points, 2 * rows, columns)]
    second_shape = [(points, 2 * rows, columns + 4 * rows)]
    block_shape = (points, 2 * rows, columns)
    tile = (2 * rows, points * rows)
    strips = points * columns // tile[1]

    away_0 = local(away_kernel(first_right), away_shape, relative, left_away, mate_away, mate_right, near, scalars=1)
    got_0 = exchange_own(away_0, True)
    later, _ = lax.optimization_barrier((later, away_0))
    away_1 = local(away_kernel(second_right), away_shape, relative, left_away, mate_away, near, later, scalars=1)
    got_1 = exchange_own(away_1, True)
    left_rest, mate_rest, _ = lax.optimization_barrier((left_rest, mate_rest, away_1))
    rest_0 = local(
        rest_kernel(first_right), rest_shape, relative, left_rest, mate_rest, mate_right, near, scalars=1, moved=8 << 20
    )
    rest_1 = local(
        rest_kernel(second_right), rest_shape, relative, left_rest, mate_rest, near, later, scalars=1, moved=8 << 20
    )
    got_0, rest_0, rest_1 = lax.optimization_barrier((got_0, rest_0, rest_1))
    second_0 = local(second_kernel, second_shape, relative, rest_0, got_0, scalars=1)
    late_0 = exchange_own(second_0, False)
    got_1, _ = lax.optimization_barrier((got_1, second_0))
    second_1 = local(second_kernel, second_shape, relative, rest_1, got_1, scalars=1)
    late_1 = exchange_own(second_1, False)
    late_0, _ = lax.optimization_barrier((late_0, second_1))
    finish_shape = [block_shape, (2, 2, *tile), (2, 2, *tile)]
    block_0, same_0, first_0 = local(finish_kernel, finish_shape, relative, rest_0, got_0, second_0, late_0, scalars=1)
    passed_0 = exchange_own(first_0, True)
    late_1, _ = lax.optimization_barrier((late_1, first_0))
    block_1, same_1, first_1 = local(finish_kernel, finish_shape, relative, rest_1, got_1, second_1, late_1, scalars=1)
    to_mate, to_next = local(
        pack_kernel, [(4 + strips, *tile), (8, *tile)], same_0, passed_0, same_1, block_0, block_1, moved=16 << 20
    )
    first_1 = exchange(first_1, 0, across)
    from_next = exchange_kp(to_next, across)
    from_mate = exchange_kp(to_mate, mate)
    out = local(
        merge_kernel, [(4, 2, points * rows, columns)],
        relative, block_0, block_1, first_1, from_next, from_mate, scalars=1,
    )
    return out.transpose(0, 2, 1, 3)


def solution(mesh):
    placed = (P("kp", None, None, "own"), P("own"))
    return jax.shard_map(
        body,
        mesh=mesh,
        in_specs=placed,
        out_specs=P(None, ("kp", "own"), None, None),
        check_vma=False,
    )
```

```python
import math

import jax
import jax.numpy as jnp
from jax import lax
from jax.experimental import pallas as pl
from jax.experimental.pallas import tpu as pltpu
from jax.sharding import PartitionSpec as P

BLOCK = 32


def local(kernel, shapes, *operands, scalars=0, moved=0):
    vmem = pl.BlockSpec(memory_space=pltpu.VMEM)
    smem = pl.BlockSpec(memory_space=pltpu.SMEM)
    several = len(shapes) > 1
    out_shape = [jax.ShapeDtypeStruct(s, jnp.bfloat16) for s in shapes]
    return pl.pallas_call(
        kernel,
        out_shape=out_shape if several else out_shape[0],
        in_specs=[smem] * scalars + [vmem] * (len(operands) - scalars),
        out_specs=[vmem] * len(shapes) if several else vmem,
        compiler_params=pltpu.CompilerParams(vmem_limit_bytes=40 * 1024 * 1024),
        cost_estimate=pl.CostEstimate(flops=0, transcendentals=0, bytes_accessed=moved),
    )(*operands)


def dots(left, right):
    return lax.dot_general(left, right, (((1,), (1,)), ((), ())), preferred_element_type=jnp.float32)


def low(value):
    return value.astype(jnp.bfloat16)


def wide(value):
    return value.astype(jnp.float32)


def left_kernel(order_ref, plain_ref, weight_ref, away_ref, rest_ref):
    points, transitions, depth = plain_ref.shape
    owners = order_ref.shape[0] - 1
    blocks = transitions // (owners * BLOCK)
    weight = weight_ref[...]
    for point in range(points):
        for slot in range(owners):
            out_ref = (away_ref, rest_ref)[slot // 2]
            for block in range(blocks):
                start = pl.multiple_of((block * owners + order_ref[slot]) * BLOCK, BLOCK)
                rows = wide(plain_ref[point, pl.ds(start, BLOCK), :]) * weight
                real = pl.ds((slot % 2 * 2 * blocks + block) * BLOCK, BLOCK)
                imag = pl.ds(((slot % 2 * 2 + 1) * blocks + block) * BLOCK, BLOCK)
                out_ref[point, real, :] = low(rows)
                out_ref[point, imag, : depth // 2] = low(-rows[:, depth // 2 :])
                out_ref[point, imag, depth // 2 :] = low(rows[:, : depth // 2])


def agreeing(order_ref, point):
    even = order_ref[order_ref.shape[0] - 1]
    return point + even - 2 * even * point


def first_right(order_ref, point, mate_ref, near_ref):
    return mate_ref[agreeing(order_ref, point)], near_ref[...]


def second_right(order_ref, point, near_ref, later_ref):
    return jnp.where(agreeing(order_ref, point) == 0, near_ref[...], later_ref[...]), later_ref[...]


def away_kernel(rights):
    def kernel(order_ref, left_ref, mate_left_ref, one_ref, other_ref, out_ref):
        points, _, columns = out_ref.shape
        half = columns // 2
        for point in range(points):
            for part, right in enumerate(rights(order_ref, point, one_ref, other_ref)):
                rows = (left_ref, mate_left_ref)[part][point]
                out_ref[point, :, part * half : (part + 1) * half] = low(dots(rows, right))

    return kernel


def rest_kernel(rights):
    def kernel(order_ref, left_ref, mate_left_ref, one_ref, other_ref, out_ref):
        _, points, count, columns = out_ref.shape
        half = columns // 2
        for point in range(points):
            for part, right in enumerate(rights(order_ref, point, one_ref, other_ref)):
                out = low(dots((left_ref, mate_left_ref)[part][point], right))
                out_ref[0, point, :, part * half : (part + 1) * half] = out[:count]
                out_ref[1, point, :, part * half : (part + 1) * half] = out[count:]

    return kernel


def picked(order_ref, slots, rows, owners, transitions):
    n = lax.broadcasted_iota(jnp.int32, (rows, transitions), 0)
    column = lax.broadcasted_iota(jnp.int32, (rows, transitions), 1)
    target = (n // BLOCK * owners) * BLOCK + n % BLOCK
    return jnp.concatenate(
        [low(jnp.where(column == target + order_ref[slot] * BLOCK, 1.0, 0.0)) for slot in slots], axis=0
    )


def second_kernel(order_ref, rest_ref, got_ref, out_ref):
    points, count, _ = out_ref.shape
    half = rest_ref.shape[3] // 2
    owners = order_ref.shape[0] - 1
    pick = picked(order_ref, (2, 1), count // 2, owners, half)
    for point in range(points):
        out_ref[point, :, : 2 * half] = low(wide(rest_ref[0, point]) + wide(got_ref[point, count:, :]))
        own = low(wide(rest_ref[1, point]) + wide(got_ref[point, :count, :]))
        for part in range(2):
            place = (2 * half + part * count, 2 * half + (part + 1) * count)
            out_ref[point, :, place[0] : place[1]] = low(dots(own[:, part * half : (part + 1) * half], pick))


def turned_part(order_ref, block_ref, second_ref, late_ref, part):
    points, count, columns = block_ref.shape
    half = columns // 2
    rows = count // 2
    owners = order_ref.shape[0] - 1
    span = pl.ds(part * half, half)
    own = jnp.concatenate(
        [block_ref[point, p * rows : (p + 1) * rows, span] for p in range(2) for point in range(points)], axis=0
    )
    pick = picked(order_ref, (3, 0), rows, owners, half)
    others = []
    for point in range(points):
        other = dots(second_ref[point, :, span], pick) + wide(late_ref[point, :, pl.ds(columns + part * count, count)])
        others.append(low(other))
    other = jnp.concatenate(
        [others[point][p * rows : (p + 1) * rows] for p in range(2) for point in range(points)], axis=0
    )
    n = lax.broadcasted_iota(jnp.int32, (count, count), 0)
    same = low(jnp.where(n == lax.broadcasted_iota(jnp.int32, (count, count), 1), 1.0, 0.0))
    pieces = []
    for out in (dots(pick, own), dots(same, other)):
        for to in range(2):
            piece = out[to * rows : (to + 1) * rows]
            pieces.append(jnp.concatenate([low(piece[:, : points * rows]), low(-piece[:, points * rows :])], axis=0))
    return (pieces[0], pieces[2]), (pieces[1], pieces[3])


def finish(rest_ref, got_ref, late_ref, block_ref):
    points, count, columns = block_ref.shape
    for point in range(points):
        total = wide(rest_ref[1, point]) + wide(got_ref[point, :count, :]) + wide(late_ref[point, :, :columns])
        block_ref[point] = low(total)


def finish_kernel(order_ref, rest_ref, got_ref, second_ref, late_ref, block_ref, same_ref, first_ref):
    finish(rest_ref, got_ref, late_ref, block_ref)
    for part in range(2):
        same, first = turned_part(order_ref, block_ref, second_ref, late_ref, part)
        for source in range(2):
            same_ref[part, source] = same[source]
            first_ref[part, source] = first[source]


def pack_kernel(same_0_ref, passed_0_ref, same_1_ref, block_0_ref, block_1_ref, to_mate_ref, to_next_ref):
    points, count, columns = block_0_ref.shape
    strips = columns // 2 // count
    for part, ref in enumerate((to_mate_ref, to_next_ref)):
        ref[0:2] = same_0_ref[part]
        ref[2:4] = passed_0_ref[part]
        to_next_ref[4 + 2 * part : 6 + 2 * part] = same_1_ref[part]
    for point in range(points):
        for stream, ref in enumerate((block_0_ref, block_1_ref)):
            for strip in range(strips):
                tile = ref[point, :, columns // 2 + strip * count : columns // 2 + (strip + 1) * count]
                to_mate_ref[4 + (point * 2 + stream) * strips + strip] = tile


def spread(order_ref, slot, lanes, columns):
    n = lax.broadcasted_iota(jnp.int32, (lanes, columns), 0)
    column = lax.broadcasted_iota(jnp.int32, (lanes, columns), 1)
    target = (n // BLOCK * (order_ref.shape[0] - 1) + order_ref[slot]) * BLOCK + n % BLOCK
    return low(jnp.where(column == target, 1.0, 0.0))


def merge_kernel(order_ref, held_ref, first_1_ref, from_next_ref, from_mate_ref, out_ref):
    _, _, height, columns = out_ref.shape
    _, count, lanes = from_mate_ref.shape
    rows = count // 2
    points = height // rows
    half = columns // 2
    even = order_ref[order_ref.shape[0] - 1]
    lanes = points * rows
    strips = columns // count
    back = 0.0
    for slot, source in enumerate((1, 3, 2, 0)):
        tiles = [from_mate_ref[source], from_next_ref[source]]
        for part in range(2):
            tiles += [from_next_ref[4 + 2 * part + source] if source < 2 else first_1_ref[part, source - 2]]
        back = back + lax.dot_general(
            jnp.concatenate(tiles, axis=0),
            spread(order_ref, slot, lanes, columns),
            (((1,), (0,)), ((), ())),
            preferred_element_type=jnp.float32,
        )
    back = low(back)
    for p in range(2):
        for kind, place in ((0, 2 * even), (2, 2 - 2 * even)):
            natural = back[kind * count + p * rows : kind * count + (p + 1) * rows]
            for row_point in range(points):
                for column_point in range(points):
                    there = natural[:, column_point * half : (column_point + 1) * half]
                    other = even == (1 if row_point == column_point else 0)
                    down = slice(row_point * rows, (row_point + 1) * rows)
                    along = slice(column_point * half, (column_point + 1) * half)
                    out_ref[place, p, down, along] = jnp.where(other, there, held_ref[place, p, down, along])
        for point in range(points):
            span = slice(point * rows, (point + 1) * rows)
            for strip in range(strips):
                tile = from_mate_ref[4 + point * strips + strip, p * rows : (p + 1) * rows, :]
                out_ref[1 + 2 * even, p, span, strip * count : (strip + 1) * count] = tile
            begin = (1 + 2 * point) * count + p * rows
            out_ref[3 - 2 * even, p, span, :] = back[begin : begin + rows]


def body(pair_density, coulomb):
    points, transitions, _, g_local = pair_density.shape
    owners = lax.axis_size("own")
    groups = lax.axis_size("kp")
    blocks = transitions // (owners * BLOCK)
    rows = blocks * BLOCK
    depth = 2 * g_local
    scale = 1.0 / math.sqrt(g_local * owners)
    me = lax.axis_index("own")
    odd = lax.axis_index("kp") % 2 == 1
    parity = odd.astype(jnp.int32)

    def exchange_kp(value, partner):
        return lax.ppermute(value, "kp", [(i, partner(i) % groups) for i in range(groups)])

    def flips(i):
        return [1, 2, 3, 0] if i % 2 == 0 else [3, 2, 1, 0]

    def exchange(value, slot, partner):
        pairs = [
            (i * owners + o, partner(i) % groups * owners + (o ^ flips(i)[slot]))
            for i in range(groups)
            for o in range(owners)
        ]
        return lax.ppermute(value, ("kp", "own"), pairs)

    def exchange_own(value, first):
        return exchange(value, 0 if first else 2, lambda i: i)

    def mate(i):
        return i + 1 if i % 2 == 0 else i - 1

    def across(i):
        return i - 1 if i % 2 == 0 else i + 1

    near_flip, far_flip = 1 + 2 * parity, 3 - 2 * parity
    relative = jnp.stack([me ^ near_flip, me ^ 2, me ^ far_flip, me, 1 - parity])

    plain = lax.optimization_barrier(pair_density.reshape(points, transitions, depth))
    near = exchange_kp(plain[0], across)
    later = exchange_kp(plain[1], across)
    mate_right = exchange_kp(plain, mate)

    weights = (jnp.concatenate([coulomb, coulomb]) * scale).reshape(1, depth)
    left_shape = [(points, 4 * rows, depth)] * 2
    left_away, left_rest = local(left_kernel, left_shape, relative, plain, weights, scalars=1, moved=4 << 20)
    mate_away, mate_rest = local(left_kernel, left_shape, relative, mate_right, weights, scalars=1, moved=4 << 20)
    near, mate_away = lax.optimization_barrier((near, mate_away))

    columns = points * transitions
    away_shape = [(points, 4 * rows, columns)]
    rest_shape = [(2, points, 2 * rows, columns)]
    second_shape = [(points, 2 * rows, columns + 4 * rows)]
    block_shape = (points, 2 * rows, columns)
    tile = (2 * rows, points * rows)
    strips = points * columns // tile[1]

    away_0 = local(away_kernel(first_right), away_shape, relative, left_away, mate_away, mate_right, near, scalars=1)
    got_0 = exchange_own(away_0, True)
    later, _ = lax.optimization_barrier((later, away_0))
    away_1 = local(away_kernel(second_right), away_shape, relative, left_away, mate_away, near, later, scalars=1)
    got_1 = exchange_own(away_1, True)
    left_rest, mate_rest, _ = lax.optimization_barrier((left_rest, mate_rest, away_1))
    rest_0 = local(
        rest_kernel(first_right), rest_shape, relative, left_rest, mate_rest, mate_right, near, scalars=1, moved=8 << 20
    )
    rest_1 = local(
        rest_kernel(second_right), rest_shape, relative, left_rest, mate_rest, near, later, scalars=1, moved=8 << 20
    )
    got_0, rest_0, rest_1 = lax.optimization_barrier((got_0, rest_0, rest_1))
    second_0 = local(second_kernel, second_shape, relative, rest_0, got_0, scalars=1)
    late_0 = exchange_own(second_0, False)
    got_1, _ = lax.optimization_barrier((got_1, second_0))
    second_1 = local(second_kernel, second_shape, relative, rest_1, got_1, scalars=1)
    late_1 = exchange_own(second_1, False)
    late_0, _ = lax.optimization_barrier((late_0, second_1))
    finish_shape = [block_shape, (2, 2, *tile), (2, 2, *tile)]
    block_0, same_0, first_0 = local(finish_kernel, finish_shape, relative, rest_0, got_0, second_0, late_0, scalars=1)
    passed_0 = exchange_own(first_0, True)
    late_1, _ = lax.optimization_barrier((late_1, first_0))
    block_1, same_1, first_1 = local(finish_kernel, finish_shape, relative, rest_1, got_1, second_1, late_1, scalars=1)
    to_mate, to_next = local(
        pack_kernel, [(4 + strips, *tile), (8, *tile)], same_0, passed_0, same_1, block_0, block_1, moved=16 << 20
    )
    first_1 = exchange(first_1, 0, across)
    from_next = exchange_kp(to_next, across)
    from_mate = exchange_kp(to_mate, mate)
    def quadrants(block):
        own = block[..., :transitions].reshape(points, 2, rows, transitions)
        lines = []
        for row_point in range(points):
            here = [odd if row_point == column_point else ~odd for column_point in range(points)]
            lines.append(jnp.concatenate([jnp.where(h, own[row_point], 0) for h in here], axis=-1))
        return jnp.concatenate(lines, axis=1)

    with_mate, with_next = quadrants(block_0), quadrants(block_1)
    nothing = jnp.zeros_like(with_mate)
    held = jnp.stack([jnp.where(odd, with_mate, with_next), nothing, jnp.where(odd, with_next, with_mate), nothing])
    held = lax.optimization_barrier(held)
    out = local(
        merge_kernel, [(4, 2, points * rows, columns)], relative, held, first_1, from_next, from_mate, scalars=1
    )
    return out.transpose(0, 2, 1, 3)


def solution(mesh):
    placed = (P("kp", None, None, "own"), P("own"))
    return jax.shard_map(
        body,
        mesh=mesh,
        in_specs=placed,
        out_specs=P(None, ("kp", "own"), None, None),
        check_vma=False,
    )
```

```python
import math

import jax
import jax.numpy as jnp
from jax import lax
from jax.experimental import pallas as pl
from jax.experimental.pallas import tpu as pltpu
from jax.sharding import PartitionSpec as P

BLOCK = 32
PARTS = 4


def local(kernel, shapes, *operands, scalars=0, moved=0):
    vmem = pl.BlockSpec(memory_space=pltpu.VMEM)
    smem = pl.BlockSpec(memory_space=pltpu.SMEM)
    several = len(shapes) > 1
    out_shape = [jax.ShapeDtypeStruct(s, jnp.bfloat16) for s in shapes]
    return pl.pallas_call(
        kernel,
        out_shape=out_shape if several else out_shape[0],
        in_specs=[smem] * scalars + [vmem] * (len(operands) - scalars),
        out_specs=[vmem] * len(shapes) if several else vmem,
        compiler_params=pltpu.CompilerParams(vmem_limit_bytes=40 * 1024 * 1024),
        cost_estimate=pl.CostEstimate(flops=0, transcendentals=0, bytes_accessed=moved),
    )(*operands)


def dots(left, right):
    return lax.dot_general(left, right, (((1,), (1,)), ((), ())), preferred_element_type=jnp.float32)


def low(value):
    return value.astype(jnp.bfloat16)


def wide(value):
    return value.astype(jnp.float32)


def left_kernel(order_ref, plain_ref, weight_ref, away_ref, rest_ref):
    points, transitions, depth = plain_ref.shape
    owners = order_ref.shape[0] - 1
    blocks = transitions // (owners * BLOCK)
    weight = weight_ref[...]
    for point in range(points):
        for slot in range(owners):
            out_ref = (away_ref, rest_ref)[slot // 2]
            for block in range(blocks):
                start = pl.multiple_of((block * owners + order_ref[slot]) * BLOCK, BLOCK)
                rows = wide(plain_ref[point, pl.ds(start, BLOCK), :]) * weight
                real = pl.ds((slot % 2 * 2 * blocks + block) * BLOCK, BLOCK)
                imag = pl.ds(((slot % 2 * 2 + 1) * blocks + block) * BLOCK, BLOCK)
                out_ref[point, real, :] = low(rows)
                out_ref[point, imag, : depth // 2] = low(-rows[:, depth // 2 :])
                out_ref[point, imag, depth // 2 :] = low(rows[:, : depth // 2])


def agreeing(order_ref, point):
    even = order_ref[order_ref.shape[0] - 1]
    return point + even - 2 * even * point


def sides(order_ref, point, left_ref, mate_left_ref, mate_ref, next_ref):
    agreed = agreeing(order_ref, point)
    own, far = left_ref[point], mate_left_ref[point]
    return (own, mate_ref[agreed]), (own, next_ref[agreed]), (far, next_ref[0]), (far, next_ref[1])


def away_kernel(order_ref, left_ref, mate_left_ref, mate_ref, next_ref, out_ref):
    for point in range(out_ref.shape[0]):
        for part, (rows, right) in enumerate(sides(order_ref, point, left_ref, mate_left_ref, mate_ref, next_ref)):
            half = right.shape[0]
            out_ref[point, :, part * half : (part + 1) * half] = low(dots(rows, right))


def rest_kernel(order_ref, left_ref, mate_left_ref, mate_ref, next_ref, out_ref):
    _, points, count, _ = out_ref.shape
    for point in range(points):
        for part, (rows, right) in enumerate(sides(order_ref, point, left_ref, mate_left_ref, mate_ref, next_ref)):
            half = right.shape[0]
            out = low(dots(rows, right))
            out_ref[0, point, :, part * half : (part + 1) * half] = out[:count]
            out_ref[1, point, :, part * half : (part + 1) * half] = out[count:]


def picked(order_ref, slots, rows, owners, transitions):
    n = lax.broadcasted_iota(jnp.int32, (rows, transitions), 0)
    column = lax.broadcasted_iota(jnp.int32, (rows, transitions), 1)
    target = (n // BLOCK * owners) * BLOCK + n % BLOCK
    return jnp.concatenate(
        [low(jnp.where(column == target + order_ref[slot] * BLOCK, 1.0, 0.0)) for slot in slots], axis=0
    )


def second_kernel(order_ref, rest_ref, got_ref, out_ref):
    points, count, _ = out_ref.shape
    columns = rest_ref.shape[3]
    half = columns // PARTS
    owners = order_ref.shape[0] - 1
    pick = picked(order_ref, (2, 1), count // 2, owners, half)
    for point in range(points):
        out_ref[point, :, :columns] = low(wide(rest_ref[0, point]) + wide(got_ref[point, count:, :]))
        own = low(wide(rest_ref[1, point]) + wide(got_ref[point, :count, :]))
        for part in range(PARTS):
            place = (columns + part * count, columns + (part + 1) * count)
            out_ref[point, :, place[0] : place[1]] = low(dots(own[:, part * half : (part + 1) * half], pick))


def turned_part(order_ref, block_ref, second_ref, late_ref, part):
    points, count, columns = block_ref.shape
    half = columns // PARTS
    rows = count // 2
    owners = order_ref.shape[0] - 1
    span = pl.ds(part * half, half)
    own = jnp.concatenate(
        [block_ref[point, p * rows : (p + 1) * rows, span] for p in range(2) for point in range(points)], axis=0
    )
    pick = picked(order_ref, (3, 0), rows, owners, half)
    others = []
    for point in range(points):
        other = dots(second_ref[point, :, span], pick) + wide(late_ref[point, :, pl.ds(columns + part * count, count)])
        others.append(low(other))
    other = jnp.concatenate(
        [others[point][p * rows : (p + 1) * rows] for p in range(2) for point in range(points)], axis=0
    )
    n = lax.broadcasted_iota(jnp.int32, (count, count), 0)
    same = low(jnp.where(n == lax.broadcasted_iota(jnp.int32, (count, count), 1), 1.0, 0.0))
    pieces = []
    for out in (dots(pick, own), dots(same, other)):
        for to in range(2):
            piece = out[to * rows : (to + 1) * rows]
            pieces.append(jnp.concatenate([low(piece[:, : points * rows]), low(-piece[:, points * rows :])], axis=0))
    return (pieces[0], pieces[2]), (pieces[1], pieces[3])


def finish(rest_ref, got_ref, late_ref, block_ref):
    points, count, columns = block_ref.shape
    for point in range(points):
        total = wide(rest_ref[1, point]) + wide(got_ref[point, :count, :]) + wide(late_ref[point, :, :columns])
        block_ref[point] = low(total)


def finish_kernel(
    order_ref, rest_ref, got_ref, second_ref, late_ref,
    block_ref, mate_same_ref, mate_first_ref, next_same_ref, next_first_ref,
):
    points, count, columns = block_ref.shape
    finish(rest_ref, got_ref, late_ref, block_ref)
    strips = columns // 2 // count
    for part in range(PARTS):
        same, first = turned_part(order_ref, block_ref, second_ref, late_ref, part)
        for source in range(2):
            if part == 0:
                mate_same_ref[source] = same[source]
                mate_first_ref[source] = first[source]
            else:
                next_same_ref[part - 1, source] = same[source]
                next_first_ref[part - 1, source] = first[source]
    for point in range(points):
        for strip in range(strips):
            tile = block_ref[point, :, columns // 2 + strip * count : columns // 2 + (strip + 1) * count]
            mate_same_ref[2 + point * strips + strip] = tile


def spread(order_ref, slot, lanes, columns):
    n = lax.broadcasted_iota(jnp.int32, (lanes, columns), 0)
    column = lax.broadcasted_iota(jnp.int32, (lanes, columns), 1)
    target = (n // BLOCK * (order_ref.shape[0] - 1) + order_ref[slot]) * BLOCK + n % BLOCK
    return low(jnp.where(column == target, 1.0, 0.0))


def merge_kernel(order_ref, block_ref, mate_first_ref, next_first_ref, next_same_ref, mate_same_ref, out_ref):
    points, count, _ = block_ref.shape
    columns = out_ref.shape[3]
    rows = count // 2
    half = columns // 2
    even = order_ref[order_ref.shape[0] - 1]
    lanes = points * rows
    strips = columns // count
    back = 0.0
    for slot, (mate_ref, next_ref, source) in enumerate(
        (
            (mate_same_ref, next_same_ref, 1),
            (mate_first_ref, next_first_ref, 1),
            (mate_first_ref, next_first_ref, 0),
            (mate_same_ref, next_same_ref, 0),
        )
    ):
        tiles = [mate_ref[source]] + [next_ref[part, source] for part in range(PARTS - 1)]
        back = back + lax.dot_general(
            jnp.concatenate(tiles, axis=0),
            spread(order_ref, slot, lanes, columns),
            (((1,), (0,)), ((), ())),
            preferred_element_type=jnp.float32,
        )
    back = low(back)
    for p in range(2):
        for part, place in ((0, 2 * even), (1, 2 - 2 * even)):
            natural = back[part * count + p * rows : part * count + (p + 1) * rows]
            for row_point in range(points):
                here = block_ref[row_point, p * rows : (p + 1) * rows, part * half : (part + 1) * half]
                for column_point in range(points):
                    there = natural[:, column_point * half : (column_point + 1) * half]
                    mine = even == (0 if row_point == column_point else 1)
                    out_ref[
                        place, p, row_point * rows : (row_point + 1) * rows, column_point * half : (column_point + 1) * half
                    ] = jnp.where(mine, here, there)
        for point in range(points):
            span = slice(point * rows, (point + 1) * rows)
            for strip in range(strips):
                tile = mate_same_ref[2 + point * strips + strip, p * rows : (p + 1) * rows, :]
                out_ref[1 + 2 * even, p, span, strip * count : (strip + 1) * count] = tile
            begin = (2 + point) * count + p * rows
            out_ref[3 - 2 * even, p, span, :] = back[begin : begin + rows]


def body(pair_density, coulomb):
    points, transitions, _, g_local = pair_density.shape
    owners = lax.axis_size("own")
    groups = lax.axis_size("kp")
    blocks = transitions // (owners * BLOCK)
    rows = blocks * BLOCK
    depth = 2 * g_local
    scale = 1.0 / math.sqrt(g_local * owners)
    me = lax.axis_index("own")
    odd = lax.axis_index("kp") % 2 == 1
    parity = odd.astype(jnp.int32)

    def exchange_kp(value, partner):
        return lax.ppermute(value, "kp", [(i, partner(i) % groups) for i in range(groups)])

    def flips(i):
        return [1, 2, 3, 0] if i % 2 == 0 else [3, 2, 1, 0]

    def exchange(value, slot, partner):
        pairs = [
            (i * owners + o, partner(i) % groups * owners + (o ^ flips(i)[slot]))
            for i in range(groups)
            for o in range(owners)
        ]
        return lax.ppermute(value, ("kp", "own"), pairs)

    def exchange_own(value, first):
        return exchange(value, 0 if first else 2, lambda i: i)

    def mate(i):
        return i + 1 if i % 2 == 0 else i - 1

    def across(i):
        return i - 1 if i % 2 == 0 else i + 1

    near_flip, far_flip = 1 + 2 * parity, 3 - 2 * parity
    relative = jnp.stack([me ^ near_flip, me ^ 2, me ^ far_flip, me, 1 - parity])

    plain = pair_density.reshape(points, transitions, depth)
    next_right = exchange_kp(plain, across)
    mate_right = exchange_kp(plain, mate)

    weights = (jnp.concatenate([coulomb, coulomb]) * scale).reshape(1, depth)
    left_shape = [(points, 4 * rows, depth)] * 2
    left_away, left_rest = local(left_kernel, left_shape, relative, plain, weights, scalars=1, moved=4 << 20)
    next_right, left_away = lax.optimization_barrier((next_right, left_away))
    mate_left, _ = lax.optimization_barrier((mate_right, next_right))
    mate_away, mate_rest = local(left_kernel, left_shape, relative, mate_left, weights, scalars=1)

    columns = points * transitions
    tile = (2 * rows, points * rows)
    strips = points * columns // tile[1]
    width = PARTS * transitions
    away_shape = [(points, 4 * rows, width)]
    rest_shape = [(2, points, 2 * rows, width)]
    second_shape = [(points, 2 * rows, width + PARTS * 2 * rows)]

    away = local(away_kernel, away_shape, relative, left_away, mate_away, mate_right, next_right, scalars=1)
    got = exchange_own(away, True)
    left_rest, mate_rest, _ = lax.optimization_barrier((left_rest, mate_rest, away))
    rest = local(
        rest_kernel, rest_shape, relative, left_rest, mate_rest, mate_right, next_right, scalars=1, moved=8 << 20
    )
    got, rest = lax.optimization_barrier((got, rest))
    second = local(second_kernel, second_shape, relative, rest, got, scalars=1)
    late = exchange_own(second, False)
    block, mate_same, mate_first, next_same, next_first = local(
        finish_kernel,
        [
            (points, 2 * rows, width),
            (2 + strips, *tile),
            (2, *tile),
            (PARTS - 1, 2, *tile),
            (PARTS - 1, 2, *tile),
        ],
        relative, rest, got, second, late, scalars=1,
    )
    mate_first = exchange(mate_first, 0, mate)
    next_first = exchange(next_first, 0, across)
    next_same = exchange_kp(next_same, across)
    mate_same = exchange_kp(mate_same, mate)
    out = local(
        merge_kernel, [(4, 2, points * rows, columns)],
        relative, block, mate_first, next_first, next_same, mate_same, scalars=1,
    )
    return out.transpose(0, 2, 1, 3)


def solution(mesh):
    placed = (P("kp", None, None, "own"), P("own"))
    return jax.shard_map(
        body,
        mesh=mesh,
        in_specs=placed,
        out_specs=P(None, ("kp", "own"), None, None),
        check_vma=False,
    )
```

```python
import math

import jax
import jax.numpy as jnp
from jax import lax
from jax.experimental import pallas as pl
from jax.experimental.pallas import tpu as pltpu
from jax.sharding import PartitionSpec as P

BLOCK = 32


def local(kernel, shapes, *operands, scalars=0, moved=0):
    vmem = pl.BlockSpec(memory_space=pltpu.VMEM)
    smem = pl.BlockSpec(memory_space=pltpu.SMEM)
    several = len(shapes) > 1
    out_shape = [jax.ShapeDtypeStruct(s, jnp.bfloat16) for s in shapes]
    return pl.pallas_call(
        kernel,
        out_shape=out_shape if several else out_shape[0],
        in_specs=[smem] * scalars + [vmem] * (len(operands) - scalars),
        out_specs=[vmem] * len(shapes) if several else vmem,
        compiler_params=pltpu.CompilerParams(vmem_limit_bytes=40 * 1024 * 1024),
        cost_estimate=pl.CostEstimate(flops=0, transcendentals=0, bytes_accessed=moved),
    )(*operands)


def dots(left, right):
    return lax.dot_general(left, right, (((1,), (1,)), ((), ())), preferred_element_type=jnp.float32)


def low(value):
    return value.astype(jnp.bfloat16)


def wide(value):
    return value.astype(jnp.float32)


def left_kernel(order_ref, plain_ref, weight_ref, away_ref, rest_ref):
    points, transitions, depth = plain_ref.shape
    owners = order_ref.shape[0] - 1
    blocks = transitions // (owners * BLOCK)
    weight = weight_ref[...]
    for point in range(points):
        for slot in range(owners):
            out_ref = (away_ref, rest_ref)[slot // 2]
            for block in range(blocks):
                start = pl.multiple_of((block * owners + order_ref[slot]) * BLOCK, BLOCK)
                rows = wide(plain_ref[point, pl.ds(start, BLOCK), :]) * weight
                real = pl.ds((slot % 2 * 2 * blocks + block) * BLOCK, BLOCK)
                imag = pl.ds(((slot % 2 * 2 + 1) * blocks + block) * BLOCK, BLOCK)
                out_ref[point, real, :] = low(rows)
                out_ref[point, imag, : depth // 2] = low(-rows[:, depth // 2 :])
                out_ref[point, imag, depth // 2 :] = low(rows[:, : depth // 2])


def agreeing(order_ref, point):
    even = order_ref[order_ref.shape[0] - 1]
    return point + even - 2 * even * point


def first_right(order_ref, point, mate_ref, near_ref):
    return mate_ref[agreeing(order_ref, point)], near_ref[...]


def second_right(order_ref, point, near_ref, later_ref):
    return jnp.where(agreeing(order_ref, point) == 0, near_ref[...], later_ref[...]), later_ref[...]


def away_kernel(rights):
    def kernel(order_ref, left_ref, mate_left_ref, one_ref, other_ref, out_ref):
        points, _, columns = out_ref.shape
        half = columns // 2
        for point in range(points):
            for part, right in enumerate(rights(order_ref, point, one_ref, other_ref)):
                rows = (left_ref, mate_left_ref)[part][point]
                out_ref[point, :, part * half : (part + 1) * half] = low(dots(rows, right))

    return kernel


def rest_kernel(rights):
    def kernel(order_ref, left_ref, mate_left_ref, one_ref, other_ref, out_ref):
        _, points, count, columns = out_ref.shape
        half = columns // 2
        for point in range(points):
            for part, right in enumerate(rights(order_ref, point, one_ref, other_ref)):
                out = low(dots((left_ref, mate_left_ref)[part][point], right))
                out_ref[0, point, :, part * half : (part + 1) * half] = out[:count]
                out_ref[1, point, :, part * half : (part + 1) * half] = out[count:]

    return kernel


def picked(order_ref, slots, rows, owners, transitions):
    n = lax.broadcasted_iota(jnp.int32, (rows, transitions), 0)
    column = lax.broadcasted_iota(jnp.int32, (rows, transitions), 1)
    target = (n // BLOCK * owners) * BLOCK + n % BLOCK
    return jnp.concatenate(
        [low(jnp.where(column == target + order_ref[slot] * BLOCK, 1.0, 0.0)) for slot in slots], axis=0
    )


def second_kernel(order_ref, rest_ref, got_ref, out_ref):
    points, count, _ = out_ref.shape
    half = rest_ref.shape[3] // 2
    owners = order_ref.shape[0] - 1
    pick = picked(order_ref, (2, 1), count // 2, owners, half)
    for point in range(points):
        out_ref[point, :, : 2 * half] = low(wide(rest_ref[0, point]) + wide(got_ref[point, count:, :]))
        own = low(wide(rest_ref[1, point]) + wide(got_ref[point, :count, :]))
        for part in range(2):
            place = (2 * half + part * count, 2 * half + (part + 1) * count)
            out_ref[point, :, place[0] : place[1]] = low(dots(own[:, part * half : (part + 1) * half], pick))


def turned_part(order_ref, block_ref, second_ref, late_ref, part):
    points, count, columns = block_ref.shape
    half = columns // 2
    rows = count // 2
    owners = order_ref.shape[0] - 1
    span = pl.ds(part * half, half)
    own = jnp.concatenate(
        [block_ref[point, p * rows : (p + 1) * rows, span] for p in range(2) for point in range(points)], axis=0
    )
    pick = picked(order_ref, (3, 0), rows, owners, half)
    others = []
    for point in range(points):
        other = dots(second_ref[point, :, span], pick) + wide(late_ref[point, :, pl.ds(columns + part * count, count)])
        others.append(low(other))
    other = jnp.concatenate(
        [others[point][p * rows : (p + 1) * rows] for p in range(2) for point in range(points)], axis=0
    )
    n = lax.broadcasted_iota(jnp.int32, (count, count), 0)
    same = low(jnp.where(n == lax.broadcasted_iota(jnp.int32, (count, count), 1), 1.0, 0.0))
    pieces = []
    for out in (dots(pick, own), dots(same, other)):
        for to in range(2):
            piece = out[to * rows : (to + 1) * rows]
            pieces.append(jnp.concatenate([low(piece[:, : points * rows]), low(-piece[:, points * rows :])], axis=0))
    return (pieces[0], pieces[2]), (pieces[1], pieces[3])


def finish(rest_ref, got_ref, late_ref, block_ref):
    points, count, columns = block_ref.shape
    for point in range(points):
        total = wide(rest_ref[1, point]) + wide(got_ref[point, :count, :]) + wide(late_ref[point, :, :columns])
        block_ref[point] = low(total)


def finish_kernel(order_ref, rest_ref, got_ref, second_ref, late_ref, block_ref, same_ref, first_ref):
    finish(rest_ref, got_ref, late_ref, block_ref)
    for part in range(2):
        same, first = turned_part(order_ref, block_ref, second_ref, late_ref, part)
        for source in range(2):
            same_ref[part, source] = same[source]
            first_ref[part, source] = first[source]


def pack_kernel(same_0_ref, passed_0_ref, same_1_ref, block_0_ref, block_1_ref, to_mate_ref, to_next_ref):
    points, count, columns = block_0_ref.shape
    strips = columns // 2 // count
    for part, ref in enumerate((to_mate_ref, to_next_ref)):
        ref[0:2] = same_0_ref[part]
        ref[2:4] = passed_0_ref[part]
        to_next_ref[4 + 2 * part : 6 + 2 * part] = same_1_ref[part]
    for point in range(points):
        for stream, ref in enumerate((block_0_ref, block_1_ref)):
            for strip in range(strips):
                tile = ref[point, :, columns // 2 + strip * count : columns // 2 + (strip + 1) * count]
                to_mate_ref[4 + (point * 2 + stream) * strips + strip] = tile


def spread(order_ref, slot, lanes, columns):
    n = lax.broadcasted_iota(jnp.int32, (lanes, columns), 0)
    column = lax.broadcasted_iota(jnp.int32, (lanes, columns), 1)
    target = (n // BLOCK * (order_ref.shape[0] - 1) + order_ref[slot]) * BLOCK + n % BLOCK
    return low(jnp.where(column == target, 1.0, 0.0))


def gathered(order_ref, sources, lanes, columns):
    back = 0.0
    for slot, tiles in enumerate(sources):
        back = back + lax.dot_general(
            jnp.concatenate(tiles, axis=0),
            spread(order_ref, slot, lanes, columns),
            (((1,), (0,)), ((), ())),
            preferred_element_type=jnp.float32,
        )
    return low(back)


def early_kernel(order_ref, block_0_ref, from_next_ref, from_mate_ref, out_ref):
    points, count, columns = block_0_ref.shape
    rows = count // 2
    half = columns // 2
    even = order_ref[order_ref.shape[0] - 1]
    strips = columns // count
    sources = [[from_mate_ref[source], from_next_ref[source]] for source in (1, 3, 2, 0)]
    back = gathered(order_ref, sources, points * rows, columns)
    for p in range(2):
        for row_point in range(points):
            down = slice(row_point * rows, (row_point + 1) * rows)
            here = block_0_ref[row_point, p * rows : (p + 1) * rows, :half]
            for column_point in range(points):
                along = slice(column_point * half, (column_point + 1) * half)
                mine = even == (0 if row_point == column_point else 1)
                out_ref[2 * even, down, p, along] = jnp.where(mine, here, back[p * rows : (p + 1) * rows, along])
            for strip in range(strips):
                tile = from_mate_ref[4 + row_point * strips + strip, p * rows : (p + 1) * rows, :]
                out_ref[1 + 2 * even, down, p, strip * count : (strip + 1) * count] = tile
        out_ref[3 - 2 * even, :rows, p, :] = back[count + p * rows : count + (p + 1) * rows]


def last_kernel(order_ref, early_ref, block_1_ref, first_1_ref, from_next_ref, out_ref, back_ref):
    del early_ref
    points, count, columns = block_1_ref.shape
    rows = count // 2
    half = columns // 2
    even = order_ref[order_ref.shape[0] - 1]
    step = pl.program_id(0)

    @pl.when(step == 0)
    def _():
        same = [[from_next_ref[4 + 2 * part + source] for part in range(2)] for source in range(2)]
        first = [[first_1_ref[part, source] for part in range(2)] for source in range(2)]
        back_ref[...] = gathered(order_ref, [same[1], first[1], first[0], same[0]], points * rows, columns)

    for p in range(2):

        @pl.when(step < points)
        def _():
            here = block_1_ref[jnp.minimum(step, points - 1), p * rows : (p + 1) * rows, :half]
            for column_point in range(points):
                along = slice(column_point * half, (column_point + 1) * half)
                mine = even == jnp.where(step == column_point, 0, 1)
                there = back_ref[p * rows : (p + 1) * rows, along]
                out_ref[0, :, p, along] = jnp.where(mine, here, there)

        @pl.when(step == points)
        def _():
            out_ref[0, :, p, :] = back_ref[count + p * rows : count + (p + 1) * rows, :]


def last(order, early, block_1, first_1, from_next):
    points, count, columns = block_1.shape
    rows = count // 2

    def place(step, order_ref):
        even = order_ref[order_ref.shape[0] - 1]
        far = step // points
        return (2 - 2 * even) * (1 - far) + (3 - 2 * even) * far, step * (1 - far) + (points - 1) * far, 0, 0

    vmem = pl.BlockSpec(memory_space=pltpu.VMEM)
    return pl.pallas_call(
        last_kernel,
        out_shape=jax.ShapeDtypeStruct(early.shape, early.dtype),
        grid_spec=pltpu.PrefetchScalarGridSpec(
            num_scalar_prefetch=1,
            grid=(points + 1,),
            in_specs=[pl.BlockSpec(memory_space=pl.ANY), vmem, vmem, vmem],
            out_specs=pl.BlockSpec((1, rows, 2, columns), place),
            scratch_shapes=[pltpu.VMEM((2 * count, columns), jnp.bfloat16)],
        ),
        input_output_aliases={1: 0},
        compiler_params=pltpu.CompilerParams(vmem_limit_bytes=40 * 1024 * 1024),
        cost_estimate=pl.CostEstimate(flops=0, transcendentals=0, bytes_accessed=0),
    )(order, early, block_1, first_1, from_next)


def body(pair_density, coulomb):
    points, transitions, _, g_local = pair_density.shape
    owners = lax.axis_size("own")
    groups = lax.axis_size("kp")
    blocks = transitions // (owners * BLOCK)
    rows = blocks * BLOCK
    depth = 2 * g_local
    scale = 1.0 / math.sqrt(g_local * owners)
    me = lax.axis_index("own")
    odd = lax.axis_index("kp") % 2 == 1
    parity = odd.astype(jnp.int32)

    def exchange_kp(value, partner):
        return lax.ppermute(value, "kp", [(i, partner(i) % groups) for i in range(groups)])

    def flips(i):
        return [1, 2, 3, 0] if i % 2 == 0 else [3, 2, 1, 0]

    def exchange(value, slot, partner):
        pairs = [
            (i * owners + o, partner(i) % groups * owners + (o ^ flips(i)[slot]))
            for i in range(groups)
            for o in range(owners)
        ]
        return lax.ppermute(value, ("kp", "own"), pairs)

    def exchange_own(value, first):
        return exchange(value, 0 if first else 2, lambda i: i)

    def mate(i):
        return i + 1 if i % 2 == 0 else i - 1

    def across(i):
        return i - 1 if i % 2 == 0 else i + 1

    near_flip, far_flip = 1 + 2 * parity, 3 - 2 * parity
    relative = jnp.stack([me ^ near_flip, me ^ 2, me ^ far_flip, me, 1 - parity])

    plain = lax.optimization_barrier(pair_density.reshape(points, transitions, depth))
    near = exchange_kp(plain[0], across)
    later = exchange_kp(plain[1], across)
    mate_right = exchange_kp(plain, mate)

    weights = (jnp.concatenate([coulomb, coulomb]) * scale).reshape(1, depth)
    left_shape = [(points, 4 * rows, depth)] * 2
    left_away, left_rest = local(left_kernel, left_shape, relative, plain, weights, scalars=1, moved=4 << 20)
    mate_away, mate_rest = local(left_kernel, left_shape, relative, mate_right, weights, scalars=1, moved=4 << 20)
    near, mate_away = lax.optimization_barrier((near, mate_away))

    columns = points * transitions
    away_shape = [(points, 4 * rows, columns)]
    rest_shape = [(2, points, 2 * rows, columns)]
    second_shape = [(points, 2 * rows, columns + 4 * rows)]
    block_shape = (points, 2 * rows, columns)
    tile = (2 * rows, points * rows)
    strips = points * columns // tile[1]

    away_0 = local(away_kernel(first_right), away_shape, relative, left_away, mate_away, mate_right, near, scalars=1)
    got_0 = exchange_own(away_0, True)
    later, _ = lax.optimization_barrier((later, away_0))
    away_1 = local(away_kernel(second_right), away_shape, relative, left_away, mate_away, near, later, scalars=1)
    got_1 = exchange_own(away_1, True)
    left_rest, mate_rest, _ = lax.optimization_barrier((left_rest, mate_rest, away_1))
    rest_0 = local(
        rest_kernel(first_right), rest_shape, relative, left_rest, mate_rest, mate_right, near, scalars=1, moved=8 << 20
    )
    rest_1 = local(
        rest_kernel(second_right), rest_shape, relative, left_rest, mate_rest, near, later, scalars=1, moved=8 << 20
    )
    got_0, rest_0, rest_1 = lax.optimization_barrier((got_0, rest_0, rest_1))
    second_0 = local(second_kernel, second_shape, relative, rest_0, got_0, scalars=1)
    late_0 = exchange_own(second_0, False)
    got_1, _ = lax.optimization_barrier((got_1, second_0))
    second_1 = local(second_kernel, second_shape, relative, rest_1, got_1, scalars=1)
    late_1 = exchange_own(second_1, False)
    late_0, _ = lax.optimization_barrier((late_0, second_1))
    finish_shape = [block_shape, (2, 2, *tile), (2, 2, *tile)]
    block_0, same_0, first_0 = local(finish_kernel, finish_shape, relative, rest_0, got_0, second_0, late_0, scalars=1)
    passed_0 = exchange_own(first_0, True)
    late_1, _ = lax.optimization_barrier((late_1, first_0))
    block_1, same_1, first_1 = local(finish_kernel, finish_shape, relative, rest_1, got_1, second_1, late_1, scalars=1)
    to_mate, to_next = local(
        pack_kernel, [(4 + strips, *tile), (8, *tile)], same_0, passed_0, same_1, block_0, block_1, moved=16 << 20
    )
    first_1 = exchange(first_1, 0, across)
    from_next = exchange_kp(to_next, across)
    from_mate = exchange_kp(to_mate, mate)
    early = local(
        early_kernel, [(4, points * rows, 2, columns)], relative, block_0, from_next, from_mate, scalars=1, moved=8 << 20
    )
    return last(relative, early, block_1, first_1, from_next)


def solution(mesh):
    placed = (P("kp", None, None, "own"), P("own"))
    return jax.shard_map(
        body,
        mesh=mesh,
        in_specs=placed,
        out_specs=P(None, ("kp", "own"), None, None),
        check_vma=False,
    )
```
